128 devices in a mesh: cast: 8 (over x_lo, z), width: 8 (over y, x_hi), thick: 2 (over core).
Axes of the slice: x: 4 (x_hi: 2, x_lo: 2; x = x_hi * 2 + x_lo), y: 4, z: 4, core: 2. Of those that a mesh axis runs over, the one named last changes fastest.
Arguments:
- velocity: float32 [3, 512, 256, 512], P(None, 'cast', ('width', 'thick')), may hold values from -6 to 6
- magnetic: float32 [3, 512, 256, 512], P(None, 'cast', ('width', 'thick')), may hold values from -6 to 6
- labels: int32 [512, 256, 512], P('cast', ('width', 'thick')), may hold values from 0 to 2
- viscosity: float32 [512, 256, 512], P('cast', ('width', 'thick')), may hold values from 0.05 to 0.5
Outputs:
- velocity_next: float32 [3, 512, 256, 512], P(None, 'cast', ('width', 'thick'))
- potential: float32 [512, 256, 512], P('cast', ('width', 'thick'))
The draws below stay inside these ranges and needn't reach their ends.
All inputs are finite; a program needn't handle non-finite values.
Results may differ from the reference program's by a relative error of at most 0.00002.
Values sent between devices are 32-bit elements; how exact they have to be, the bound alone decides.
No kernel may reach another device: no remote copies, remote signals or barrier semaphores. Data moves between devices by JAX's collectives and lax.ppermute only.
A program may use at most 192 MiB of HBM per device.

```python
import math
import jax
import jax.numpy as jnp

NZ = 512
ITERS = 4
NX = 512
NY = 256


def plant(array, own_key, least, top_value):
    spot = [jax.random.randint(jax.random.fold_in(own_key, axis), (), 0, length) for axis, length in enumerate(array.shape)]
    main_axis = array.shape.index(max(array.shape))
    next_to = spot[:main_axis] + [(spot[main_axis] + 1) % array.shape[main_axis]] + spot[main_axis + 1:]
    return array.at[tuple(spot)].set(least).at[tuple(next_to)].set(top_value)


def levels(rng, dims, cuts, smallest, largest):
    factor_of = 1.0
    for axis_at, parts in cuts:
        draws = jax.random.uniform(jax.random.fold_in(jax.random.fold_in(rng, 6), axis_at), (parts,), jnp.float32, smallest / len(cuts), largest / len(cuts))
        factor_of = factor_of * jnp.repeat(jnp.exp(draws), dims[axis_at] // parts).reshape((-1,) + (1,) * (len(dims) - 1 - axis_at))
    return factor_of


def normal_values(stream_key, dims, scale, most, pieces=(), dtype=jnp.bfloat16):
    values = scale * jax.random.normal(stream_key, dims, jnp.float32)
    if pieces:
        values = values * levels(stream_key, dims, pieces, -0.22, 0.18)
    return jnp.clip(values, -most, most).astype(dtype)


def setup_inputs(seed: int = 0) -> dict:
    splits = jax.random.split(jax.random.key(seed), 5)
    velocity = normal_values(splits[0], (3, NX, NY, NZ), 1.0, 6.0, ((1, 8), (2, 16)), jnp.float32)
    magnetic = normal_values(splits[1], (3, NX, NY, NZ), 1.0, 6.0, ((1, 8), (2, 16)), jnp.float32)
    labels = plant(jax.random.randint(splits[2], (NX, NY, NZ), 0, 3), jax.random.fold_in(splits[2], 1), 0, 2).astype(jnp.int32)
    viscosity = jnp.clip(jnp.exp(math.log(0.5) - 2.3025851 * jax.random.uniform(splits[3], (NX, NY, NZ), jnp.float32) ** levels(splits[3], (NX, NY, NZ), ((0, 8), (1, 16)), -0.2, 0.2)), 0.05, 0.5)
    return {"velocity": velocity, "magnetic": magnetic, "labels": labels, "viscosity": viscosity}


time_step = 0.1
force_gain = 0.3


def conductivity(labels):
    return jnp.where(labels == 0, 1.0, jnp.where(labels == 1, 0.7, 4.0)).astype(jnp.float32)


def pad_three(field):
    return jnp.pad(field, [(0, 0)] * (field.ndim - 3) + [(1, 1)] * 3)


def neighbour(padded, dim, step):
    leading = padded.ndim - 3
    count = padded.shape[leading + dim]
    index = [slice(None)] * leading + [slice(1, -1)] * 3
    index[leading + dim] = slice(1 + step, count - 1 + step)
    return padded[tuple(index)]


def center(padded):
    leading = padded.ndim - 3
    return padded[tuple([slice(None)] * leading + [slice(1, -1)] * 3)]


def cross(left, right):
    return jnp.stack([left[1] * right[2] - left[2] * right[1],
                      left[2] * right[0] - left[0] * right[2],
                      left[0] * right[1] - left[1] * right[0]])


def sweep_weight(k):
    return 2.0 / (2.15 + 1.75 * math.cos(math.pi * (2 * k + 1) / (2 * ITERS)))


def prepare(sig_pad, field_pad):
    sig_c = center(sig_pad)
    field_c = center(field_pad)
    faces = []
    source = jnp.zeros_like(sig_c)
    diag = 0.05 * sig_c
    for dim in range(3):
        for step in (1, -1):
            sig_n = neighbour(sig_pad, dim, step)
            face = 2.0 * sig_c * sig_n / (sig_c + sig_n)
            faces.append((dim, step, face))
            source = source + step * face * (field_c[dim] + neighbour(field_pad[dim], dim, step)) * 0.5
            diag = diag + face
    return faces, source, diag


def relax(phi_pad, faces, source, diag, omega):
    phi = center(phi_pad)
    total = jnp.zeros_like(phi)
    for dim, step, face in faces:
        total = total + face * neighbour(phi_pad, dim, step)
    return phi + omega * ((total - source) / diag - phi)


def lorentz(phi_pad, sigma, field, magnetic):
    grads = [0.5 * (neighbour(phi_pad, d, 1) - neighbour(phi_pad, d, -1)) for d in range(3)]
    current = jnp.stack([sigma * (field[d] - grads[d]) for d in range(3)])
    return cross(current, magnetic)


def predict(vel_pad, visc_pad, force):
    vel = center(vel_pad)
    visc = center(visc_pad)
    result = []
    for comp in range(3):
        advect = jnp.zeros_like(visc)
        spread = jnp.zeros_like(visc)
        for dim in range(3):
            upper = neighbour(vel_pad[comp], dim, 1)
            lower = neighbour(vel_pad[comp], dim, -1)
            advect = advect + vel[dim] * (upper - lower) * 0.5
            spread = spread + 0.5 * (visc + neighbour(visc_pad, dim, 1)) * (upper - vel[comp])
            spread = spread + 0.5 * (visc + neighbour(visc_pad, dim, -1)) * (lower - vel[comp])
        result.append(vel[comp] + time_step * (spread - advect) + force_gain * force[comp])
    return jnp.stack(result)


def reference(velocity, magnetic, labels, viscosity):
    sigma = conductivity(labels)
    field = cross(velocity, magnetic)
    faces, source, diag = prepare(pad_three(sigma), pad_three(field))
    potential = jnp.zeros_like(sigma)
    for k in range(ITERS):
        potential = relax(pad_three(potential), faces, source, diag, sweep_weight(k))
    force = lorentz(pad_three(potential), sigma, field, magnetic)
    velocity_next = predict(pad_three(velocity), pad_three(viscosity), force)
    return velocity_next, potential
```

```python
import functools
import math

import jax
import jax.numpy as jnp
from jax import lax
from jax.experimental import pallas as pl
from jax.experimental.pallas import tpu as pltpu
from jax.sharding import PartitionSpec as P

ITERS = 4
time_step = 0.1
force_gain = 0.3

NXL = 64
NYL = 16
NT = 4
PAD = 16
CELLS = NXL * NYL
ROWS = CELLS + 2 * PAD
F32 = jnp.float32
WIDTH = ("width", "thick")
MIB = 1024 * 1024


def sweep_weight(k):
    return 2.0 / (2.15 + 1.75 * math.cos(math.pi * (2 * k + 1) / (2 * ITERS)))


def lanes(shape):
    return lax.broadcasted_iota(jnp.int32, shape, 2)


def sublanes(shape):
    return lax.broadcasted_iota(jnp.int32, shape, 1)


def z_up(a):
    r = pltpu.roll(a, 127, 2)
    after = jnp.concatenate([r[1:], jnp.zeros_like(r[:1])], axis=0)
    return jnp.where(lanes(a.shape) == 127, after, r)


def z_down(a):
    r = pltpu.roll(a, 1, 2)
    before = jnp.concatenate([jnp.zeros_like(r[:1]), r[:-1]], axis=0)
    return jnp.where(lanes(a.shape) == 0, before, r)


def recip(d):
    y = pl.reciprocal(d, approx=True)
    return y * (2.0 - d * y)


def low_rows():
    return pl.ds(PAD, NXL, stride=NYL)


def high_rows():
    return pl.ds(PAD + NYL - 1, NXL, stride=NYL)


LOW_PLANE = pl.ds(PAD, NYL)
HIGH_PLANE = pl.ds(PAD + CELLS - NYL, NYL)


def edge_slices():
    return (low_rows(), high_rows(), LOW_PLANE, HIGH_PLANE)


def zero_pads(ref):
    shape = ref.shape[:-2] + (PAD, 128)
    lead = (slice(None),) * (len(ref.shape) - 2)
    ref[lead + (pl.ds(0, PAD),)] = jnp.zeros(shape, F32)
    ref[lead + (pl.ds(PAD + CELLS, PAD),)] = jnp.zeros(shape, F32)


def row_of(x):
    return pl.multiple_of(PAD + x * NYL, NYL)


CHUNKS = 4


def load_kernel(vel, mag, lab, v, b, sig, e, ylo, yhi, xlo, xhi, labv, sem):
    per = CELLS // CHUNKS
    for ch in range(CHUNKS):
        src = pl.ds(ch * per, per)
        dst = pl.ds(PAD + ch * per, per)
        for t in range(NT):
            col = pl.ds(128 * t, 128)
            for c in range(3):
                pltpu.make_async_copy(vel.at[c, src, col], v.at[c, t, dst], sem.at[ch, 0]).start()
                pltpu.make_async_copy(mag.at[c, src, col], b.at[c, t, dst], sem.at[ch, 1]).start()
            pltpu.make_async_copy(lab.at[src, col], labv.at[t, src], sem.at[ch, 2]).start()
    for ref in (v, sig, e):
        zero_pads(ref)
    for ch in range(CHUNKS):
        src = pl.ds(ch * per, per)
        dst = pl.ds(PAD + ch * per, per)
        pltpu.make_async_copy(v.at[:, :, dst], v.at[:, :, dst], sem.at[ch, 0]).wait()
        pltpu.make_async_copy(b.at[:, :, dst], b.at[:, :, dst], sem.at[ch, 1]).wait()
        pltpu.make_async_copy(labv.at[:, src], labv.at[:, src], sem.at[ch, 2]).wait()

        @pl.loop(0, per // 8, unroll=4)
        def _(i):
            raw = pl.ds(pl.multiple_of(ch * per + i * 8, 8), 8)
            at = pl.ds(pl.multiple_of(PAD + ch * per + i * 8, 8), 8)
            lb = labv[:, raw, :]
            sig[:, at, :] = jnp.where(lb == 0, 1.0, jnp.where(lb == 1, 0.7, 4.0)).astype(F32)
            v0, v1, v2 = (v[c, :, at, :] for c in range(3))
            b0, b1, b2 = (b[c, :, at, :] for c in range(3))
            e[0, :, at, :] = v1 * b2 - v2 * b1
            e[1, :, at, :] = v2 * b0 - v0 * b2
            e[2, :, at, :] = v0 * b1 - v1 * b0

    for out, rows, d in zip((ylo, yhi, xlo, xhi), edge_slices(), (1, 1, 0, 0)):
        out[0] = sig[:, rows, :]
        out[1] = e[d, :, rows, :]


def face_kernel(w0, sig, e, v, visc, f, src, inv, phi, nu, vylo, vyhi, vxlo, vxhi, sem):
    copies = [
        pltpu.make_async_copy(visc.at[:, pl.ds(128 * t, 128)], nu.at[t, pl.ds(PAD, CELLS)], sem.at[t])
        for t in range(NT)
    ]
    for copy in copies:
        copy.start()
    for ref in (f, phi, nu):
        zero_pads(ref)
    shape = (NT, 8, 128)
    zero = jnp.zeros(shape, F32)
    sub = sublanes(shape)

    def face(a, n):
        return (2.0 * a) * n * recip(a + n)

    def body(x, carry):
        fxm, qxm, sc, exc = carry
        r = row_of(x)
        fx, qx, sp, exp = [], [], [], []
        fy, qy, fz, qz = [], [], [], []
        for y in range(2):
            at = pl.ds(r + 8 * y, 8)
            up = pl.ds(r + 8 * y + 1, 8)
            ahead = pl.ds(r + NYL + 8 * y, 8)
            sp.append(sig[:, ahead, :])
            exp.append(e[0, :, ahead, :])
            fx.append(face(sc[y], sp[y]))
            qx.append(fx[y] * (exc[y] + exp[y]))
            g = face(sc[y], sig[:, up, :])
            if y == 1:
                g = jnp.where(sub == 7, 0.0, g)
            fy.append(g)
            qy.append(g * (e[1, :, at, :] + e[1, :, up, :]))
            g = face(sc[y], z_up(sc[y]))
            ez = e[2, :, at, :]
            fz.append(g)
            qz.append(g * (ez + z_up(ez)))
        rf = [pltpu.roll(a, 1, 1) for a in fy]
        rq = [pltpu.roll(a, 1, 1) for a in qy]
        for y in range(2):
            at = pl.ds(r + 8 * y, 8)
            fym = jnp.where(sub == 0, rf[1 - y], rf[y])
            qym = jnp.where(sub == 0, rq[1 - y], rq[y])
            source = 0.5 * (((qx[y] - qxm[y]) + (qy[y] - qym)) + (qz[y] - z_down(qz[y])))
            diag = ((fx[y] + fxm[y]) + (fy[y] + fym)) + (fz[y] + z_down(fz[y])) + 0.05 * sc[y]
            inverse = recip(diag)
            f[0, :, at, :] = fx[y]
            f[1, :, at, :] = fy[y]
            f[2, :, at, :] = fz[y]
            src[:, at, :] = source
            inv[:, at, :] = inverse
            phi[:, at, :] = (-w0) * (source * inverse)
        return (tuple(fx), tuple(qx), tuple(sp), tuple(exp))

    first = [pl.ds(PAD + 8 * y, 8) for y in range(2)]
    start = (
        (zero, zero),
        (zero, zero),
        tuple(sig[:, at, :] for at in first),
        tuple(e[0, :, at, :] for at in first),
    )
    lax.fori_loop(0, NXL, body, start, unroll=2)
    for copy in copies:
        copy.wait()
    for out, rows in zip((vylo, vyhi, vxlo, vxhi), edge_slices()):
        for c in range(3):
            out[c] = v[c, :, rows, :]
        out[3] = nu[:, rows, :]


def first_edge_kernel(w0, hyl, hyh, hxl, hxh, sig, e, src_in, inv_in, phi_in,
                      src, inv, phi, cyl, cyh, cxl, cxh, oyl, oyh, oxl, oxh):
    del src_in, inv_in, phi_in
    place = lax.axis_index("width") * 2 + lax.axis_index("thick")
    cast = lax.axis_index("cast")
    inside = (place > 0, place < lax.axis_size(WIDTH) - 1, cast > 0, cast < lax.axis_size("cast") - 1)
    sides = tuple(zip((hyl, hyh, hxl, hxh), (cyl, cyh, cxl, cxh), (oyl, oyh, oxl, oxh), edge_slices(),
                      (1, 1, 0, 0), (-0.5, 0.5, -0.5, 0.5), inside))
    for halo, coef, _, rows, d, sign, ok in sides:
        s = sig[:, rows, :]
        n = halo[0] * jnp.where(ok, 1.0, 0.0).astype(F32)
        g = (2.0 * s) * n * recip(s + n)
        coef[...] = g
        src[:, rows, :] = src[:, rows, :] + sign * (g * (e[d, :, rows, :] + halo[1]))
        inv[:, rows, :] = recip(recip(inv[:, rows, :]) + g)
    for _, coef, _, rows, _, _, _ in sides:
        i = inv[:, rows, :]
        coef[...] = coef[...] * i
        phi[:, rows, :] = (-w0) * (src[:, rows, :] * i)
    for _, _, out, rows, _, _, _ in sides:
        out[...] = phi[:, rows, :]


def predictor(v, nu, vnew, x0, x1):
    shape = (NT, 8, 128)
    sub = sublanes(shape)

    @pl.loop(x0, x1)
    def _(x):
        r = row_of(x)
        for y in range(2):
            base = r + 8 * y
            at = pl.ds(base, 8)
            ups = (pl.ds(base + NYL, 8), pl.ds(base + 1, 8))
            downs = (pl.ds(base - NYL, 8), pl.ds(base - 1, 8))
            n = nu[:, at, :]
            vc = [v[c, :, at, :] for c in range(3)]
            coefs = []
            total = None
            for d in range(3):
                above = nu[:, ups[d], :] if d < 2 else z_up(n)
                below = nu[:, downs[d], :] if d < 2 else z_down(n)
                up = (0.5 * time_step) * ((n + above) - vc[d])
                down = (0.5 * time_step) * ((n + below) + vc[d])
                if d == 1 and y == 1:
                    up = jnp.where(sub == 7, 0.0, up)
                if d == 1 and y == 0:
                    down = jnp.where(sub == 0, 0.0, down)
                coefs.append((up, down))
                both = up + down
                total = both if total is None else total + both
            keep = 1.0 - total
            for c in range(3):
                acc = keep * vc[c]
                for d in range(3):
                    above = v[c, :, ups[d], :] if d < 2 else z_up(vc[c])
                    below = v[c, :, downs[d], :] if d < 2 else z_down(vc[c])
                    acc = acc + coefs[d][0] * above + coefs[d][1] * below
                vnew[c, :, at, :] = acc


def sweep_kernel(w, x0, x1, phi, f, src, inv, v, nu, *rest):
    out, vnew = rest[-2:]
    zero_pads(out)
    shape = (NT, 8, 128)
    zero = jnp.zeros(shape, F32)

    def body(x, carry):
        pxm, pc = carry
        r = row_of(x)
        px, pn = [], []
        for y in range(2):
            base = r + 8 * y
            at = pl.ds(base, 8)
            pn.append(phi[:, pl.ds(base + NYL, 8), :])
            fx = f[0, :, at, :]
            c = pc[y]
            px.append(fx * c)
            t = fx * pn[y] + pxm[y]
            t = t + f[1, :, at, :] * phi[:, pl.ds(base + 1, 8), :]
            t = t + f[1, :, pl.ds(base - 1, 8), :] * phi[:, pl.ds(base - 1, 8), :]
            fz = f[2, :, at, :]
            t = t + fz * z_up(c)
            t = t + z_down(fz * c)
            out[:, at, :] = c + w * ((t - src[:, at, :]) * inv[:, at, :] - c)
        return tuple(px), tuple(pn)

    start = ((zero, zero), tuple(phi[:, pl.ds(PAD + 8 * y, 8), :] for y in range(2)))
    lax.fori_loop(0, NXL, body, start, unroll=4)
    predictor(v, nu, vnew, x0, x1)


def edge_kernel(w, phi_in, cyl, cyh, cxl, cxh, hyl, hyh, hxl, hxh, phi, oyl, oyh, oxl, oxh):
    del phi_in
    for coef, halo, rows in zip((cyl, cyh, cxl, cxh), (hyl, hyh, hxl, hxh), edge_slices()):
        phi[:, rows, :] = phi[:, rows, :] + w * (coef[...] * halo[...])
    for out, rows in zip((oyl, oyh, oxl, oxh), edge_slices()):
        out[...] = phi[:, rows, :]


def force_kernel(phi, sig, e, b, vnew_in, potential, vnew, sem):
    del vnew_in
    copies = [
        pltpu.make_async_copy(phi.at[t, pl.ds(PAD, CELLS)], potential.at[:, pl.ds(128 * t, 128)], sem.at[t])
        for t in range(NT)
    ]
    for copy in copies:
        copy.start()
    shape = (NT, 8, 128)
    sub = sublanes(shape)

    @pl.loop(0, NXL, unroll=2)
    def _(x):
        r = row_of(x)
        for y in range(2):
            base = r + 8 * y
            at = pl.ds(base, 8)
            p = phi[:, at, :]
            yu = phi[:, pl.ds(base + 1, 8), :]
            yd = phi[:, pl.ds(base - 1, 8), :]
            if y == 1:
                yu = jnp.where(sub == 7, 0.0, yu)
            else:
                yd = jnp.where(sub == 0, 0.0, yd)
            diffs = (
                phi[:, pl.ds(base + NYL, 8), :] - phi[:, pl.ds(base - NYL, 8), :],
                yu - yd,
                z_up(p) - z_down(p),
            )
            s = force_gain * sig[:, at, :]
            cur = [s * (e[d, :, at, :] - 0.5 * diffs[d]) for d in range(3)]
            bb = [b[d, :, at, :] for d in range(3)]
            vnew[0, :, at, :] = vnew[0, :, at, :] + (cur[1] * bb[2] - cur[2] * bb[1])
            vnew[1, :, at, :] = vnew[1, :, at, :] + (cur[2] * bb[0] - cur[0] * bb[2])
            vnew[2, :, at, :] = vnew[2, :, at, :] + (cur[0] * bb[1] - cur[1] * bb[0])

    for copy in copies:
        copy.wait()


def last_kernel(sig, b, v, nu, hyl, hyh, hxl, hxh, gyl, gyh, gxl, gxh, vnew_in, result, vnew, sem):
    del vnew_in
    place = lax.axis_index("width") * 2 + lax.axis_index("thick")
    cast = lax.axis_index("cast")
    inside = (place > 0, place < lax.axis_size(WIDTH) - 1, cast > 0, cast < lax.axis_size("cast") - 1)
    sides = zip((hyl, hyh, hxl, hxh), (gyl, gyh, gxl, gxh), edge_slices(), (1, 1, 0, 0), (1.0, -1.0, 1.0, -1.0), inside)
    for halo, flow, rows, d, sign, ok in sides:
        mask = jnp.where(ok, 1.0, 0.0).astype(F32)
        cur = (0.5 * force_gain * sign) * (mask * (sig[:, rows, :] * halo[...]))
        n1, n2 = (d + 1) % 3, (d + 2) % 3
        add = {n1: -cur * b[n2, :, rows, :], n2: cur * b[n1, :, rows, :]}
        hn = mask * flow[3]
        along = v[d, :, rows, :]
        coef = (0.5 * time_step) * ((nu[:, rows, :] + hn) + sign * along)
        gone = (0.5 * time_step) * hn if d == 0 else coef
        for c in range(3):
            new = vnew[c, :, rows, :] + (coef * (mask * flow[c]) - gone * v[c, :, rows, :])
            if c in add:
                new = new + add[c]
            vnew[c, :, rows, :] = new
    copies = [
        pltpu.make_async_copy(vnew.at[c, t, pl.ds(PAD, CELLS)], result.at[c, :, pl.ds(128 * t, 128)], sem.at[c, t])
        for c in range(3)
        for t in range(NT)
    ]
    for copy in copies:
        copy.start()
    for copy in copies:
        copy.wait()


def resident(*shape):
    return pltpu.VMEM(shape, F32)


def in_vmem(x):
    return pltpu.with_memory_space_constraint(x, pltpu.VMEM)


def in_hbm(x):
    return pltpu.with_memory_space_constraint(x, pltpu.HBM)


IN_VMEM = pl.BlockSpec(memory_space=pltpu.VMEM)
IN_HBM = pl.BlockSpec(memory_space=pl.ANY)

FIELD = (NT, ROWS, 128)
YP = (NT, NXL, 128)
XP = (NT, NYL, 128)


def run(kernel, name, ins, outs, aliases=None, scratch=(), flops=0, moved=0, limit=8 * MIB):
    args = [in_hbm(a) if hbm else in_vmem(a) for a, hbm in ins]
    return pl.pallas_call(
        kernel,
        out_shape=outs,
        in_specs=[IN_HBM if hbm else IN_VMEM for _, hbm in ins],
        out_specs=[IN_HBM if isinstance(o, jax.ShapeDtypeStruct) else IN_VMEM for o in outs],
        input_output_aliases=aliases or {},
        scratch_shapes=list(scratch),
        compiler_params=pltpu.CompilerParams(vmem_limit_bytes=limit),
        cost_estimate=pl.CostEstimate(flops=flops, bytes_accessed=moved, transcendentals=0),
        name=name,
    )(*args)


def vm(*arrays):
    return [(a, False) for a in arrays]


def ring(axis, step):
    n = lax.axis_size(axis)
    return [(i, (i + step) % n) for i in range(n)]


def exchange(ylo, yhi, xlo, xhi):
    hyl = lax.ppermute(yhi, WIDTH, ring(WIDTH, 1))
    hyh = lax.ppermute(ylo, WIDTH, ring(WIDTH, -1))
    hxl = lax.ppermute(xhi, "cast", ring("cast", 1))
    hxh = lax.ppermute(xlo, "cast", ring("cast", -1))
    return hyl, hyh, hxl, hxh


def local(velocity, magnetic, labels, viscosity):
    vel = velocity.reshape(3, CELLS, NT * 128)
    mag = magnetic.reshape(3, CELLS, NT * 128)
    lab = labels.reshape(CELLS, NT * 128)
    visc = viscosity.reshape(CELLS, NT * 128)
    dma = pltpu.SemaphoreType.DMA
    w = [sweep_weight(k) for k in range(ITERS)]

    pair = [resident(2, *YP)] * 2 + [resident(2, *XP)] * 2
    quad = [resident(4, *YP)] * 2 + [resident(4, *XP)] * 2
    plain = [resident(*YP)] * 2 + [resident(*XP)] * 2

    v, b, sig, e, *edges = run(
        load_kernel, "load", [(vel, True), (mag, True), (lab, True)],
        [resident(3, *FIELD), resident(3, *FIELD), resident(*FIELD), resident(3, *FIELD)] + pair,
        scratch=[pltpu.VMEM((NT, CELLS, 128), jnp.int32), dma((CHUNKS, 3))],
    )
    halos = exchange(*edges)
    f, src, inv, phi, nu, *flow = run(
        functools.partial(face_kernel, w[0]), "faces", vm(sig, e, v) + [(visc, True)],
        [resident(3, *FIELD), resident(*FIELD), resident(*FIELD), resident(*FIELD), resident(*FIELD)] + quad,
        scratch=[dma((NT,))], flops=10_000_000, moved=20 * MIB,
    )
    src, inv, phi, *rest = run(
        functools.partial(first_edge_kernel, w[0]), "edges1", vm(*halos, sig, e, src, inv, phi),
        [resident(*FIELD)] * 3 + plain + plain,
        aliases={6: 0, 7: 1, 8: 2},
    )
    coefs, edges = rest[:4], rest[4:]
    flow_halos = exchange(*flow)
    vnew = None
    cuts = (0, 22, 43, 64)
    for k in range(1, ITERS):
        halos = exchange(*edges)
        ins = vm(phi, f, src, inv, v, nu)
        aliases = {}
        if vnew is not None:
            ins = ins + vm(vnew)
            aliases = {6: 1}
        phi, vnew = run(
            functools.partial(sweep_kernel, w[k], cuts[k - 1], cuts[k]), f"sweep{k}", ins,
            [resident(*FIELD), resident(3, *FIELD)], aliases=aliases, flops=10_000_000, moved=16 * MIB,
        )
        phi, *edges = run(
            functools.partial(edge_kernel, w[k]), f"edges{k + 1}", vm(phi, *coefs, *halos),
            [resident(*FIELD)] + plain, aliases={0: 0},
        )
    halos = exchange(*edges)
    potential, vnew = run(
        force_kernel, "force", vm(phi, sig, e, b, vnew),
        [jax.ShapeDtypeStruct((CELLS, NT * 128), F32), resident(3, *FIELD)],
        aliases={4: 1}, scratch=[dma((NT,))], flops=10_000_000, moved=16 * MIB,
    )
    result, _ = run(
        last_kernel, "last", vm(sig, b, v, nu, *halos, *flow_halos, vnew),
        [jax.ShapeDtypeStruct((3, CELLS, NT * 128), F32), resident(3, *FIELD)],
        aliases={12: 1}, scratch=[dma((3, NT))],
    )
    return result.reshape(velocity.shape), potential.reshape(labels.shape)


def solution(mesh):
    fields = P(None, "cast", WIDTH, None)
    scalar = P("cast", WIDTH, None)
    return jax.shard_map(
        local,
        mesh=mesh,
        in_specs=(fields, fields, scalar, scalar),
        out_specs=(fields, scalar),
        check_vma=False,
    )
```

```python
import functools
import math

import jax
import jax.numpy as jnp
from jax import lax
from jax.experimental import pallas as pl
from jax.experimental.pallas import tpu as pltpu
from jax.sharding import PartitionSpec as P

ITERS = 4
time_step = 0.1
force_gain = 0.3

NXL = 64
NYL = 16
NT = 4
PAD = 16
CELLS = NXL * NYL
ROWS = CELLS + 2 * PAD
F32 = jnp.float32
WIDTH = ("width", "thick")
MIB = 1024 * 1024
SHAPE = (NT, 8, 128)
OUTSIDE = 1e30


def sweep_weight(k):
    return 2.0 / (2.15 + 1.75 * math.cos(math.pi * (2 * k + 1) / (2 * ITERS)))


def z_up(a, fill=0.0):
    r = pltpu.roll(a, 127, 2)
    after = jnp.concatenate([r[1:], jnp.full_like(r[:1], fill)], axis=0)
    return jnp.where(lax.broadcasted_iota(jnp.int32, a.shape, 2) == 127, after, r)


def z_down(a):
    r = pltpu.roll(a, 1, 2)
    before = jnp.concatenate([jnp.zeros_like(r[:1]), r[:-1]], axis=0)
    return jnp.where(lax.broadcasted_iota(jnp.int32, a.shape, 2) == 0, before, r)


def recip(d):
    return pltpu.reciprocal(d, approx=True)


def sublanes():
    return lax.broadcasted_iota(jnp.int32, SHAPE, 1)


def row_of(x):
    return pl.multiple_of(PAD + x * NYL, NYL)


def fill_pads(ref, value=0.0):
    lead = (slice(None),) * (len(ref.shape) - 2)
    block = jnp.full(ref.shape[:-2] + (PAD, 128), value, F32)
    ref[lead + (pl.ds(0, PAD),)] = block
    ref[lead + (pl.ds(PAD + CELLS, PAD),)] = block


class Sides:
    def __init__(self, x0=0, planes=NXL):
        thick = lax.axis_index("thick")
        place = lax.axis_index("width") * 2 + thick
        cast = lax.axis_index("cast")
        last = lax.axis_size("width") * 2 - 1
        near = (NYL - 1) * (1 - thick)
        far = (NYL - 1) * thick

        def rows(pad):
            start = pad + x0 * NYL
            return (
                pl.ds(start + near, planes, stride=NYL),
                pl.ds(start + far, planes, stride=NYL),
                pl.ds(pad, NYL),
                pl.ds(pad + CELLS - NYL, NYL),
            )

        self.rows = rows(PAD)
        self.inner = rows(0)
        self.dims = (1, 1, 0, 0)
        high = jnp.where(thick == 0, 1.0, -1.0).astype(F32)
        self.signs = (high, -high, -1.0, 1.0)

        def inside(ok):
            return jnp.where(ok, 1.0, 0.0).astype(F32)

        self.masks = (
            1.0,
            inside(((thick == 0) & (place > 0)) | ((thick == 1) & (place < last))),
            inside(cast > 0),
            inside(cast < lax.axis_size("cast") - 1),
        )


CHUNKS = 4


def load_kernel(vel, mag, lab, v, hat, e, oa, ob, ol, oh, braw, lraw, sem):
    per = CELLS // CHUNKS
    for ch in range(CHUNKS):
        src = pl.ds(ch * per, per)
        dst = pl.ds(PAD + ch * per, per)
        for t in range(NT):
            pltpu.make_async_copy(vel.at[:, src, pl.ds(128 * t, 128)], v.at[:, t, dst], sem.at[ch, t]).start()
        pltpu.make_async_copy(mag.at[:, src], braw.at[:, src], sem.at[ch, NT]).start()
        pltpu.make_async_copy(lab.at[src], lraw.at[src], sem.at[ch, NT + 1]).start()
    fill_pads(v)
    fill_pads(e)
    fill_pads(hat, OUTSIDE)
    for ch in range(CHUNKS):
        src = pl.ds(ch * per, per)
        dst = pl.ds(PAD + ch * per, per)
        for t in range(NT):
            pltpu.make_async_copy(vel.at[:, src, pl.ds(128 * t, 128)], v.at[:, t, dst], sem.at[ch, t]).wait()
        pltpu.make_async_copy(mag.at[:, src], braw.at[:, src], sem.at[ch, NT]).wait()
        pltpu.make_async_copy(lab.at[src], lraw.at[src], sem.at[ch, NT + 1]).wait()

        @pl.loop(0, per // 8, unroll=8)
        def _(i):
            raw = pl.ds(pl.multiple_of(ch * per + i * 8, 8), 8)
            at = pl.ds(pl.multiple_of(PAD + ch * per + i * 8, 8), 8)
            for t in range(NT):
                col = pl.ds(128 * t, 128)
                lb = lraw[raw, col]
                hat[t, at, :] = jnp.where(lb == 0, 0.5, jnp.where(lb == 1, 0.5 / 0.7, 0.125)).astype(F32)
                v0, v1, v2 = (v[c, t, at, :] for c in range(3))
                b0, b1, b2 = (braw[c, raw, col] for c in range(3))
                e[0, t, at, :] = v1 * b2 - v2 * b1
                e[1, t, at, :] = v2 * b0 - v0 * b2
                e[2, t, at, :] = v0 * b1 - v1 * b0

    sides = Sides()
    for out, rows, d in zip((oa, ob, ol, oh), sides.rows, sides.dims):
        out[0] = hat[:, rows, :]
        out[1] = e[d, :, rows, :]
        out[2] = v[0, :, rows, :]


def faces(w0, hat, e, f, src, inv, phi):
    zero = jnp.zeros(SHAPE, F32)
    sub = sublanes()

    def body(x, carry):
        fxm, qxm, hc, exc = carry
        r = row_of(x)
        fxo, qxo, hn, exn = [], [], [], []
        for y in range(2):
            base = r + 8 * y
            at, up, down = pl.ds(base, 8), pl.ds(base + 1, 8), pl.ds(base - 1, 8)
            ahead = pl.ds(base + NYL, 8)
            c = hc[y]
            hn.append(hat[:, ahead, :])
            exn.append(e[0, :, ahead, :])
            fx = recip(c + hn[y])
            qx = fx * (exc[y] + exn[y])
            fxo.append(fx)
            qxo.append(qx)
            ey = e[1, :, at, :]
            fy = recip(c + hat[:, up, :])
            fym = recip(c + hat[:, down, :])
            if y == 1:
                fy = jnp.where(sub == 7, 0.0, fy)
            else:
                fym = jnp.where(sub == 0, 0.0, fym)
            fz = recip(c + z_up(c, OUTSIDE))
            ez = e[2, :, at, :]
            qz = fz * (ez + z_up(ez))
            total = (qx - qxm[y]) + (fy * (ey + e[1, :, up, :]) - fym * (ey + e[1, :, down, :])) + (qz - z_down(qz))
            diag = ((fx + fxm[y]) + (fy + fym)) + (fz + z_down(fz)) + 0.025 * recip(c)
            source = 0.5 * total
            inverse = recip(diag)
            f[0, :, at, :] = fx
            f[1, :, at, :] = fy
            f[2, :, at, :] = fz
            src[:, at, :] = source
            inv[:, at, :] = inverse
            phi[:, at, :] = (-w0) * (source * inverse)
        return tuple(fxo), tuple(qxo), tuple(hn), tuple(exn)

    first = [pl.ds(PAD + 8 * y, 8) for y in range(2)]
    start = (
        (zero, zero),
        (zero, zero),
        tuple(hat[:, at, :] for at in first),
        tuple(e[0, :, at, :] for at in first),
    )
    lax.fori_loop(0, NXL, body, start, unroll=8)


def face_kernel(w0, planes, hat, e, v, visc, f, src, inv, phi, nu, vnew, sem):
    copies = [
        pltpu.make_async_copy(visc.at[:, pl.ds(128 * t, 128)], nu.at[t, pl.ds(PAD, CELLS)], sem.at[t])
        for t in range(NT)
    ]
    for copy in copies:
        copy.start()
    f[1, :, 0:PAD, :] = jnp.zeros((NT, PAD, 128), F32)
    fill_pads(phi)
    fill_pads(nu)
    faces(w0, hat, e, f, src, inv, phi)
    for copy in copies:
        copy.wait()
    predictor(v, nu, vnew, *planes)


def first_edge_kernel(w0, ha, hb, hl, hh, hat, e, v, src_in, inv_in, phi_in,
                      src, inv, phi, ca, cb, cl, ch, oa, ob, ol, oh):
    del src_in, inv_in, phi_in
    s = Sides()
    sides = tuple(zip((ha, hb, hl, hh), (ca, cb, cl, ch), (oa, ob, ol, oh), s.rows, s.dims, s.signs, s.masks))
    for halo, coef, _, rows, d, sign, mask in sides:
        g = mask * recip(hat[:, rows, :] + halo[0])
        coef[...] = g
        src[:, rows, :] = src[:, rows, :] + (0.5 * sign) * (g * (e[d, :, rows, :] + halo[1]))
        inv[:, rows, :] = recip(recip(inv[:, rows, :]) + g)
    for _, coef, _, rows, _, _, _ in sides:
        i = inv[:, rows, :]
        coef[...] = coef[...] * i
        phi[:, rows, :] = (-w0) * (src[:, rows, :] * i)
    for _, _, out, rows, _, _, _ in sides:
        out[0] = phi[:, rows, :]
        out[1] = v[1, :, rows, :]


def edge_kernel(w, comp, phi_in, ca, cb, cl, ch, ha, hb, hl, hh, *rest):
    del phi_in
    flow = rest[0] if comp is not None else None
    phi, *outs = rest[-5:]
    rows_of = Sides().rows
    for coef, halo, rows in zip((ca, cb, cl, ch), (ha, hb, hl, hh), rows_of):
        phi[:, rows, :] = phi[:, rows, :] + w * (coef[...] * halo[0])
    for out, rows in zip(outs, rows_of):
        out[0] = phi[:, rows, :]
        if comp is not None:
            out[1] = flow[comp, :, rows, :] if len(flow.shape) == 4 else flow[:, rows, :]


def predictor(v, nu, vnew, x0, x1):
    sub = sublanes()
    half = 0.5 * time_step

    @pl.loop(x0, x1, unroll=8)
    def _(x):
        r = row_of(x)
        for y in range(2):
            base = r + 8 * y
            at = pl.ds(base, 8)
            ups = (pl.ds(base + NYL, 8), pl.ds(base + 1, 8))
            downs = (pl.ds(base - NYL, 8), pl.ds(base - 1, 8))
            n = nu[:, at, :]
            vc = [v[c, :, at, :] for c in range(3)]
            coefs = []
            total = None
            for d in range(3):
                above = nu[:, ups[d], :] if d < 2 else z_up(n)
                below = nu[:, downs[d], :] if d < 2 else z_down(n)
                up = (n + above) - vc[d]
                down = (n + below) + vc[d]
                if d == 1 and y == 1:
                    up = jnp.where(sub == 7, 0.0, up)
                if d == 1 and y == 0:
                    down = jnp.where(sub == 0, 0.0, down)
                coefs.append((up, down))
                both = up + down
                total = both if total is None else total + both
            keep = 1.0 - half * total
            for c in range(3):
                acc = None
                for d in range(3):
                    above = v[c, :, ups[d], :] if d < 2 else z_up(vc[c])
                    below = v[c, :, downs[d], :] if d < 2 else z_down(vc[c])
                    term = coefs[d][0] * above + coefs[d][1] * below
                    acc = term if acc is None else acc + term
                vnew[c, :, at, :] = half * acc + keep * vc[c]


def sweep_kernel(w, planes, phi, f, src, inv, v, nu, vnew_in, out, vnew):
    del vnew_in
    fill_pads(out)
    zero = jnp.zeros(SHAPE, F32)

    def body(x, carry):
        pxm, pc = carry
        r = row_of(x)
        px, pn = [], []
        for y in range(2):
            base = r + 8 * y
            at, up, down = pl.ds(base, 8), pl.ds(base + 1, 8), pl.ds(base - 1, 8)
            pn.append(phi[:, pl.ds(base + NYL, 8), :])
            fx = f[0, :, at, :]
            c = pc[y]
            px.append(fx * c)
            t = fx * pn[y] + pxm[y]
            t = t + f[1, :, at, :] * phi[:, up, :]
            t = t + f[1, :, down, :] * phi[:, down, :]
            fz = f[2, :, at, :]
            t = t + fz * z_up(c)
            t = t + z_down(fz * c)
            out[:, at, :] = c + w * ((t - src[:, at, :]) * inv[:, at, :] - c)
        return tuple(px), tuple(pn)

    start = ((zero, zero), tuple(phi[:, pl.ds(PAD + 8 * y, 8), :] for y in range(2)))
    lax.fori_loop(0, NXL, body, start, unroll=16)
    predictor(v, nu, vnew, *planes)


def force_kernel(phi, hat, e, mag, v, nu, *rest):
    flows = [rest[4 * i : 4 * i + 4] for i in range(4)]
    potential, vnew, *edge_b = rest[17:23]
    bv, sem = rest[23:]
    per = CELLS // CHUNKS

    def magnetic(ch):
        src = pl.ds(ch * per, per)
        return [
            pltpu.make_async_copy(mag.at[:, src, pl.ds(128 * t, 128)], bv.at[:, t, src], sem.at[ch, t])
            for t in range(NT)
        ]

    copies = [
        pltpu.make_async_copy(
            phi.at[t, pl.ds(PAD, CELLS)], potential.at[:, pl.ds(128 * t, 128)], sem.at[CHUNKS, t]
        )
        for t in range(NT)
    ]
    for ch in range(CHUNKS):
        for copy in magnetic(ch):
            copy.start()
    for copy in copies:
        copy.start()

    s = Sides()
    half = 0.5 * time_step
    for i in range(4):
        rows, d, sign, mask = s.rows[i], s.dims[i], s.signs[i], s.masks[i]
        other = [mask * flows[0][i][2], mask * flows[1][i][1], mask * flows[2][i][1]]
        hn = mask * flows[3][i][1]
        coef = half * ((nu[:, rows, :] + hn) - sign * v[d, :, rows, :])
        gone = half * hn if d == 0 else coef
        for c in range(3):
            vnew[c, :, rows, :] = vnew[c, :, rows, :] + (coef * other[c] - gone * v[c, :, rows, :])

    sub = sublanes()
    for ch in range(CHUNKS):
        for copy in magnetic(ch):
            copy.wait()

        @pl.loop(ch * (NXL // CHUNKS), (ch + 1) * (NXL // CHUNKS), unroll=8)
        def _(x):
            r = row_of(x)
            for y in range(2):
                base = r + 8 * y
                at = pl.ds(base, 8)
                raw = pl.ds(pl.multiple_of(x * NYL + 8 * y, 8), 8)
                p = phi[:, at, :]
                yu = phi[:, pl.ds(base + 1, 8), :]
                yd = phi[:, pl.ds(base - 1, 8), :]
                if y == 1:
                    yu = jnp.where(sub == 7, 0.0, yu)
                else:
                    yd = jnp.where(sub == 0, 0.0, yd)
                diffs = (
                    phi[:, pl.ds(base + NYL, 8), :] - phi[:, pl.ds(base - NYL, 8), :],
                    yu - yd,
                    z_up(p) - z_down(p),
                )
                g = (0.5 * force_gain) * recip(hat[:, at, :])
                cur = [g * (e[d, :, at, :] - 0.5 * diffs[d]) for d in range(3)]
                b0, b1, b2 = (bv[c, :, raw, :] for c in range(3))
                c0, c1, c2 = cur
                vnew[0, :, at, :] = vnew[0, :, at, :] + (c1 * b2 - c2 * b1)
                vnew[1, :, at, :] = vnew[1, :, at, :] + (c2 * b0 - c0 * b2)
                vnew[2, :, at, :] = vnew[2, :, at, :] + (c0 * b1 - c1 * b0)

    for i in range(4):
        rows, d, sign = s.rows[i], s.dims[i], s.signs[i]
        inner = s.inner[i]
        n1, n2 = (d + 1) % 3, (d + 2) % 3
        g = (0.25 * force_gain * sign) * (s.masks[i] * recip(hat[:, rows, :]))
        edge_b[i][0] = g * bv[n2, :, inner, :]
        edge_b[i][1] = -g * bv[n1, :, inner, :]
    for copy in copies:
        copy.wait()


def last_kernel(ka, kb, kl, kh, ha, hb, hl, hh, vnew_in, result, vnew, sem):
    del vnew_in
    planes = NXL // CHUNKS
    copies = []
    for ch in range(CHUNKS):
        s = Sides(ch * planes, planes)
        some = pl.ds(ch * planes, planes)
        todo = [(ka, ha, 0, some), (kb, hb, 1, some)]
        if ch == 0:
            todo.append((kl, hl, 2, pl.ds(0, NYL)))
        if ch == CHUNKS - 1:
            todo.append((kh, hh, 3, pl.ds(0, NYL)))
        for k, h, i, part in todo:
            rows, d = s.rows[i], s.dims[i]
            halo = h[0, :, part, :]
            for j, c in enumerate(((d + 1) % 3, (d + 2) % 3)):
                vnew[c, :, rows, :] = vnew[c, :, rows, :] + k[j, :, part, :] * halo
        per = planes * NYL
        for t in range(NT):
            copy = pltpu.make_async_copy(
                vnew.at[:, t, pl.ds(PAD + ch * per, per)],
                result.at[:, pl.ds(ch * per, per), pl.ds(128 * t, 128)],
                sem.at[ch, t],
            )
            copy.start()
            copies.append(copy)
    for copy in copies:
        copy.wait()


def resident(*shape):
    return pltpu.VMEM(shape, F32)


def in_vmem(x):
    return pltpu.with_memory_space_constraint(x, pltpu.VMEM)


def in_hbm(x):
    return pltpu.with_memory_space_constraint(x, pltpu.HBM)


IN_VMEM = pl.BlockSpec(memory_space=pltpu.VMEM)
IN_HBM = pl.BlockSpec(memory_space=pl.ANY)

FIELD = (NT, ROWS, 128)


def run(kernel, name, ins, outs, aliases=None, scratch=(), flops=0, moved=0, limit=8 * MIB):
    args = [in_hbm(a) if hbm else in_vmem(a) for a, hbm in ins]
    return pl.pallas_call(
        kernel,
        out_shape=outs,
        in_specs=[IN_HBM if hbm else IN_VMEM for _, hbm in ins],
        out_specs=[IN_HBM if isinstance(o, jax.ShapeDtypeStruct) else IN_VMEM for o in outs],
        input_output_aliases=aliases or {},
        scratch_shapes=list(scratch),
        compiler_params=pltpu.CompilerParams(vmem_limit_bytes=limit),
        cost_estimate=pl.CostEstimate(flops=flops, bytes_accessed=moved, transcendentals=0),
        name=name,
    )(*args)


def vm(*arrays):
    return [(a, False) for a in arrays]


def ring(axis, step):
    n = lax.axis_size(axis)
    return [(i, (i + step) % n) for i in range(n)]


def exchange(a, b, low, high):
    n = lax.axis_size("width") * 2
    across = [(i, (((i + 1) ^ 1) - 1) % n) for i in range(n)]
    hb = lax.ppermute(b, WIDTH, across)
    hl = lax.ppermute(high, "cast", ring("cast", 1))
    hh = lax.ppermute(low, "cast", ring("cast", -1))
    ha = lax.ppermute(a, "thick", [(0, 1), (1, 0)])
    return ha, hb, hl, hh


def edge_planes(n):
    return [resident(n, NT, NXL, 128)] * 2 + [resident(n, NT, NYL, 128)] * 2


def local(velocity, magnetic, labels, viscosity):
    vel = velocity.reshape(3, CELLS, NT * 128)
    mag = magnetic.reshape(3, CELLS, NT * 128)
    lab = labels.reshape(CELLS, NT * 128)
    visc = viscosity.reshape(CELLS, NT * 128)
    dma = pltpu.SemaphoreType.DMA
    w = [sweep_weight(k) for k in range(ITERS)]
    field, fields = resident(*FIELD), resident(3, *FIELD)
    cuts = (0, 16, 32, 48, 64)

    v, hat, e, *edges = run(
        load_kernel, "load", [(vel, True), (mag, True), (lab, True)],
        [fields, field, fields] + edge_planes(3),
        scratch=[
            pltpu.VMEM((3, CELLS, NT * 128), F32),
            pltpu.VMEM((CELLS, NT * 128), jnp.int32),
            dma((CHUNKS, NT + 2)),
        ],
        limit=12 * MIB,
    )
    halos = exchange(*edges)
    flows = [halos]
    f, src, inv, phi, nu, vnew = run(
        functools.partial(face_kernel, w[0], cuts[:2]), "faces", vm(hat, e, v) + [(visc, True)],
        [fields, field, field, field, field, fields],
        scratch=[dma((NT,))], flops=10_000_000, moved=20 * MIB,
    )
    src, inv, phi, *rest = run(
        functools.partial(first_edge_kernel, w[0]), "edges1", vm(*halos, hat, e, v, src, inv, phi),
        [field] * 3 + [resident(*o.shape[1:]) for o in edge_planes(1)] + edge_planes(2),
        aliases={7: 0, 8: 1, 9: 2},
    )
    coefs, edges = rest[:4], rest[4:]
    for k in range(1, ITERS):
        halos = exchange(*edges)
        flows.append(halos)
        phi, vnew = run(
            functools.partial(sweep_kernel, w[k], cuts[k : k + 2]), f"sweep{k}", vm(phi, f, src, inv, v, nu, vnew),
            [field, fields], aliases={6: 1}, flops=10_000_000, moved=16 * MIB,
        )
        comp, flow = ((2, [v]), (0, [nu]), (None, []))[k - 1]
        phi, *edges = run(
            functools.partial(edge_kernel, w[k], comp), f"edges{k + 1}", vm(phi, *coefs, *halos, *flow),
            [field] + edge_planes(1 if comp is None else 2), aliases={0: 0},
        )
    halos = exchange(*edges)
    potential, vnew, *products = run(
        force_kernel, "force",
        vm(phi, hat, e) + [(mag, True)] + vm(v, nu, *[h for group in flows for h in group], vnew),
        [jax.ShapeDtypeStruct((CELLS, NT * 128), F32), fields] + edge_planes(2),
        aliases={22: 1}, scratch=[pltpu.VMEM((3, NT, CELLS, 128), F32), dma((CHUNKS + 1, NT))],
        flops=10_000_000, moved=16 * MIB, limit=12 * MIB,
    )
    result, _ = run(
        last_kernel, "last", vm(*products, *halos, vnew),
        [jax.ShapeDtypeStruct((3, CELLS, NT * 128), F32), fields],
        aliases={8: 1}, scratch=[dma((CHUNKS, NT))],
    )
    return result.reshape(velocity.shape), potential.reshape(labels.shape)


def solution(mesh):
    fields = P(None, "cast", WIDTH, None)
    scalar = P("cast", WIDTH, None)
    return jax.shard_map(
        local,
        mesh=mesh,
        in_specs=(fields, fields, scalar, scalar),
        out_specs=(fields, scalar),
        check_vma=False,
    )
```

```python
import functools
import math

import jax
import jax.numpy as jnp
from jax import lax
from jax.experimental import pallas as pl
from jax.experimental.pallas import tpu as pltpu
from jax.sharding import PartitionSpec as P

ITERS = 4
time_step = 0.1
force_gain = 0.3

NXL = 64
NYL = 16
NT = 4
PAD = 16
CELLS = NXL * NYL
ROWS = CELLS + 2 * PAD
F32 = jnp.float32
WIDTH = ("width", "thick")
MIB = 1024 * 1024
SHAPE = (NT, 8, 128)
OUTSIDE = 1e30


def sweep_weight(k):
    return 2.0 / (2.15 + 1.75 * math.cos(math.pi * (2 * k + 1) / (2 * ITERS)))


def z_up(a, fill=0.0):
    r = pltpu.roll(a, 127, 2)
    after = jnp.concatenate([r[1:], jnp.full_like(r[:1], fill)], axis=0)
    return jnp.where(lax.broadcasted_iota(jnp.int32, a.shape, 2) == 127, after, r)


def z_down(a):
    r = pltpu.roll(a, 1, 2)
    before = jnp.concatenate([jnp.zeros_like(r[:1]), r[:-1]], axis=0)
    return jnp.where(lax.broadcasted_iota(jnp.int32, a.shape, 2) == 0, before, r)


def recip(d):
    return pltpu.reciprocal(d, approx=True)


def sublanes():
    return lax.broadcasted_iota(jnp.int32, SHAPE, 1)


def row_of(x):
    return pl.multiple_of(PAD + x * NYL, NYL)


def fill_pads(ref, value=0.0):
    lead = (slice(None),) * (len(ref.shape) - 2)
    block = jnp.full(ref.shape[:-2] + (PAD, 128), value, F32)
    ref[lead + (pl.ds(0, PAD),)] = block
    ref[lead + (pl.ds(PAD + CELLS, PAD),)] = block


class Sides:
    def __init__(self, x0=0, planes=NXL):
        thick = lax.axis_index("thick")
        place = lax.axis_index("width") * 2 + thick
        cast = lax.axis_index("cast")
        last = lax.axis_size("width") * 2 - 1
        near = self.near = (NYL - 1) * (1 - thick)
        far = self.far = (NYL - 1) * thick

        def rows(pad):
            start = pad + x0 * NYL
            return (
                pl.ds(start + near, planes, stride=NYL),
                pl.ds(start + far, planes, stride=NYL),
                pl.ds(pad, NYL),
                pl.ds(pad + CELLS - NYL, NYL),
            )

        self.rows = rows(PAD)
        self.inner = rows(0)
        self.dims = (1, 1, 0, 0)
        high = jnp.where(thick == 0, 1.0, -1.0).astype(F32)
        self.signs = (high, -high, -1.0, 1.0)

        def inside(ok):
            return jnp.where(ok, 1.0, 0.0).astype(F32)

        self.masks = (
            1.0,
            inside(((thick == 0) & (place > 0)) | ((thick == 1) & (place < last))),
            inside(cast > 0),
            inside(cast < lax.axis_size("cast") - 1),
        )


CHUNKS = 8


def load_kernel(vel, mag, lab, v, hat, e, vnew, oa, ob, ol, oh, ka, kb, kl, kh, b, lraw, sem):
    per = CELLS // CHUNKS

    def copies(ch):
        src = pl.ds(ch * per, per)
        dst = pl.ds(PAD + ch * per, per)
        for t in range(NT):
            col = pl.ds(128 * t, 128)
            yield pltpu.make_async_copy(vel.at[:, src, col], v.at[:, t, dst], sem.at[ch, t])
            yield pltpu.make_async_copy(mag.at[:, src, col], b.at[:, t, src], sem.at[ch, NT + t])
        yield pltpu.make_async_copy(lab.at[src], lraw.at[src], sem.at[ch, 2 * NT])

    for ch in range(CHUNKS):
        for copy in copies(ch):
            copy.start()
    fill_pads(v)
    fill_pads(e)
    fill_pads(hat, OUTSIDE)
    for ch in range(CHUNKS):
        for copy in copies(ch):
            copy.wait()

        @pl.loop(0, per // 8, unroll=8)
        def _(i):
            raw = pl.ds(pl.multiple_of(ch * per + i * 8, 8), 8)
            at = pl.ds(pl.multiple_of(PAD + ch * per + i * 8, 8), 8)
            for t in range(NT):
                lb = lraw[raw, pl.ds(128 * t, 128)]
                melt, shell = lb == 0, lb == 1
                hat[t, at, :] = jnp.where(melt, 0.5, jnp.where(shell, 0.5 / 0.7, 0.125)).astype(F32)
                gain = jnp.where(melt, 1.0, jnp.where(shell, 0.7, 4.0)).astype(F32) * force_gain
                v0, v1, v2 = (v[c, t, at, :] for c in range(3))
                b0, b1, b2 = (b[c, t, raw, :] for c in range(3))
                e0, e1, e2 = v1 * b2 - v2 * b1, v2 * b0 - v0 * b2, v0 * b1 - v1 * b0
                e[0, t, at, :] = e0
                e[1, t, at, :] = e1
                e[2, t, at, :] = e2
                vnew[0, t, at, :] = gain * (e1 * b2 - e2 * b1)
                vnew[1, t, at, :] = gain * (e2 * b0 - e0 * b2)
                vnew[2, t, at, :] = gain * (e0 * b1 - e1 * b0)

    sides = Sides()
    for out, rows, d in zip((oa, ob, ol, oh), sides.rows, sides.dims):
        out[0] = hat[:, rows, :]
        out[1] = e[d, :, rows, :]
        for c in range(1 if d else 3):
            out[2 + c] = v[c, :, rows, :]

    for i, k in enumerate((ka, kb, kl, kh)):
        rows, at, d = sides.rows[i], sides.inner[i], sides.dims[i]
        n1, n2 = (d + 1) % 3, (d + 2) % 3
        g = (0.25 * force_gain * sides.signs[i]) * (sides.masks[i] * recip(hat[:, rows, :]))
        k[0] = g * b[n2, :, at, :]
        k[1] = -g * b[n1, :, at, :]


def faces(w0, hat, e, f, src, inv, phi):
    zero = jnp.zeros(SHAPE, F32)
    sub = sublanes()

    def body(x, carry):
        fxm, qxm, hc, exc = carry
        r = row_of(x)
        fxo, qxo, hn, exn = [], [], [], []
        for y in range(2):
            base = r + 8 * y
            at, up, down = pl.ds(base, 8), pl.ds(base + 1, 8), pl.ds(base - 1, 8)
            ahead = pl.ds(base + NYL, 8)
            c = hc[y]
            hn.append(hat[:, ahead, :])
            exn.append(e[0, :, ahead, :])
            fx = recip(c + hn[y])
            qx = fx * (exc[y] + exn[y])
            fxo.append(fx)
            qxo.append(qx)
            ey = e[1, :, at, :]
            fy = recip(c + hat[:, up, :])
            fym = recip(c + hat[:, down, :])
            if y == 1:
                fy = jnp.where(sub == 7, 0.0, fy)
            else:
                fym = jnp.where(sub == 0, 0.0, fym)
            fz = recip(c + z_up(c, OUTSIDE))
            ez = e[2, :, at, :]
            qz = fz * (ez + z_up(ez))
            total = (qx - qxm[y]) + (fy * (ey + e[1, :, up, :]) - fym * (ey + e[1, :, down, :])) + (qz - z_down(qz))
            diag = ((fx + fxm[y]) + (fy + fym)) + (fz + z_down(fz)) + 0.025 * recip(c)
            source = 0.5 * total
            inverse = recip(diag)
            f[0, :, at, :] = fx
            f[1, :, at, :] = fy
            f[2, :, at, :] = fz
            src[:, at, :] = source
            inv[:, at, :] = inverse
            phi[:, at, :] = (-w0) * (source * inverse)
        return tuple(fxo), tuple(qxo), tuple(hn), tuple(exn)

    first = [pl.ds(PAD + 8 * y, 8) for y in range(2)]
    start = (
        (zero, zero),
        (zero, zero),
        tuple(hat[:, at, :] for at in first),
        tuple(e[0, :, at, :] for at in first),
    )
    lax.fori_loop(0, NXL, body, start, unroll=8)


def face_kernel(w0, hat, e, v, vnew, f, src, inv, phi):
    del v, vnew
    f[1, :, 0:PAD, :] = jnp.zeros((NT, PAD, 128), F32)
    fill_pads(phi)
    faces(w0, hat, e, f, src, inv, phi)


PHI, BEHIND, SOURCE, INVERSE, FACE_Y, FACE_Z, LINES = range(7)
LOW, HIGH = 0, 1


def put_planes(outs, phi, f):
    for out, edge, behind, face in zip(outs, (0, NXL - 1), (1, NXL - 2), (0, NXL - 2)):
        out[PHI] = phi[:, pl.ds(PAD + edge * NYL, NYL), :]
        out[BEHIND] = f[0, :, pl.ds(PAD + face * NYL, NYL), :] * phi[:, pl.ds(PAD + behind * NYL, NYL), :]


def first_edge_kernel(w0, ha, hb, hl, hh, hat, e, v, f_in, src_in, inv_in, phi_in,
                      f, src, inv, phi, ca, cb, cl, ch, oa, ob, ol, oh):
    del f_in, src_in, inv_in, phi_in
    s = Sides()
    coefs = (ca, cb, cl, ch)
    for pair in ((0, 1), (2, 3)):
        got = []
        for i in pair:
            halo, rows, d = (ha, hb, hl, hh)[i], s.rows[i], s.dims[i]
            g = s.masks[i] * recip(hat[:, rows, :] + halo[0])
            q = (0.5 * s.signs[i]) * (g * (e[d, :, rows, :] + halo[1]))
            got.append((i, rows, g, src[:, rows, :] + q, recip(recip(inv[:, rows, :]) + g)))
        for i, rows, g, source, inverse in got:
            coefs[i][...] = g
            src[:, rows, :] = source
            inv[:, rows, :] = inverse
    f[0, :, pl.ds(0, PAD), :] = cl[...]
    f[0, :, s.rows[3], :] = ch[...]
    got = []
    for i in range(4):
        rows = s.rows[i]
        inverse = inv[:, rows, :]
        got.append((i, rows, coefs[i][...] * inverse, (-w0) * (src[:, rows, :] * inverse)))
    for i, rows, coef, value in got:
        coefs[i][...] = coef
        phi[:, rows, :] = value
    for out, rows in zip((oa, ob), s.rows):
        out[0] = phi[:, rows, :]
        out[1] = v[1, :, rows, :]
    put_planes((ol, oh), phi, f)
    for out, rows, line in zip((ol, oh), s.rows[2:], (0, NXL - 1)):
        out[SOURCE] = src[:, rows, :]
        out[INVERSE] = inv[:, rows, :]
        out[FACE_Y] = f[1, :, rows, :]
        out[FACE_Z] = f[2, :, rows, :]
        out[LINES] = jnp.zeros((NT, NYL, 128), F32)
        for j, coef in enumerate((ca, cb)):
            out[LINES, :, pl.ds(j, 1), :] = coef[:, pl.ds(line, 1), :]


def add_sides(w, phi, coefs, halos, rows):
    got = [phi[:, r, :] + w * (c[...] * h) for c, h, r in zip(coefs, halos, rows)]
    for r, value in zip(rows, got):
        phi[:, r, :] = value


def wide_edge_kernel(w, last, old, f, phi_in, ca, cb, cl, ch, kl, kh, ha, hb, hl, hh, *rest):
    del phi_in
    s = Sides()
    phi, *outs = rest[-3:]
    halves = ((ca, cb), (ha[0], hb[0])), ((cl, ch), (hl[PHI], hh[PHI]))
    for (coefs, halos), rows in zip(halves, (s.rows[:2], s.rows[2:])):
        add_sides(w, phi, coefs, halos, rows)
    beyond = (pl.ds(0, PAD), pl.ds(PAD + CELLS, PAD))
    for side, (k, h) in enumerate(((kl, hl), (kh, hh))):
        c = h[PHI]
        face = f[0, :, beyond[0], :] if side == LOW else f[0, :, s.rows[3], :]
        fy, fz = k[FACE_Y], k[FACE_Z]
        t = face * old[:, s.rows[2 + side], :] + h[BEHIND]
        t = t + fy * pltpu.roll(c, NYL - 1, 1) + pltpu.roll(fy * c, 1, 1)
        t = t + fz * z_up(c) + z_down(fz * c)
        phi[:, beyond[side], :] = s.masks[2 + side] * (c + w * ((t - k[SOURCE]) * k[INVERSE] - c))
    for out, rows, at in zip(outs, s.rows, (s.near, s.far)):
        out[0, :, pl.ds(0, NXL), :] = phi[:, rows, :]
        out[0, :, pl.ds(NXL, 8), :] = jnp.zeros(SHAPE, F32)
        for side, h in enumerate((hl, hh)):
            out[0, :, pl.ds(NXL + side, 1), :] = h[PHI, :, pl.ds(at, 1), :]
        if not last:
            v = rest[0]
            out[1, :, pl.ds(0, NXL), :] = v[2, :, rows, :]
            out[1, :, pl.ds(NXL, 8), :] = jnp.zeros(SHAPE, F32)


def narrow_edge_kernel(w, w_before, f, nu, phi_in, ca, cb, cl, ch, kl, kh, ha, hb, phi, oa, ob, ol, oh):
    del phi_in
    s = Sides()
    inner = pl.ds(0, NXL)
    add_sides(w, phi, (ca, cb), (ha[0, :, inner, :], hb[0, :, inner, :]), s.rows[:2])
    for j, (h, at) in enumerate(((ha, s.near), (hb, s.far))):
        for side, (k, c, plane) in enumerate(((kl, cl, 0), (kh, ch, NXL - 1))):
            missing = w_before * (k[LINES, :, pl.ds(j, 1), :] * h[0, :, pl.ds(NXL + side, 1), :])
            row = pl.ds(PAD + plane * NYL + at, 1)
            phi[:, row, :] = phi[:, row, :] + w * (c[:, pl.ds(at, 1), :] * missing)
    for out, rows in zip((oa, ob), s.rows):
        out[0] = phi[:, rows, :]
        out[1] = nu[:, rows, :]
    put_planes((ol, oh), phi, f)
    for out, rows in zip((ol, oh), s.rows[2:]):
        out[2] = nu[:, rows, :]


def predictor(v, nu, vnew, x0, x1):
    sub = sublanes()
    half = 0.5 * time_step

    @pl.loop(x0, x1, unroll=8)
    def _(x):
        r = row_of(x)
        for y in range(2):
            base = r + 8 * y
            at = pl.ds(base, 8)
            ups = (pl.ds(base + NYL, 8), pl.ds(base + 1, 8))
            downs = (pl.ds(base - NYL, 8), pl.ds(base - 1, 8))
            n = nu[:, at, :]
            vc = [v[c, :, at, :] for c in range(3)]
            coefs = []
            total = None
            for d in range(3):
                above = nu[:, ups[d], :] if d < 2 else z_up(n)
                below = nu[:, downs[d], :] if d < 2 else z_down(n)
                up = (n + above) - vc[d]
                down = (n + below) + vc[d]
                if d == 1 and y == 1:
                    up = jnp.where(sub == 7, 0.0, up)
                if d == 1 and y == 0:
                    down = jnp.where(sub == 0, 0.0, down)
                coefs.append((up, down))
                both = up + down
                total = both if total is None else total + both
            keep = 1.0 - half * total
            for c in range(3):
                acc = None
                for d in range(3):
                    above = v[c, :, ups[d], :] if d < 2 else z_up(vc[c])
                    below = v[c, :, downs[d], :] if d < 2 else z_down(vc[c])
                    term = coefs[d][0] * above + coefs[d][1] * below
                    acc = term if acc is None else acc + term
                vnew[c, :, at, :] = vnew[c, :, at, :] + (half * acc + keep * vc[c])


def sweep_kernel(w, phi, f, src, inv, out):
    fill_pads(out)

    def body(x, carry):
        pxm, pc = carry
        r = row_of(x)
        px, pn = [], []
        for y in range(2):
            base = r + 8 * y
            at, up, down = pl.ds(base, 8), pl.ds(base + 1, 8), pl.ds(base - 1, 8)
            pn.append(phi[:, pl.ds(base + NYL, 8), :])
            fx = f[0, :, at, :]
            c = pc[y]
            px.append(fx * c)
            t = fx * pn[y] + pxm[y]
            t = t + f[1, :, at, :] * phi[:, up, :]
            t = t + f[1, :, down, :] * phi[:, down, :]
            fz = f[2, :, at, :]
            t = t + fz * z_up(c)
            t = t + z_down(fz * c)
            out[:, at, :] = c + w * ((t - src[:, at, :]) * inv[:, at, :] - c)
        return tuple(px), tuple(pn)

    before = tuple(f[0, :, pl.ds(8 * y, 8), :] * phi[:, pl.ds(8 * y, 8), :] for y in range(2))
    start = (before, tuple(phi[:, pl.ds(PAD + 8 * y, 8), :] for y in range(2)))
    lax.fori_loop(0, NXL, body, start, unroll=16)


def sweep_predict_kernel(w, planes, phi, f, src, inv, v, nu, vnew_in, out, vnew):
    del vnew_in
    sweep_kernel(w, phi, f, src, inv, out)
    predictor(v, nu, vnew, *planes)


def sweep_load_kernel(w, planes, phi, f, src, inv, v, visc, vnew_in, out, nu, vnew, sem):
    del vnew_in
    copies = [
        pltpu.make_async_copy(visc.at[:, pl.ds(128 * t, 128)], nu.at[t, pl.ds(PAD, CELLS)], sem.at[t])
        for t in range(NT)
    ]
    for copy in copies:
        copy.start()
    fill_pads(nu)
    sweep_kernel(w, phi, f, src, inv, out)
    for copy in copies:
        copy.wait()
    predictor(v, nu, vnew, *planes)


def force_kernel(phi, hat, b, v, nu, *rest):
    flows = [rest[0:4], rest[4:6], rest[6:8], rest[8:12]]
    potential, vnew, sem = rest[13:]
    copies = [
        pltpu.make_async_copy(phi.at[t, pl.ds(PAD, CELLS)], potential.at[:, pl.ds(128 * t, 128)], sem.at[t])
        for t in range(NT)
    ]
    for copy in copies:
        copy.start()

    s = Sides()
    half = 0.5 * time_step
    inner = pl.ds(0, NXL)
    for pair in ((0, 1), (2, 3)):
        got = []
        for i in pair:
            rows, d, sign, mask = s.rows[i], s.dims[i], s.signs[i], s.masks[i]
            if d:
                other = [flows[0][i][2], flows[1][i][1], flows[2][i][1, :, inner, :]]
                hn = mask * flows[3][i][1]
            else:
                other = [flows[0][i][2 + c] for c in range(3)]
                hn = mask * flows[3][i][2]
            vc = [v[c, :, rows, :] for c in range(3)]
            coef = half * ((nu[:, rows, :] + hn) - sign * vc[d])
            gone = half * hn if d == 0 else coef
            got.append([vnew[c, :, rows, :] + (coef * (mask * other[c]) - gone * vc[c]) for c in range(3)])
        for i, values in zip(pair, got):
            for c in range(3):
                vnew[c, :, s.rows[i], :] = values[c]

    sub = sublanes()
    @pl.loop(0, NXL, unroll=8)
    def _(x):
        r = row_of(x)
        for y in range(2):
            base = r + 8 * y
            at = pl.ds(base, 8)
            raw = pl.ds(pl.multiple_of(x * NYL + 8 * y, 8), 8)
            p = phi[:, at, :]
            yu = phi[:, pl.ds(base + 1, 8), :]
            yd = phi[:, pl.ds(base - 1, 8), :]
            if y == 1:
                yu = jnp.where(sub == 7, 0.0, yu)
            else:
                yd = jnp.where(sub == 0, 0.0, yd)
            diffs = (
                phi[:, pl.ds(base + NYL, 8), :] - phi[:, pl.ds(base - NYL, 8), :],
                yu - yd,
                z_up(p) - z_down(p),
            )
            g = (-0.25 * force_gain) * recip(hat[:, at, :])
            c0, c1, c2 = (g * diff for diff in diffs)
            for t in range(NT):
                b0, b1, b2 = (b[c, raw, pl.ds(128 * t, 128)] for c in range(3))
                vnew[0, t, at, :] = vnew[0, t, at, :] + (c1[t] * b2 - c2[t] * b1)
                vnew[1, t, at, :] = vnew[1, t, at, :] + (c2[t] * b0 - c0[t] * b2)
                vnew[2, t, at, :] = vnew[2, t, at, :] + (c0[t] * b1 - c1[t] * b0)

    for copy in copies:
        copy.wait()


PARTS = 4


def last_kernel(w, ka, kb, kl, kh, cl, ch, ha, hb, vnew_in, result, vnew, sem):
    del vnew_in
    planes = NXL // PARTS
    copies = []
    for part in range(PARTS):
        s = Sides(part * planes, planes)
        some = pl.ds(part * planes, planes)
        got = []
        for k, h, rows in ((ka, ha, s.rows[0]), (kb, hb, s.rows[1])):
            halo = h[0, :, some, :]
            got += [(c, rows, vnew[c, :, rows, :] + k[j, :, some, :] * halo) for j, c in enumerate((2, 0))]
        for c, rows, value in got:
            vnew[c, :, rows, :] = value
        corners = ([(kl, cl, LOW, 0)] if part == 0 else []) + ([(kh, ch, HIGH, NXL - 1)] if part == PARTS - 1 else [])
        for k, lines, side, plane in corners:
            for j, (h, at) in enumerate(((ha, s.near), (hb, s.far))):
                missing = w * (lines[LINES, :, pl.ds(j, 1), :] * h[0, :, pl.ds(NXL + side, 1), :])
                row = pl.ds(PAD + plane * NYL + at, 1)
                for i, c in enumerate((1, 2)):
                    vnew[c, :, row, :] = vnew[c, :, row, :] + k[i, :, pl.ds(at, 1), :] * missing
        per = planes * NYL
        for t in range(NT):
            copy = pltpu.make_async_copy(
                vnew.at[:, t, pl.ds(PAD + part * per, per)],
                result.at[:, pl.ds(part * per, per), pl.ds(128 * t, 128)],
                sem.at[part, t],
            )
            copy.start()
            copies.append(copy)
    for copy in copies:
        copy.wait()


def resident(*shape):
    return pltpu.VMEM(shape, F32)


def in_vmem(x):
    return pltpu.with_memory_space_constraint(x, pltpu.VMEM)


def in_hbm(x):
    return pltpu.with_memory_space_constraint(x, pltpu.HBM)


IN_VMEM = pl.BlockSpec(memory_space=pltpu.VMEM)
IN_HBM = pl.BlockSpec(memory_space=pl.ANY)

FIELD = (NT, ROWS, 128)


def run(kernel, name, ins, outs, aliases=None, scratch=(), flops=0, moved=0, limit=6 * MIB):
    args = [in_hbm(a) if hbm else in_vmem(a) for a, hbm in ins]
    return pl.pallas_call(
        kernel,
        out_shape=outs,
        in_specs=[IN_HBM if hbm else IN_VMEM for _, hbm in ins],
        out_specs=[IN_HBM if isinstance(o, jax.ShapeDtypeStruct) else IN_VMEM for o in outs],
        input_output_aliases=aliases or {},
        scratch_shapes=list(scratch),
        compiler_params=pltpu.CompilerParams(vmem_limit_bytes=limit),
        cost_estimate=pl.CostEstimate(flops=flops, bytes_accessed=moved, transcendentals=0),
        name=name,
    )(*args)


def vm(*arrays):
    return [(a, False) for a in arrays]


def ring(axis, step):
    n = lax.axis_size(axis)
    return [(i, (i + step) % n) for i in range(n)]


def across(a, b):
    n = lax.axis_size("width") * 2
    return (
        lax.ppermute(a, "thick", [(0, 1), (1, 0)]),
        lax.ppermute(b, WIDTH, [(i, (((i + 1) ^ 1) - 1) % n) for i in range(n)]),
    )


def along(low, high):
    return lax.ppermute(high, "cast", ring("cast", 1)), lax.ppermute(low, "cast", ring("cast", -1))


def rows_of(n, planes=NXL):
    return [resident(n, NT, planes, 128)] * 2


def planes_of(n):
    return [resident(n, NT, NYL, 128)] * 2


def local(velocity, magnetic, labels, viscosity):
    vel = velocity.reshape(3, CELLS, NT * 128)
    mag = magnetic.reshape(3, CELLS, NT * 128)
    lab = labels.reshape(CELLS, NT * 128)
    visc = viscosity.reshape(CELLS, NT * 128)
    dma = pltpu.SemaphoreType.DMA
    w = [sweep_weight(k) for k in range(ITERS)]
    field, fields = resident(*FIELD), resident(3, *FIELD)
    work = dict(flops=10_000_000, moved=16 * MIB)

    v, hat, e, vnew, *edges = run(
        load_kernel, "load", [(vel, True), (mag, True), (lab, True)],
        [fields, field, fields, fields] + rows_of(3) + planes_of(5) + rows_of(2) + planes_of(2),
        scratch=[
            pltpu.VMEM((3, NT, CELLS, 128), F32),
            pltpu.VMEM((CELLS, NT * 128), jnp.int32),
            dma((CHUNKS, 2 * NT + 1)),
        ],
        limit=10 * MIB,
    )
    edges, products = edges[:4], edges[4:]
    h1 = (*across(*edges[:2]), *along(*edges[2:]))
    f, src, inv, phi = run(
        functools.partial(face_kernel, w[0]), "faces", vm(hat, e, v, vnew), [fields, field, field, field], **work
    )
    f, src, inv, phi, *rest = run(
        functools.partial(first_edge_kernel, w[0]), "edges1", vm(*h1, hat, e, v, f, src, inv, phi),
        [fields] + [field] * 3 + [resident(NT, NXL, 128)] * 2 + [resident(NT, NYL, 128)] * 2 + rows_of(2) + planes_of(7),
        aliases={7: 0, 8: 1, 9: 2, 10: 3},
    )
    coefs, edges = rest[:4], rest[4:]

    h2 = (*across(*edges[:2]), *along(*edges[2:]))
    lines = h2[2:]
    old = phi
    phi, nu, vnew = run(
        functools.partial(sweep_load_kernel, w[1], (0, 32)), "sweep1",
        vm(phi, f, src, inv, v) + [(visc, True)] + vm(vnew),
        [field, field, fields], aliases={6: 2}, scratch=[dma((NT,))], **work,
    )
    phi, *edges = run(
        functools.partial(wide_edge_kernel, w[1], False), "edges2", vm(old, f, phi, *coefs, *lines, *h2, v),
        [field] + rows_of(2, NXL + 8), aliases={2: 0},
    )

    h3 = across(*edges)
    phi, vnew = run(
        functools.partial(sweep_predict_kernel, w[2], (32, 64)), "sweep2", vm(phi, f, src, inv, v, nu, vnew),
        [field, fields], aliases={6: 1}, **work,
    )
    phi, *edges = run(
        functools.partial(narrow_edge_kernel, w[2], w[1]), "edges3", vm(f, nu, phi, *coefs, *lines, *h3),
        [field] + rows_of(2) + planes_of(3), aliases={2: 0},
    )

    h4 = (*across(*edges[:2]), *along(*edges[2:]))
    old = phi
    (phi,) = run(functools.partial(sweep_kernel, w[3]), "sweep3", vm(phi, f, src, inv), [field], **work)
    phi, *edges = run(
        functools.partial(wide_edge_kernel, w[3], True), "edges4", vm(old, f, phi, *coefs, *lines, *h4),
        [field] + rows_of(1, NXL + 8), aliases={2: 0},
    )

    h5 = across(*edges)
    potential, vnew = run(
        force_kernel, "force", vm(phi, hat, mag, v, nu, *h1, *h2[:2], *h3, *h4, vnew),
        [jax.ShapeDtypeStruct((CELLS, NT * 128), F32), fields],
        aliases={17: 1}, scratch=[dma((NT,))], **work,
    )
    result, _ = run(
        functools.partial(last_kernel, w[3]), "last", vm(*products, *lines, *h5, vnew),
        [jax.ShapeDtypeStruct((3, CELLS, NT * 128), F32), fields],
        aliases={8: 1}, scratch=[dma((PARTS, NT))],
    )
    return result.reshape(velocity.shape), potential.reshape(labels.shape)


def solution(mesh):
    fields = P(None, "cast", WIDTH, None)
    scalar = P("cast", WIDTH, None)
    return jax.shard_map(
        local,
        mesh=mesh,
        in_specs=(fields, fields, scalar, scalar),
        out_specs=(fields, scalar),
        check_vma=False,
    )
```

```python
import functools
import math

import jax
import jax.numpy as jnp
from jax import lax
from jax.experimental import pallas as pl
from jax.experimental.pallas import tpu as pltpu
from jax.sharding import PartitionSpec as P

ITERS = 4
time_step = 0.1
force_gain = 0.3

NXL = 64
NYL = 16
NT = 4
PAD = 16
CELLS = NXL * NYL
ROWS = CELLS + 2 * PAD
F32 = jnp.float32
WIDTH = ("width", "thick")
MIB = 1024 * 1024
SHAPE = (NT, 8, 128)
OUTSIDE = 1e30


def sweep_weight(k):
    return 2.0 / (2.15 + 1.75 * math.cos(math.pi * (2 * k + 1) / (2 * ITERS)))


def z_up(a, fill=0.0):
    r = pltpu.roll(a, 127, 2)
    after = jnp.concatenate([r[1:], jnp.full_like(r[:1], fill)], axis=0)
    return jnp.where(lax.broadcasted_iota(jnp.int32, a.shape, 2) == 127, after, r)


def z_down(a):
    r = pltpu.roll(a, 1, 2)
    before = jnp.concatenate([jnp.zeros_like(r[:1]), r[:-1]], axis=0)
    return jnp.where(lax.broadcasted_iota(jnp.int32, a.shape, 2) == 0, before, r)


def recip(d):
    return pltpu.reciprocal(d, approx=True)


def sublanes():
    return lax.broadcasted_iota(jnp.int32, SHAPE, 1)


def row_of(x):
    return pl.multiple_of(PAD + x * NYL, NYL)


def fill_pads(ref, value=0.0):
    lead = (slice(None),) * (len(ref.shape) - 2)
    block = jnp.full(ref.shape[:-2] + (PAD, 128), value, F32)
    ref[lead + (pl.ds(0, PAD),)] = block
    ref[lead + (pl.ds(PAD + CELLS, PAD),)] = block


class Sides:
    def __init__(self, x0=0, planes=NXL):
        thick = lax.axis_index("thick")
        place = lax.axis_index("width") * 2 + thick
        last = lax.axis_size("width") * 2 - 1
        cast = lax.axis_index("cast")
        odd = lax.rem(cast, 2)
        self.near = (NYL - 1) * (1 - thick)
        self.far = (NYL - 1) * thick
        self.high = (1 - odd, odd)
        self.edge = tuple(h * (NXL - 1) for h in self.high)

        def plane(x):
            return pl.ds(pl.multiple_of(x * NYL, NYL), NYL)

        self.beyond = tuple(plane(h * (NXL + 1)) for h in self.high)
        self.face_in = tuple(plane(h * NXL) for h in self.high)
        self.behind = tuple(plane(1 + 1 + h * (NXL - 3)) for h in self.high)
        self.face_behind = tuple(plane(1 + h * (NXL - 2)) for h in self.high)

        def rows(pad):
            start = pad + x0 * NYL
            return (
                pl.ds(start + self.near, planes, stride=NYL),
                pl.ds(start + self.far, planes, stride=NYL),
                *(plane(pad // NYL + x) for x in self.edge),
            )

        self.rows = rows(PAD)
        self.inner = rows(0)
        self.dims = (1, 1, 0, 0)

        def number(condition, yes, no):
            return jnp.where(condition, yes, no).astype(F32)

        up = number(thick == 0, 1.0, -1.0)
        ahead = number(odd == 0, 1.0, -1.0)
        self.signs = (up, -up, ahead, -ahead)
        self.masks = (
            1.0,
            number(((thick == 0) & (place > 0)) | ((thick == 1) & (place < last)), 1.0, 0.0),
            1.0,
            number((cast > 0) & (cast < lax.axis_size("cast") - 1), 1.0, 0.0),
        )


CHUNKS = 8


def load_kernel(vel, mag, lab, v, hat, e, vnew, oa, ob, ol, oh, ka, kb, kl, kh, b, lraw, sem):
    per = CELLS // CHUNKS

    def copies(ch):
        src = pl.ds(ch * per, per)
        dst = pl.ds(PAD + ch * per, per)
        for t in range(NT):
            col = pl.ds(128 * t, 128)
            yield pltpu.make_async_copy(vel.at[:, src, col], v.at[:, t, dst], sem.at[ch, t])
            yield pltpu.make_async_copy(mag.at[:, src, col], b.at[:, t, src], sem.at[ch, NT + t])
        yield pltpu.make_async_copy(lab.at[src], lraw.at[src], sem.at[ch, 2 * NT])

    for ch in range(CHUNKS):
        for copy in copies(ch):
            copy.start()
    fill_pads(v)
    fill_pads(e)
    fill_pads(hat, OUTSIDE)
    for ch in range(CHUNKS):
        for copy in copies(ch):
            copy.wait()

        @pl.loop(0, per // 8, unroll=8)
        def _(i):
            raw = pl.ds(pl.multiple_of(ch * per + i * 8, 8), 8)
            at = pl.ds(pl.multiple_of(PAD + ch * per + i * 8, 8), 8)
            for t in range(NT):
                lb = lraw[raw, pl.ds(128 * t, 128)]
                melt, shell = lb == 0, lb == 1
                hat[t, at, :] = jnp.where(melt, 0.5, jnp.where(shell, 0.5 / 0.7, 0.125)).astype(F32)
                gain = jnp.where(melt, 1.0, jnp.where(shell, 0.7, 4.0)).astype(F32) * force_gain
                v0, v1, v2 = (v[c, t, at, :] for c in range(3))
                b0, b1, b2 = (b[c, t, raw, :] for c in range(3))
                e0, e1, e2 = v1 * b2 - v2 * b1, v2 * b0 - v0 * b2, v0 * b1 - v1 * b0
                e[0, t, at, :] = e0
                e[1, t, at, :] = e1
                e[2, t, at, :] = e2
                vnew[0, t, at, :] = gain * (e1 * b2 - e2 * b1)
                vnew[1, t, at, :] = gain * (e2 * b0 - e0 * b2)
                vnew[2, t, at, :] = gain * (e0 * b1 - e1 * b0)

    sides = Sides()
    for out, rows, d in zip((oa, ob, ol, oh), sides.rows, sides.dims):
        out[0] = hat[:, rows, :]
        out[1] = e[d, :, rows, :]
        if d:
            out[2] = v[0, :, rows, :]

    for i, k in enumerate((ka, kb, kl, kh)):
        rows, at, d = sides.rows[i], sides.inner[i], sides.dims[i]
        n1, n2 = (d + 1) % 3, (d + 2) % 3
        g = (0.25 * force_gain * sides.signs[i]) * (sides.masks[i] * recip(hat[:, rows, :]))
        k[0] = g * b[n2, :, at, :]
        k[1] = -g * b[n1, :, at, :]


def faces(w0, hat, e, f, src, inv, phi):
    zero = jnp.zeros(SHAPE, F32)
    sub = sublanes()

    def body(x, carry):
        fxm, qxm, hc, exc = carry
        r = row_of(x)
        fxo, qxo, hn, exn = [], [], [], []
        for y in range(2):
            base = r + 8 * y
            at, up, down = pl.ds(base, 8), pl.ds(base + 1, 8), pl.ds(base - 1, 8)
            ahead = pl.ds(base + NYL, 8)
            c = hc[y]
            hn.append(hat[:, ahead, :])
            exn.append(e[0, :, ahead, :])
            fx = recip(c + hn[y])
            qx = fx * (exc[y] + exn[y])
            fxo.append(fx)
            qxo.append(qx)
            ey = e[1, :, at, :]
            fy = recip(c + hat[:, up, :])
            fym = recip(c + hat[:, down, :])
            if y == 1:
                fy = jnp.where(sub == 7, 0.0, fy)
            else:
                fym = jnp.where(sub == 0, 0.0, fym)
            fz = recip(c + z_up(c, OUTSIDE))
            ez = e[2, :, at, :]
            qz = fz * (ez + z_up(ez))
            total = (qx - qxm[y]) + (fy * (ey + e[1, :, up, :]) - fym * (ey + e[1, :, down, :])) + (qz - z_down(qz))
            diag = ((fx + fxm[y]) + (fy + fym)) + (fz + z_down(fz)) + 0.025 * recip(c)
            source = 0.5 * total
            inverse = recip(diag)
            f[0, :, at, :] = fx
            f[1, :, at, :] = fy
            f[2, :, at, :] = fz
            src[:, at, :] = source
            inv[:, at, :] = inverse
            phi[:, at, :] = (-w0) * (source * inverse)
        return tuple(fxo), tuple(qxo), tuple(hn), tuple(exn)

    first = [pl.ds(PAD + 8 * y, 8) for y in range(2)]
    start = (
        (zero, zero),
        (zero, zero),
        tuple(hat[:, at, :] for at in first),
        tuple(e[0, :, at, :] for at in first),
    )
    lax.fori_loop(0, NXL, body, start, unroll=8)


def face_kernel(w0, hat, e, v, vnew, f, src, inv, phi):
    del v, vnew
    f[1, :, 0:PAD, :] = jnp.zeros((NT, PAD, 128), F32)
    fill_pads(phi)
    faces(w0, hat, e, f, src, inv, phi)


SOURCE, INVERSE, BEHIND, FLOW = (pl.ds(i * NYL, NYL) for i in range(4))
LINES = 4 * NYL


def flux_behind(phi, f, s, side):
    return f[0, :, s.face_behind[side], :] * phi[:, s.behind[side], :]


def first_edge_kernel(w0, ha, hb, hl, hh, hat, e, v, f_in, src_in, inv_in, phi_in,
                      f, src, inv, phi, ca, cb, cl, ch, oa, ob, ol, oh):
    del f_in, src_in, inv_in, phi_in
    s = Sides()
    coefs = (ca, cb, cl, ch)
    for pair in ((0, 1), (2, 3)):
        got = []
        for i in pair:
            halo, rows, d = (ha, hb, hl, hh)[i], s.rows[i], s.dims[i]
            g = s.masks[i] * recip(hat[:, rows, :] + halo[0])
            q = (0.5 * s.signs[i]) * (g * (e[d, :, rows, :] + halo[1]))
            got.append((i, rows, g, src[:, rows, :] + q, recip(recip(inv[:, rows, :]) + g)))
        for i, rows, g, source, inverse in got:
            coefs[i][...] = g
            src[:, rows, :] = source
            inv[:, rows, :] = inverse
    for rows, coef in zip(s.face_in, (cl, ch)):
        f[0, :, rows, :] = coef[...]
    got = []
    for i in range(4):
        rows = s.rows[i]
        inverse = inv[:, rows, :]
        got.append((i, rows, coefs[i][...] * inverse, (-w0) * (src[:, rows, :] * inverse)))
    for i, rows, coef, value in got:
        coefs[i][...] = coef
        phi[:, rows, :] = value
    for out, rows in zip((oa, ob), s.rows):
        out[0] = phi[:, rows, :]
    for c in range(1, 3):
        oa[c] = v[c, :, s.rows[0], :]
    for i, (out, rows, x) in enumerate(zip((ol, oh), s.rows[2:], s.edge)):
        out[:, SOURCE, :] = src[:, rows, :]
        out[:, INVERSE, :] = inv[:, rows, :]
        out[:, BEHIND, :] = flux_behind(phi, f, s, i)
        out[:, FLOW, :] = v[0, :, rows, :]
        out[:, pl.ds(LINES, 8), :] = jnp.zeros(SHAPE, F32)
        for j, coef in enumerate((ca, cb)):
            out[:, pl.ds(LINES + j, 1), :] = coef[:, pl.ds(x, 1), :]


def add_sides(w, phi, coefs, halos, rows):
    got = [phi[:, r, :] + w * (c[...] * h) for c, h, r in zip(coefs, halos, rows)]
    for r, value in zip(rows, got):
        phi[:, r, :] = value


def wide_edge_kernel(w, w0, old, f, phi_in, ca, cb, cl, ch, rl, rh, kl, kh, ha, hb, *rest):
    del phi_in
    s = Sides()
    phi, *outs = rest[-3:]
    ks = (kl, kh)
    if w0 is None:
        beyond = [(h[0], h[1]) for h in rest[:2]]
    else:
        beyond = [((-w0) * (k[:, SOURCE, :] * k[:, INVERSE, :]), k[:, BEHIND, :]) for k in ks]
    halves = ((ca, cb), (ha[0], hb[0])), ((cl, ch), (beyond[0][0], beyond[1][0]))
    for (coefs, halos), rows in zip(halves, (s.rows[:2], s.rows[2:])):
        add_sides(w, phi, coefs, halos, rows)
    row = lax.broadcasted_iota(jnp.int32, (NT, NYL, 128), 1)
    for side, (r, k, (c, flux)) in enumerate(zip((rl, rh), ks, beyond)):
        hat = r[0]
        fy = jnp.where(row == NYL - 1, 0.0, recip(hat + pltpu.roll(hat, NYL - 1, 1)))
        fz = recip(hat + z_up(hat, OUTSIDE))
        t = f[0, :, s.face_in[side], :] * old[:, s.rows[2 + side], :] + flux
        t = t + fy * pltpu.roll(c, NYL - 1, 1) + pltpu.roll(fy * c, 1, 1)
        t = t + fz * z_up(c) + z_down(fz * c)
        phi[:, s.beyond[side], :] = s.masks[2 + side] * (c + w * ((t - k[:, SOURCE, :]) * k[:, INVERSE, :] - c))
    for out, rows, at in zip(outs, s.rows, (s.near, s.far)):
        out[0, :, pl.ds(0, NXL), :] = phi[:, rows, :]
        out[0, :, pl.ds(NXL, 8), :] = jnp.zeros(SHAPE, F32)
        for side, (c, _) in enumerate(beyond):
            line = jnp.sum(jnp.where(row == at, c, 0.0), axis=1, keepdims=True)
            out[0, :, pl.ds(NXL + side, 1), :] = line


def narrow_edge_kernel(w, w_before, f, v, nu, phi_in, ca, cb, cl, ch, kl, kh, ha, hb, phi, oa, ob, ol, oh):
    del phi_in
    s = Sides()
    inner = pl.ds(0, NXL)
    add_sides(w, phi, (ca, cb), (ha[0, :, inner, :], hb[0, :, inner, :]), s.rows[:2])
    for j, (h, at) in enumerate(((ha, s.near), (hb, s.far))):
        for side, (k, c, plane) in enumerate(zip((kl, kh), (cl, ch), s.edge)):
            missing = w_before * (k[:, pl.ds(LINES + j, 1), :] * h[0, :, pl.ds(NXL + side, 1), :])
            row = pl.ds(PAD + plane * NYL + at, 1)
            phi[:, row, :] = phi[:, row, :] + w * (c[:, pl.ds(at, 1), :] * missing)
    for out, rows in zip((oa, ob), s.rows):
        out[0] = phi[:, rows, :]
    oa[1] = nu[:, s.rows[0], :]
    for i, (out, rows) in enumerate(zip((ol, oh), s.rows[2:])):
        out[0] = phi[:, rows, :]
        out[1] = flux_behind(phi, f, s, i)
        out[2] = v[1, :, rows, :]
        out[3] = v[2, :, rows, :]
        out[4] = nu[:, rows, :]


def predictor(v, nu, vnew, x0, x1):
    sub = sublanes()
    half = 0.5 * time_step

    @pl.loop(x0, x1, unroll=8)
    def _(x):
        r = row_of(x)
        for y in range(2):
            base = r + 8 * y
            at = pl.ds(base, 8)
            ups = (pl.ds(base + NYL, 8), pl.ds(base + 1, 8))
            downs = (pl.ds(base - NYL, 8), pl.ds(base - 1, 8))
            n = nu[:, at, :]
            vc = [v[c, :, at, :] for c in range(3)]
            coefs = []
            total = None
            for d in range(3):
                above = nu[:, ups[d], :] if d < 2 else z_up(n)
                below = nu[:, downs[d], :] if d < 2 else z_down(n)
                up = (n + above) - vc[d]
                down = (n + below) + vc[d]
                if d == 1 and y == 1:
                    up = jnp.where(sub == 7, 0.0, up)
                if d == 1 and y == 0:
                    down = jnp.where(sub == 0, 0.0, down)
                coefs.append((up, down))
                both = up + down
                total = both if total is None else total + both
            keep = 1.0 - half * total
            for c in range(3):
                acc = None
                for d in range(3):
                    above = v[c, :, ups[d], :] if d < 2 else z_up(vc[c])
                    below = v[c, :, downs[d], :] if d < 2 else z_down(vc[c])
                    term = coefs[d][0] * above + coefs[d][1] * below
                    acc = term if acc is None else acc + term
                vnew[c, :, at, :] = vnew[c, :, at, :] + (half * acc + keep * vc[c])


def sweep_kernel(w, phi, f, src, inv, out):
    fill_pads(out)

    def body(x, carry):
        pxm, pc = carry
        r = row_of(x)
        px, pn = [], []
        for y in range(2):
            base = r + 8 * y
            at, up, down = pl.ds(base, 8), pl.ds(base + 1, 8), pl.ds(base - 1, 8)
            pn.append(phi[:, pl.ds(base + NYL, 8), :])
            fx = f[0, :, at, :]
            c = pc[y]
            px.append(fx * c)
            t = fx * pn[y] + pxm[y]
            t = t + f[1, :, at, :] * phi[:, up, :]
            t = t + f[1, :, down, :] * phi[:, down, :]
            fz = f[2, :, at, :]
            t = t + fz * z_up(c)
            t = t + z_down(fz * c)
            out[:, at, :] = c + w * ((t - src[:, at, :]) * inv[:, at, :] - c)
        return tuple(px), tuple(pn)

    before = tuple(f[0, :, pl.ds(8 * y, 8), :] * phi[:, pl.ds(8 * y, 8), :] for y in range(2))
    start = (before, tuple(phi[:, pl.ds(PAD + 8 * y, 8), :] for y in range(2)))
    lax.fori_loop(0, NXL, body, start, unroll=16)


def sweep_flow_kernel(w, phi, f, src, inv, v, nu, out, flow):
    rows = Sides().rows[1]
    flow[0] = v[1, :, rows, :]
    flow[1] = v[2, :, rows, :]
    flow[2] = nu[:, rows, :]
    sweep_kernel(w, phi, f, src, inv, out)


def predict_kernel(planes, v, nu, vnew_in, vnew):
    del vnew_in
    predictor(v, nu, vnew, *planes)


def sweep_predict_kernel(w, planes, phi, f, src, inv, v, nu, vnew_in, out, vnew):
    del vnew_in
    sweep_kernel(w, phi, f, src, inv, out)
    predictor(v, nu, vnew, *planes)


def sweep_load_kernel(w, planes, phi, f, src, inv, v, visc, vnew_in, out, nu, vnew, sem):
    del vnew_in
    copies = [
        pltpu.make_async_copy(visc.at[:, pl.ds(128 * t, 128)], nu.at[t, pl.ds(PAD, CELLS)], sem.at[t])
        for t in range(NT)
    ]
    for copy in copies:
        copy.start()
    fill_pads(nu)
    sweep_kernel(w, phi, f, src, inv, out)
    for copy in copies:
        copy.wait()
    predictor(v, nu, vnew, *planes)


def force_kernel(phi, hat, b, v, nu, *rest):
    near0, far0, near1, near2, far, first_l, first_h, low, high = rest[:9]
    sent = (
        (near0[2], near1[1], near1[2], near2[1]),
        (far0[2], far[0], far[1], far[2]),
        (first_l[:, FLOW, :], low[2], low[3], low[4]),
        (first_h[:, FLOW, :], high[2], high[3], high[4]),
    )
    potential, vnew, sem = rest[10:]
    copies = [
        pltpu.make_async_copy(phi.at[t, pl.ds(PAD, CELLS)], potential.at[:, pl.ds(128 * t, 128)], sem.at[t])
        for t in range(NT)
    ]
    for copy in copies:
        copy.start()

    s = Sides()
    half = 0.5 * time_step
    for pair in ((0, 1), (2, 3)):
        got = []
        for i in pair:
            rows, d, sign, mask = s.rows[i], s.dims[i], s.signs[i], s.masks[i]
            other = sent[i][:3]
            hn = mask * sent[i][3]
            vc = [v[c, :, rows, :] for c in range(3)]
            coef = half * ((nu[:, rows, :] + hn) - sign * vc[d])
            gone = half * hn if d == 0 else coef
            got.append([vnew[c, :, rows, :] + (coef * (mask * other[c]) - gone * vc[c]) for c in range(3)])
        for i, values in zip(pair, got):
            for c in range(3):
                vnew[c, :, s.rows[i], :] = values[c]

    sub = sublanes()
    @pl.loop(0, NXL, unroll=8)
    def _(x):
        r = row_of(x)
        for y in range(2):
            base = r + 8 * y
            at = pl.ds(base, 8)
            raw = pl.ds(pl.multiple_of(x * NYL + 8 * y, 8), 8)
            p = phi[:, at, :]
            yu = phi[:, pl.ds(base + 1, 8), :]
            yd = phi[:, pl.ds(base - 1, 8), :]
            if y == 1:
                yu = jnp.where(sub == 7, 0.0, yu)
            else:
                yd = jnp.where(sub == 0, 0.0, yd)
            diffs = (
                phi[:, pl.ds(base + NYL, 8), :] - phi[:, pl.ds(base - NYL, 8), :],
                yu - yd,
                z_up(p) - z_down(p),
            )
            g = (-0.25 * force_gain) * recip(hat[:, at, :])
            c0, c1, c2 = (g * diff for diff in diffs)
            for t in range(NT):
                b0, b1, b2 = (b[c, raw, pl.ds(128 * t, 128)] for c in range(3))
                vnew[0, t, at, :] = vnew[0, t, at, :] + (c1[t] * b2 - c2[t] * b1)
                vnew[1, t, at, :] = vnew[1, t, at, :] + (c2[t] * b0 - c0[t] * b2)
                vnew[2, t, at, :] = vnew[2, t, at, :] + (c0[t] * b1 - c1[t] * b0)

    for copy in copies:
        copy.wait()


PARTS = 4


def last_kernel(w, ka, kb, kl, kh, cl, ch, ha, hb, vnew_in, result, vnew, sem):
    del vnew_in
    planes = NXL // PARTS
    copies = []
    s = Sides()
    for side, (k, lines, plane) in enumerate(zip((kl, kh), (cl, ch), s.edge)):
        for j, (h, at) in enumerate(((ha, s.near), (hb, s.far))):
            missing = w * (lines[:, pl.ds(LINES + j, 1), :] * h[0, :, pl.ds(NXL + side, 1), :])
            row = pl.ds(PAD + plane * NYL + at, 1)
            for i, c in enumerate((1, 2)):
                vnew[c, :, row, :] = vnew[c, :, row, :] + k[i, :, pl.ds(at, 1), :] * missing
    for part in range(PARTS):
        s = Sides(part * planes, planes)
        some = pl.ds(part * planes, planes)
        got = []
        for k, h, rows in ((ka, ha, s.rows[0]), (kb, hb, s.rows[1])):
            halo = h[0, :, some, :]
            got += [(c, rows, vnew[c, :, rows, :] + k[j, :, some, :] * halo) for j, c in enumerate((2, 0))]
        for c, rows, value in got:
            vnew[c, :, rows, :] = value
        per = planes * NYL
        for t in range(NT):
            copy = pltpu.make_async_copy(
                vnew.at[:, t, pl.ds(PAD + part * per, per)],
                result.at[:, pl.ds(part * per, per), pl.ds(128 * t, 128)],
                sem.at[part, t],
            )
            copy.start()
            copies.append(copy)
    for copy in copies:
        copy.wait()


def resident(*shape):
    return pltpu.VMEM(shape, F32)


def in_vmem(x):
    return pltpu.with_memory_space_constraint(x, pltpu.VMEM)


def in_hbm(x):
    return pltpu.with_memory_space_constraint(x, pltpu.HBM)


IN_VMEM = pl.BlockSpec(memory_space=pltpu.VMEM)
IN_HBM = pl.BlockSpec(memory_space=pl.ANY)

FIELD = (NT, ROWS, 128)


def run(kernel, name, ins, outs, aliases=None, scratch=(), flops=0, moved=0, limit=6 * MIB):
    args = [in_hbm(a) if hbm else in_vmem(a) for a, hbm in ins]
    return pl.pallas_call(
        kernel,
        out_shape=outs,
        in_specs=[IN_HBM if hbm else IN_VMEM for _, hbm in ins],
        out_specs=[IN_HBM if isinstance(o, jax.ShapeDtypeStruct) else IN_VMEM for o in outs],
        input_output_aliases=aliases or {},
        scratch_shapes=list(scratch),
        compiler_params=pltpu.CompilerParams(vmem_limit_bytes=limit),
        cost_estimate=pl.CostEstimate(flops=flops, bytes_accessed=moved, transcendentals=0),
        name=name,
    )(*args)


def vm(*arrays):
    return [(a, False) for a in arrays]


def next_chip(b):
    n = lax.axis_size("width") * 2
    return lax.ppermute(b, WIDTH, [(i, (((i + 1) ^ 1) - 1) % n) for i in range(n)])


def across(a, b):
    return lax.ppermute(a, "thick", [(0, 1), (1, 0)]), next_chip(b)


def along(a, b):
    n, m = lax.axis_size("cast"), lax.axis_size("width") * 2
    second = []
    for i in range(n):
        j = ((i + 1) ^ 1) - 1
        second += [(i * m + k, j * m + k if 0 <= j < n else i * m + (k ^ 1)) for k in range(m)]
    return (
        lax.ppermute(a, "cast", [(i, i ^ 1) for i in range(n)]),
        lax.ppermute(b, ("cast", *WIDTH), second),
    )


def rows_of(n, planes=NXL):
    return [resident(n, NT, planes, 128)] * 2


def planes_of(n):
    return [resident(n, NT, NYL, 128)] * 2


def local(velocity, magnetic, labels, viscosity):
    vel = velocity.reshape(3, CELLS, NT * 128)
    mag = magnetic.reshape(3, CELLS, NT * 128)
    lab = labels.reshape(CELLS, NT * 128)
    visc = viscosity.reshape(CELLS, NT * 128)
    dma = pltpu.SemaphoreType.DMA
    w = [sweep_weight(k) for k in range(ITERS)]
    field, fields = resident(*FIELD), resident(3, *FIELD)
    work = dict(flops=10_000_000, moved=16 * MIB)

    v, hat, e, vnew, *edges = run(
        load_kernel, "load", [(vel, True), (mag, True), (lab, True)],
        [fields, field, fields, fields] + rows_of(3) + planes_of(2) + rows_of(2) + planes_of(2),
        scratch=[
            pltpu.VMEM((3, NT, CELLS, 128), F32),
            pltpu.VMEM((CELLS, NT * 128), jnp.int32),
            dma((CHUNKS, 2 * NT + 1)),
        ],
        limit=10 * MIB,
    )
    edges, products = edges[:4], edges[4:]
    h1 = (*across(*edges[:2]), *along(*edges[2:]))
    f, src, inv, phi = run(
        functools.partial(face_kernel, w[0]), "faces", vm(hat, e, v, vnew), [fields, field, field, field], **work
    )
    f, src, inv, phi, *rest = run(
        functools.partial(first_edge_kernel, w[0]), "edges1", vm(*h1, hat, e, v, f, src, inv, phi),
        [fields] + [field] * 3 + [resident(NT, NXL, 128)] * 2 + [resident(NT, NYL, 128)] * 2
        + [resident(3, NT, NXL, 128), resident(1, NT, NXL, 128)] + [resident(NT, LINES + 8, 128)] * 2,
        aliases={7: 0, 8: 1, 9: 2, 10: 3},
    )
    coefs, edges = rest[:4], rest[4:]

    h2 = (*across(*edges[:2]), *along(*edges[2:]))
    lines = h2[2:]
    old = phi
    phi, nu, vnew = run(
        functools.partial(sweep_load_kernel, w[1], (0, 24)), "sweep1",
        vm(phi, f, src, inv, v) + [(visc, True)] + vm(vnew),
        [field, field, fields], aliases={6: 2}, scratch=[dma((NT,))], **work,
    )
    phi, *edges = run(
        functools.partial(wide_edge_kernel, w[1], w[0]), "edges2", vm(old, f, phi, *coefs, *h1[2:], *lines, *h2[:2]),
        [field] + rows_of(1, NXL + 8), aliases={2: 0},
    )

    h3 = across(*edges)
    phi, flow = run(
        functools.partial(sweep_flow_kernel, w[2]), "sweep2", vm(phi, f, src, inv, v, nu),
        [field, resident(3, NT, NXL, 128)], **work,
    )
    (vnew,) = run(
        functools.partial(predict_kernel, (24, 48)), "predict", vm(v, nu, vnew), [fields], aliases={2: 0}, **work
    )
    flow = next_chip(flow)
    phi, *edges = run(
        functools.partial(narrow_edge_kernel, w[2], w[1]), "edges3", vm(f, v, nu, phi, *coefs, *lines, *h3),
        [field, resident(2, NT, NXL, 128), resident(1, NT, NXL, 128)] + planes_of(5), aliases={3: 0},
    )

    h4 = (*across(*edges[:2]), *along(*edges[2:]))
    old = phi
    phi, vnew = run(
        functools.partial(sweep_predict_kernel, w[3], (48, 64)), "sweep3", vm(phi, f, src, inv, v, nu, vnew),
        [field, fields], aliases={6: 1}, **work,
    )
    phi, *edges = run(
        functools.partial(wide_edge_kernel, w[3], None), "edges4",
        vm(old, f, phi, *coefs, *h1[2:], *lines, *h4, flow),
        [field] + rows_of(1, NXL + 8), aliases={2: 0},
    )

    h5 = across(*edges)
    potential, vnew = run(
        force_kernel, "force", vm(phi, hat, mag, v, nu, *h1[:2], h2[0], h4[0], flow, *lines, *h4[2:], vnew),
        [jax.ShapeDtypeStruct((CELLS, NT * 128), F32), fields],
        aliases={14: 1}, scratch=[dma((NT,))], **work,
    )
    result, _ = run(
        functools.partial(last_kernel, w[3]), "last", vm(*products, *lines, *h5, vnew),
        [jax.ShapeDtypeStruct((3, CELLS, NT * 128), F32), fields],
        aliases={8: 1}, scratch=[dma((PARTS, NT))],
    )
    return result.reshape(velocity.shape), potential.reshape(labels.shape)


def solution(mesh):
    fields = P(None, "cast", WIDTH, None)
    scalar = P("cast", WIDTH, None)
    return jax.shard_map(
        local,
        mesh=mesh,
        in_specs=(fields, fields, scalar, scalar),
        out_specs=(fields, scalar),
        check_vma=False,
    )
```

```python
import functools
import math

import jax
import jax.numpy as jnp
from jax import lax
from jax.experimental import pallas as pl
from jax.experimental.pallas import tpu as pltpu
from jax.sharding import PartitionSpec as P

ITERS = 4
time_step = 0.1
force_gain = 0.3

NXL = 64
NYL = 16
NT = 4
PAD = 16
CELLS = NXL * NYL
ROWS = CELLS + 2 * PAD
F32 = jnp.float32
WIDTH = ("width", "thick")
MIB = 1024 * 1024
SHAPE = (NT, 8, 128)
OUTSIDE = 1e30


def sweep_weight(k):
    return 2.0 / (2.15 + 1.75 * math.cos(math.pi * (2 * k + 1) / (2 * ITERS)))


def z_up(a, fill=0.0):
    r = pltpu.roll(a, 127, 2)
    after = jnp.concatenate([r[1:], jnp.full_like(r[:1], fill)], axis=0)
    return jnp.where(lax.broadcasted_iota(jnp.int32, a.shape, 2) == 127, after, r)


def z_down(a, fill=0.0):
    r = pltpu.roll(a, 1, 2)
    before = jnp.concatenate([jnp.full_like(r[:1], fill), r[:-1]], axis=0)
    return jnp.where(lax.broadcasted_iota(jnp.int32, a.shape, 2) == 0, before, r)


def recip(d):
    return pltpu.reciprocal(d, approx=True)


def sublanes():
    return lax.broadcasted_iota(jnp.int32, SHAPE, 1)


def row_of(x):
    return pl.multiple_of(PAD + x * NYL, NYL)


def fill_pads(ref, value=0.0):
    lead = (slice(None),) * (len(ref.shape) - 2)
    block = jnp.full(ref.shape[:-2] + (PAD, 128), value, F32)
    ref[lead + (pl.ds(0, PAD),)] = block
    ref[lead + (pl.ds(PAD + CELLS, PAD),)] = block


class Sides:
    def __init__(self, x0=0, planes=NXL):
        thick = lax.axis_index("thick")
        place = lax.axis_index("width") * 2 + thick
        last = lax.axis_size("width") * 2 - 1
        cast = lax.axis_index("cast")
        odd = lax.rem(cast, 2)
        self.near = (NYL - 1) * (1 - thick)
        self.far = (NYL - 1) * thick
        self.high = (1 - odd, odd)
        self.edge = tuple(h * (NXL - 1) for h in self.high)

        def plane(x):
            return pl.ds(pl.multiple_of(x * NYL, NYL), NYL)

        self.beyond = tuple(plane(h * (NXL + 1)) for h in self.high)
        self.face_in = tuple(plane(h * NXL) for h in self.high)
        self.behind = tuple(plane(1 + 1 + h * (NXL - 3)) for h in self.high)
        self.face_behind = tuple(plane(1 + h * (NXL - 2)) for h in self.high)

        def rows(pad):
            start = pad + x0 * NYL
            return (
                pl.ds(start + self.near, planes, stride=NYL),
                pl.ds(start + self.far, planes, stride=NYL),
                *(plane(pad // NYL + x) for x in self.edge),
            )

        self.rows = rows(PAD)
        self.inner = rows(0)
        self.dims = (1, 1, 0, 0)

        def number(condition, yes, no):
            return jnp.where(condition, yes, no).astype(F32)

        up = number(thick == 0, 1.0, -1.0)
        ahead = number(odd == 0, 1.0, -1.0)
        self.signs = (up, -up, ahead, -ahead)
        self.masks = (
            1.0,
            number(((thick == 0) & (place > 0)) | ((thick == 1) & (place < last)), 1.0, 0.0),
            1.0,
            number((cast > 0) & (cast < lax.axis_size("cast") - 1), 1.0, 0.0),
        )


CHUNKS = 4
PER = CELLS // CHUNKS


def columns(source, chunk, target, sem, pad):
    rows = pl.ds(chunk * PER, PER)
    at = pl.ds(pad + chunk * PER, PER)
    return [pltpu.make_async_copy(source.at[rows, pl.ds(128 * t, 128)], target.at[t, at], sem(t)) for t in range(NT)]


def load_kernel(vel, mag, lab, v, b, hat, e, oa, ob, ol, oh, lraw, ve, be, sem, edge_sem):
    s = Sides()

    def copies(ch):
        some = pl.ds(ch * PER, PER)
        out = [pltpu.make_async_copy(lab.at[some], lraw.at[some], sem.at[ch, 4 * NT])]
        for i, comp in enumerate((0, 2)):
            out += columns(vel.at[comp], ch, v.at[comp], lambda t: sem.at[ch, i * NT + t], PAD)
            out += columns(mag.at[comp], ch, b.at[i], lambda t: sem.at[ch, (2 + i) * NT + t], 0)
        return out

    outer = []
    for i in range(2):
        rows = s.inner[2 + i]
        outer += [
            pltpu.make_async_copy(vel.at[1, rows], ve.at[i], edge_sem.at[i, 0]),
            pltpu.make_async_copy(mag.at[1, rows], be.at[i], edge_sem.at[i, 1]),
        ]
    chunks = [copies(ch) for ch in range(CHUNKS)]
    for copy in chunks[0] + outer + [copy for chunk in chunks[1:] for copy in chunk]:
        copy.start()
    fill_pads(v)
    fill_pads(e)
    fill_pads(hat, OUTSIDE)
    for ch in range(CHUNKS):
        for copy in chunks[ch]:
            copy.wait()

        @pl.loop(0, PER // 8, unroll=8)
        def _(i):
            raw = pl.ds(pl.multiple_of(ch * PER + i * 8, 8), 8)
            at = pl.ds(pl.multiple_of(PAD + ch * PER + i * 8, 8), 8)
            for t in range(NT):
                label = lraw[raw, pl.ds(128 * t, 128)]
                hat[t, at, :] = jnp.where(label == 0, 0.5, jnp.where(label == 1, 0.5 / 0.7, 0.125)).astype(F32)
                e[1, t, at, :] = v[2, t, at, :] * b[0, t, raw, :] - v[0, t, at, :] * b[1, t, raw, :]

    for copy in outer:
        copy.wait()
    for i, out in enumerate((ol, oh)):
        rows, inner = s.rows[2 + i], s.inner[2 + i]
        out[0] = hat[:, rows, :]
        for t in range(NT):
            col = pl.ds(128 * t, 128)
            out[1, t] = ve[i, :, col] * b[1, t, inner, :] - v[2, t, rows, :] * be[i, :, col]
    for out, rows in zip((oa, ob), s.rows):
        out[0] = hat[:, rows, :]
        out[1] = e[1, :, rows, :]
    ob[2] = v[0, :, s.rows[1], :]


def rest_kernel(w0, vel, mag, visc, hat, b, v_in, e_in, v, e, vnew, f, src, inv, phi, nu, near,
                ka, kb, kl, kh, mid, sem, visc_sem):
    del v_in, e_in
    chunks = [
        columns(vel.at[1], ch, v.at[1], lambda t: sem.at[ch, t], PAD)
        + columns(mag.at[1], ch, mid, lambda t: sem.at[ch, NT + t], 0)
        for ch in range(CHUNKS)
    ]
    last = [
        pltpu.make_async_copy(visc.at[:, pl.ds(128 * t, 128)], nu.at[t, pl.ds(PAD, CELLS)], visc_sem.at[t])
        for t in range(NT)
    ]
    for copy in [copy for chunk in chunks for copy in chunk] + last:
        copy.start()
    f[1, :, 0:PAD, :] = jnp.zeros((NT, PAD, 128), F32)
    fill_pads(phi)
    fill_pads(nu)
    for ch in range(CHUNKS):
        for copy in chunks[ch]:
            copy.wait()

        @pl.loop(0, PER // 8, unroll=8)
        def _(i):
            raw = pl.ds(pl.multiple_of(ch * PER + i * 8, 8), 8)
            at = pl.ds(pl.multiple_of(PAD + ch * PER + i * 8, 8), 8)
            v0, v1, v2 = (v[c, :, at, :] for c in range(3))
            b0, b1, b2 = b[0, :, raw, :], mid[:, raw, :], b[1, :, raw, :]
            e1 = e[1, :, at, :]
            e0, e2 = v1 * b2 - v2 * b1, v0 * b1 - v1 * b0
            e[0, :, at, :] = e0
            e[2, :, at, :] = e2
            gain = (0.5 * force_gain) * recip(hat[:, at, :])
            vnew[0, :, at, :] = gain * (e1 * b2 - e2 * b1)
            vnew[1, :, at, :] = gain * (e2 * b0 - e0 * b2)
            vnew[2, :, at, :] = gain * (e0 * b1 - e1 * b0)

    faces(w0, hat, e, f, src, inv, phi)
    s = Sides()
    fields = [b.at[0], mid, b.at[1]]
    for i, k in enumerate((ka, kb, kl, kh)):
        rows, at, d = s.rows[i], s.inner[i], s.dims[i]
        n1, n2 = (d + 1) % 3, (d + 2) % 3
        g = (0.25 * force_gain * s.signs[i]) * (s.masks[i] * recip(hat[:, rows, :]))
        k[0] = g * fields[n2][:, at, :]
        k[1] = -g * fields[n1][:, at, :]
    for copy in last:
        copy.wait()
    for c in range(3):
        near[c] = v[c, :, s.rows[0], :]
    near[3] = nu[:, s.rows[0], :]


def faces(w0, hat, e, f, src, inv, phi):
    zero = jnp.zeros(SHAPE, F32)
    sub = sublanes()

    def body(x, carry):
        fxm, qxm, hc, exc = carry
        r = row_of(x)
        fxo, qxo, hn, exn = [], [], [], []
        for y in range(2):
            base = r + 8 * y
            at, up, down = pl.ds(base, 8), pl.ds(base + 1, 8), pl.ds(base - 1, 8)
            ahead = pl.ds(base + NYL, 8)
            c = hc[y]
            hn.append(hat[:, ahead, :])
            exn.append(e[0, :, ahead, :])
            fx = recip(c + hn[y])
            qx = fx * (exc[y] + exn[y])
            fxo.append(fx)
            qxo.append(qx)
            ey = e[1, :, at, :]
            fy = recip(c + hat[:, up, :])
            fym = recip(c + hat[:, down, :])
            if y == 1:
                fy = jnp.where(sub == 7, 0.0, fy)
            else:
                fym = jnp.where(sub == 0, 0.0, fym)
            ez = e[2, :, at, :]
            fz = recip(c + z_up(c, OUTSIDE))
            fzm = recip(c + z_down(c, OUTSIDE))
            qy = fy * (ey + e[1, :, up, :]) - fym * (ey + e[1, :, down, :])
            qz = fz * (ez + z_up(ez)) - fzm * (ez + z_down(ez))
            source = 0.5 * (((qx - qxm[y]) + qy) + qz)
            inverse = recip((((fx + fxm[y]) + (fy + fym)) + (fz + fzm)) + 0.025 * recip(c))
            f[0, :, at, :] = fx
            f[1, :, at, :] = fy
            f[2, :, at, :] = fz
            src[:, at, :] = source
            inv[:, at, :] = inverse
            phi[:, at, :] = (-w0) * (source * inverse)
        return tuple(fxo), tuple(qxo), tuple(hn), tuple(exn)

    first = [pl.ds(PAD + 8 * y, 8) for y in range(2)]
    start = (
        (zero, zero),
        (zero, zero),
        tuple(hat[:, at, :] for at in first),
        tuple(e[0, :, at, :] for at in first),
    )
    lax.fori_loop(0, NXL, body, start, unroll=8)


SOURCE, INVERSE, BEHIND, *FLOW = (pl.ds(i * NYL, NYL) for i in range(6))
LINES = 6 * NYL


def flux_behind(phi, f, s, side):
    return f[0, :, s.face_behind[side], :] * phi[:, s.behind[side], :]


def first_edge_kernel(w0, ha, hb, hl, hh, sa, sb, sl, sh, v, near, f_in, src_in, inv_in, phi_in,
                      f, src, inv, phi, ca, cb, cl, ch, oa, ob, ol, oh):
    del f_in, src_in, inv_in, phi_in
    s = Sides()
    halos, sent, coefs = (ha, hb, hl, hh), (sa, sb, sl, sh), (ca, cb, cl, ch)

    def add(i):
        rows = s.rows[i]
        g = s.masks[i] * recip(sent[i][0] + halos[i][0])
        source = src[:, rows, :] + (0.5 * s.signs[i]) * (g * (sent[i][1] + halos[i][1]))
        return g, source, recip(recip(inv[:, rows, :]) + g)

    got = [add(i) for i in (2, 3)]
    for i, (g, source, inverse) in zip((2, 3), got):
        rows = s.rows[i]
        f[0, :, s.face_in[i - 2], :] = g
        coefs[i][...] = g
        src[:, rows, :] = source
        inv[:, rows, :] = inverse
        phi[:, rows, :] = (-w0) * (source * inverse)
    got = [add(i) for i in (0, 1)]
    for i, (g, source, inverse) in zip((0, 1), got):
        rows = s.rows[i]
        value = (-w0) * (source * inverse)
        coefs[i][...] = g * inverse
        src[:, rows, :] = source
        inv[:, rows, :] = inverse
        phi[:, rows, :] = value
        (oa, ob)[i][0] = value
    for c in range(3):
        oa[1 + c] = near[c]
    for i, (out, rows, x) in enumerate(zip((ol, oh), s.rows[2:], s.edge)):
        inverse = inv[:, rows, :]
        coefs[2 + i][...] = coefs[2 + i][...] * inverse
        out[:, SOURCE, :] = src[:, rows, :]
        out[:, INVERSE, :] = inverse
        out[:, BEHIND, :] = flux_behind(phi, f, s, i)
        for c in range(3):
            out[:, FLOW[c], :] = v[c, :, rows, :]
        out[:, pl.ds(LINES, 8), :] = jnp.zeros(SHAPE, F32)
        for j, coef in enumerate((ca, cb)):
            out[:, pl.ds(LINES + j, 1), :] = coef[:, pl.ds(x, 1), :]


def add_sides(w, phi, coefs, halos, rows):
    got = [phi[:, r, :] + w * (c[...] * h) for c, h, r in zip(coefs, halos, rows)]
    for r, value in zip(rows, got):
        phi[:, r, :] = value
    return got


def wide_edge_kernel(w, w0, old, f, phi_in, ca, cb, cl, ch, rl, rh, kl, kh, ha, hb, *rest):
    del phi_in
    s = Sides()
    phi, *outs = rest[-3:]
    ks = (kl, kh)
    if w0 is None:
        beyond = [(h[0], h[1]) for h in rest[:2]]
    else:
        beyond = [((-w0) * (k[:, SOURCE, :] * k[:, INVERSE, :]), k[:, BEHIND, :]) for k in ks]
    add_sides(w, phi, (cl, ch), (beyond[0][0], beyond[1][0]), s.rows[2:])
    edges = add_sides(w, phi, (ca, cb), (ha[0], hb[0]), s.rows[:2])
    row = lax.broadcasted_iota(jnp.int32, (NT, NYL, 128), 1)
    for side, (r, k, (c, flux)) in enumerate(zip((rl, rh), ks, beyond)):
        hat = r[0]
        fy = jnp.where(row == NYL - 1, 0.0, recip(hat + pltpu.roll(hat, NYL - 1, 1)))
        fz = recip(hat + z_up(hat, OUTSIDE))
        t = f[0, :, s.face_in[side], :] * old[:, s.rows[2 + side], :] + flux
        t = t + fy * pltpu.roll(c, NYL - 1, 1) + pltpu.roll(fy * c, 1, 1)
        t = t + fz * z_up(c) + z_down(fz * c)
        phi[:, s.beyond[side], :] = s.masks[2 + side] * (c + w * ((t - k[:, SOURCE, :]) * k[:, INVERSE, :] - c))
    for out, values, at in zip(outs, edges, (s.near, s.far)):
        out[0, :, pl.ds(0, NXL), :] = values
        more = out.shape[2] - NXL
        out[0, :, pl.ds(NXL, more), :] = jnp.zeros((NT, more, 128), F32)
        for side, (c, _) in enumerate(beyond):
            line = jnp.sum(jnp.where(row == at, c, 0.0), axis=1, keepdims=True)
            out[0, :, pl.ds(NXL + side, 1), :] = line


def narrow_edge_kernel(w, w_before, f, nu, near, phi_in, ca, cb, cl, ch, kl, kh, ha, hb, phi, oa, ob, ol, oh):
    del phi_in
    s = Sides()
    for j, (h, at) in enumerate(((ha, s.near), (hb, s.far))):
        for side, (k, c, plane) in enumerate(zip((kl, kh), (cl, ch), s.edge)):
            missing = w_before * (k[:, pl.ds(LINES + j, 1), :] * h[0, :, pl.ds(NXL + side, 1), :])
            row = pl.ds(PAD + plane * NYL + at, 1)
            phi[:, row, :] = phi[:, row, :] + w * (c[:, pl.ds(at, 1), :] * missing)
    inner = pl.ds(0, NXL)
    oa[0], ob[0] = add_sides(w, phi, (ca, cb), (ha[0, :, inner, :], hb[0, :, inner, :]), s.rows[:2])
    oa[1] = near[3]
    for i, (out, rows) in enumerate(zip((ol, oh), s.rows[2:])):
        out[0] = phi[:, rows, :]
        out[1] = flux_behind(phi, f, s, i)
        out[2] = nu[:, rows, :]


def predictor(v, nu, vnew, x0, x1):
    sub = sublanes()
    half = 0.5 * time_step

    @pl.loop(x0, x1, unroll=8)
    def _(x):
        r = row_of(x)
        for y in range(2):
            base = r + 8 * y
            at = pl.ds(base, 8)
            ups = (pl.ds(base + NYL, 8), pl.ds(base + 1, 8))
            downs = (pl.ds(base - NYL, 8), pl.ds(base - 1, 8))
            n = nu[:, at, :]
            vc = [v[c, :, at, :] for c in range(3)]
            coefs = []
            total = None
            for d in range(3):
                above = nu[:, ups[d], :] if d < 2 else z_up(n)
                below = nu[:, downs[d], :] if d < 2 else z_down(n)
                up = (n + above) - vc[d]
                down = (n + below) + vc[d]
                if d == 1 and y == 1:
                    up = jnp.where(sub == 7, 0.0, up)
                if d == 1 and y == 0:
                    down = jnp.where(sub == 0, 0.0, down)
                coefs.append((up, down))
                both = up + down
                total = both if total is None else total + both
            keep = 1.0 - half * total
            for c in range(3):
                acc = None
                for d in range(3):
                    above = v[c, :, ups[d], :] if d < 2 else z_up(vc[c])
                    below = v[c, :, downs[d], :] if d < 2 else z_down(vc[c])
                    term = coefs[d][0] * above + coefs[d][1] * below
                    acc = term if acc is None else acc + term
                vnew[c, :, at, :] = vnew[c, :, at, :] + (half * acc + keep * vc[c])


def sweep_kernel(w, phi, f, src, inv, out):
    fill_pads(out)

    def body(x, carry):
        pxm, pc = carry
        r = row_of(x)
        px, pn = [], []
        for y in range(2):
            base = r + 8 * y
            at, up, down = pl.ds(base, 8), pl.ds(base + 1, 8), pl.ds(base - 1, 8)
            pn.append(phi[:, pl.ds(base + NYL, 8), :])
            fx = f[0, :, at, :]
            c = pc[y]
            px.append(fx * c)
            t = fx * pn[y] + pxm[y]
            t = t + f[1, :, at, :] * phi[:, up, :]
            t = t + f[1, :, down, :] * phi[:, down, :]
            fz = f[2, :, at, :]
            t = t + fz * z_up(c)
            t = t + z_down(fz * c)
            out[:, at, :] = c + w * ((t - src[:, at, :]) * inv[:, at, :] - c)
        return tuple(px), tuple(pn)

    before = tuple(f[0, :, pl.ds(8 * y, 8), :] * phi[:, pl.ds(8 * y, 8), :] for y in range(2))
    start = (before, tuple(phi[:, pl.ds(PAD + 8 * y, 8), :] for y in range(2)))
    lax.fori_loop(0, NXL, body, start, unroll=16)


def sweep_flow_kernel(w, phi, f, src, inv, v, nu, out, flow):
    rows = Sides().rows[1]
    flow[0] = v[1, :, rows, :]
    flow[1] = v[2, :, rows, :]
    flow[2] = nu[:, rows, :]
    sweep_kernel(w, phi, f, src, inv, out)


def sweep_predict_kernel(w, planes, phi, f, src, inv, v, nu, vnew_in, out, vnew):
    del vnew_in
    sweep_kernel(w, phi, f, src, inv, out)
    predictor(v, nu, vnew, *planes)


def force_kernel(phi, hat, b, v, nu, *rest):
    far0, near, near_nu, far, *along = rest[:8]
    sent = (
        (near[1], near[2], near[3], near_nu[1]),
        (far0[2], far[0], far[1], far[2]),
        *((*(along[i][:, rows, :] for rows in FLOW), along[2 + i][2]) for i in range(2)),
    )
    potential, vnew, sem = rest[9:]
    copies = [
        pltpu.make_async_copy(phi.at[t, pl.ds(PAD, CELLS)], potential.at[:, pl.ds(128 * t, 128)], sem.at[t])
        for t in range(NT)
    ]
    for copy in copies:
        copy.start()

    s = Sides()
    half = 0.5 * time_step
    for pair in ((0, 1), (2, 3)):
        got = []
        for i in pair:
            rows, d, sign, mask = s.rows[i], s.dims[i], s.signs[i], s.masks[i]
            other = sent[i][:3]
            hn = mask * sent[i][3]
            vc = [v[c, :, rows, :] for c in range(3)]
            coef = half * ((nu[:, rows, :] + hn) - sign * vc[d])
            gone = half * hn if d == 0 else coef
            got.append([vnew[c, :, rows, :] + (coef * (mask * other[c]) - gone * vc[c]) for c in range(3)])
        for i, values in zip(pair, got):
            for c in range(3):
                vnew[c, :, s.rows[i], :] = values[c]

    sub = sublanes()
    @pl.loop(0, NXL, unroll=8)
    def _(x):
        r = row_of(x)
        for y in range(2):
            base = r + 8 * y
            at = pl.ds(base, 8)
            raw = pl.ds(pl.multiple_of(x * NYL + 8 * y, 8), 8)
            p = phi[:, at, :]
            yu = phi[:, pl.ds(base + 1, 8), :]
            yd = phi[:, pl.ds(base - 1, 8), :]
            if y == 1:
                yu = jnp.where(sub == 7, 0.0, yu)
            else:
                yd = jnp.where(sub == 0, 0.0, yd)
            diffs = (
                phi[:, pl.ds(base + NYL, 8), :] - phi[:, pl.ds(base - NYL, 8), :],
                yu - yd,
                z_up(p) - z_down(p),
            )
            g = (-0.25 * force_gain) * recip(hat[:, at, :])
            c0, c1, c2 = (g * diff for diff in diffs)
            for t in range(NT):
                b0, b1, b2 = (b[c, raw, pl.ds(128 * t, 128)] for c in range(3))
                vnew[0, t, at, :] = vnew[0, t, at, :] + (c1[t] * b2 - c2[t] * b1)
                vnew[1, t, at, :] = vnew[1, t, at, :] + (c2[t] * b0 - c0[t] * b2)
                vnew[2, t, at, :] = vnew[2, t, at, :] + (c0[t] * b1 - c1[t] * b0)

    for copy in copies:
        copy.wait()


PARTS = 4


def last_kernel(w, ka, kb, kl, kh, cl, ch, ha, hb, vnew_in, result, vnew, sem):
    del vnew_in
    planes = NXL // PARTS
    copies = []
    s = Sides()
    for side, (k, lines, plane) in enumerate(zip((kl, kh), (cl, ch), s.edge)):
        for j, (h, at) in enumerate(((ha, s.near), (hb, s.far))):
            missing = w * (lines[:, pl.ds(LINES + j, 1), :] * h[0, :, pl.ds(NXL + side, 1), :])
            row = pl.ds(PAD + plane * NYL + at, 1)
            for i, c in enumerate((1, 2)):
                vnew[c, :, row, :] = vnew[c, :, row, :] + k[i, :, pl.ds(at, 1), :] * missing
    for part in range(PARTS):
        s = Sides(part * planes, planes)
        some = pl.ds(part * planes, planes)
        got = []
        for k, h, rows in ((ka, ha, s.rows[0]), (kb, hb, s.rows[1])):
            halo = h[0, :, some, :]
            got += [(c, rows, vnew[c, :, rows, :] + k[j, :, some, :] * halo) for j, c in enumerate((2, 0))]
        for c, rows, value in got:
            vnew[c, :, rows, :] = value
        per = planes * NYL
        for t in range(NT):
            copy = pltpu.make_async_copy(
                vnew.at[:, t, pl.ds(PAD + part * per, per)],
                result.at[:, pl.ds(part * per, per), pl.ds(128 * t, 128)],
                sem.at[part, t],
            )
            copy.start()
            copies.append(copy)
    for copy in copies:
        copy.wait()


def resident(*shape):
    return pltpu.VMEM(shape, F32)


def in_vmem(x):
    return pltpu.with_memory_space_constraint(x, pltpu.VMEM)


def in_hbm(x):
    return pltpu.with_memory_space_constraint(x, pltpu.HBM)


IN_VMEM = pl.BlockSpec(memory_space=pltpu.VMEM)
IN_HBM = pl.BlockSpec(memory_space=pl.ANY)

FIELD = (NT, ROWS, 128)


def run(kernel, name, ins, outs, aliases=None, scratch=(), flops=0, moved=0, limit=4 * MIB):
    args = [in_hbm(a) if hbm else in_vmem(a) for a, hbm in ins]
    return pl.pallas_call(
        kernel,
        out_shape=outs,
        in_specs=[IN_HBM if hbm else IN_VMEM for _, hbm in ins],
        out_specs=[IN_HBM if isinstance(o, jax.ShapeDtypeStruct) else IN_VMEM for o in outs],
        input_output_aliases=aliases or {},
        scratch_shapes=list(scratch),
        compiler_params=pltpu.CompilerParams(vmem_limit_bytes=limit),
        cost_estimate=pl.CostEstimate(flops=flops, bytes_accessed=moved, transcendentals=0),
        name=name,
    )(*args)


def vm(*arrays):
    return [(a, False) for a in arrays]


def next_chip(b):
    n = lax.axis_size("width") * 2
    return lax.ppermute(b, WIDTH, [(i, (((i + 1) ^ 1) - 1) % n) for i in range(n)])


def across(a, b):
    hb = next_chip(b)
    return lax.ppermute(a, "thick", [(0, 1), (1, 0)]), hb


def along(a, b):
    n, m = lax.axis_size("cast"), lax.axis_size("width") * 2
    second = []
    for i in range(n):
        j = ((i + 1) ^ 1) - 1
        second += [(i * m + k, j * m + k if 0 <= j < n else i * m + (k ^ 1)) for k in range(m)]
    hb = lax.ppermute(b, ("cast", *WIDTH), second)
    return lax.ppermute(a, "cast", [(i, i ^ 1) for i in range(n)]), hb


def rows_of(n, planes=NXL):
    return [resident(n, NT, planes, 128)] * 2


def planes_of(n):
    return [resident(n, NT, NYL, 128)] * 2


def local(velocity, magnetic, labels, viscosity):
    vel = velocity.reshape(3, CELLS, NT * 128)
    mag = magnetic.reshape(3, CELLS, NT * 128)
    lab = labels.reshape(CELLS, NT * 128)
    visc = viscosity.reshape(CELLS, NT * 128)
    dma = pltpu.SemaphoreType.DMA
    w = [sweep_weight(k) for k in range(ITERS)]
    field, fields = resident(*FIELD), resident(3, *FIELD)
    work = dict(flops=10_000_000, moved=16 * MIB)

    v, b, hat, e, *edges = run(
        load_kernel, "load", [(vel, True), (mag, True), (lab, True)],
        [fields, resident(2, NT, CELLS, 128), field, fields, resident(2, NT, NXL, 128), resident(3, NT, NXL, 128)] + planes_of(2),
        scratch=[
            pltpu.VMEM((CELLS, NT * 128), jnp.int32),
            pltpu.VMEM((2, NYL, NT * 128), F32),
            pltpu.VMEM((2, NYL, NT * 128), F32),
            dma((CHUNKS, 4 * NT + 1)),
            dma((2, 2)),
        ],
    )
    h1 = (*across(*edges[:2]), *along(*edges[2:]))
    v, e, vnew, f, src, inv, phi, nu, near, *products = run(
        functools.partial(rest_kernel, w[0]), "faces",
        [(vel, True), (mag, True), (visc, True)] + vm(hat, b, v, e),
        [fields, fields, fields, fields, field, field, field, field, resident(4, NT, NXL, 128)]
        + rows_of(2) + planes_of(2),
        aliases={5: 0, 6: 1},
        scratch=[pltpu.VMEM((NT, CELLS, 128), F32), dma((CHUNKS, 2 * NT)), dma((NT,))], **work,
    )
    f, src, inv, phi, *rest = run(
        functools.partial(first_edge_kernel, w[0]), "edges1", vm(*h1, *edges, v, near, f, src, inv, phi),
        [fields] + [field] * 3 + [resident(NT, NXL, 128)] * 2 + [resident(NT, NYL, 128)] * 2
        + [resident(4, NT, NXL, 128), resident(1, NT, NXL, 128)] + [resident(NT, LINES + 8, 128)] * 2,
        aliases={10: 0, 11: 1, 12: 2, 13: 3},
    )
    coefs, edges = rest[:4], rest[4:]

    h2 = (*across(*edges[:2]), *along(*edges[2:]))
    lines = h2[2:]
    old = phi
    phi, vnew = run(
        functools.partial(sweep_predict_kernel, w[1], (0, 24)), "sweep1", vm(phi, f, src, inv, v, nu, vnew),
        [field, fields], aliases={6: 1}, **work,
    )
    phi, *edges = run(
        functools.partial(wide_edge_kernel, w[1], w[0]), "edges2",
        vm(old, f, phi, *coefs, *h1[2:], *lines, *h2[:2]),
        [field, resident(1, NT, NXL + 8, 128), resident(1, NT, NXL + 16, 128)], aliases={2: 0},
    )

    h3 = across(*edges)
    phi, flow = run(
        functools.partial(sweep_flow_kernel, w[2]), "sweep2", vm(phi, f, src, inv, v, nu),
        [field, resident(3, NT, NXL, 128)], **work,
    )
    flow = next_chip(flow)
    phi, *edges = run(
        functools.partial(narrow_edge_kernel, w[2], w[1]), "edges3", vm(f, nu, near, phi, *coefs, *lines, *h3),
        [field, resident(2, NT, NXL, 128), resident(1, NT, NXL, 128)] + planes_of(3), aliases={3: 0},
    )

    h4 = (*across(*edges[:2]), *along(*edges[2:]))
    old = phi
    phi, vnew = run(
        functools.partial(sweep_predict_kernel, w[3], (24, 64)), "sweep3", vm(phi, f, src, inv, v, nu, vnew),
        [field, fields], aliases={6: 1}, **work,
    )
    phi, *edges = run(
        functools.partial(wide_edge_kernel, w[3], None), "edges4",
        vm(old, f, phi, *coefs, *h1[2:], *lines, *h4, flow),
        [field, resident(1, NT, NXL + 8, 128), resident(1, NT, NXL + 16, 128)], aliases={2: 0},
    )

    h5 = across(*edges)
    potential, vnew = run(
        force_kernel, "force", vm(phi, hat, mag, v, nu, h1[1], h2[0], h4[0], flow, *lines, *h4[2:], vnew),
        [jax.ShapeDtypeStruct((CELLS, NT * 128), F32), fields],
        aliases={13: 1}, scratch=[dma((NT,))], **work,
    )
    result, _ = run(
        functools.partial(last_kernel, w[3]), "last", vm(*products, *lines, *h5, vnew),
        [jax.ShapeDtypeStruct((3, CELLS, NT * 128), F32), fields],
        aliases={8: 1}, scratch=[dma((PARTS, NT))],
    )
    return result.reshape(velocity.shape), potential.reshape(labels.shape)


def solution(mesh):
    fields = P(None, "cast", WIDTH, None)
    scalar = P("cast", WIDTH, None)
    return jax.shard_map(
        local,
        mesh=mesh,
        in_specs=(fields, fields, scalar, scalar),
        out_specs=(fields, scalar),
        check_vma=False,
    )
```

```python
import functools
import math

import jax
import jax.numpy as jnp
from jax import lax
from jax.experimental import pallas as pl
from jax.experimental.pallas import tpu as pltpu
from jax.sharding import PartitionSpec as P

ITERS = 4
time_step = 0.1
force_gain = 0.3

NXL = 64
NYL = 16
NT = 4
PAD = 16
CELLS = NXL * NYL
ROWS = CELLS + 2 * PAD
F32 = jnp.float32
WIDTH = ("width", "thick")
MIB = 1024 * 1024
SHAPE = (NT, 8, 128)
OUTSIDE = 1e30


def sweep_weight(k):
    return 2.0 / (2.15 + 1.75 * math.cos(math.pi * (2 * k + 1) / (2 * ITERS)))


def z_up(a, fill=0.0):
    r = pltpu.roll(a, 127, 2)
    after = jnp.concatenate([r[1:], jnp.full_like(r[:1], fill)], axis=0)
    return jnp.where(lax.broadcasted_iota(jnp.int32, a.shape, 2) == 127, after, r)


def z_down(a, fill=0.0):
    r = pltpu.roll(a, 1, 2)
    before = jnp.concatenate([jnp.full_like(r[:1], fill), r[:-1]], axis=0)
    return jnp.where(lax.broadcasted_iota(jnp.int32, a.shape, 2) == 0, before, r)


def recip(d):
    return pltpu.reciprocal(d, approx=True)


def sublanes():
    return lax.broadcasted_iota(jnp.int32, SHAPE, 1)


def row_of(x):
    return pl.multiple_of(PAD + x * NYL, NYL)


def fill_pads(ref, value=0.0):
    lead = (slice(None),) * (len(ref.shape) - 2)
    block = jnp.full(ref.shape[:-2] + (PAD, 128), value, F32)
    ref[lead + (pl.ds(0, PAD),)] = block
    ref[lead + (pl.ds(PAD + CELLS, PAD),)] = block


class Sides:
    def __init__(self, x0=0, planes=NXL):
        thick = lax.axis_index("thick")
        place = lax.axis_index("width") * 2 + thick
        last = lax.axis_size("width") * 2 - 1
        cast = lax.axis_index("cast")
        odd = lax.rem(cast, 2)
        self.near = (NYL - 1) * (1 - thick)
        self.far = (NYL - 1) * thick
        self.high = (1 - odd, odd)
        self.edge = tuple(h * (NXL - 1) for h in self.high)

        def plane(x):
            return pl.ds(pl.multiple_of(x * NYL, NYL), NYL)

        self.beyond = tuple(plane(h * (NXL + 1)) for h in self.high)
        self.face_in = tuple(plane(h * NXL) for h in self.high)
        self.behind = tuple(plane(1 + 1 + h * (NXL - 3)) for h in self.high)
        self.face_behind = tuple(plane(1 + h * (NXL - 2)) for h in self.high)

        def rows(pad):
            start = pad + x0 * NYL
            return (
                pl.ds(start + self.near, planes, stride=NYL),
                pl.ds(start + self.far, planes, stride=NYL),
                *(plane(pad // NYL + x) for x in self.edge),
            )

        self.rows = rows(PAD)
        self.inner = rows(0)
        self.dims = (1, 1, 0, 0)

        def number(condition, yes, no):
            return jnp.where(condition, yes, no).astype(F32)

        up = number(thick == 0, 1.0, -1.0)
        ahead = number(odd == 0, 1.0, -1.0)
        self.signs = (up, -up, ahead, -ahead)
        self.masks = (
            1.0,
            number(((thick == 0) & (place > 0)) | ((thick == 1) & (place < last)), 1.0, 0.0),
            1.0,
            number((cast > 0) & (cast < lax.axis_size("cast") - 1), 1.0, 0.0),
        )


CHUNKS = 4
PER = CELLS // CHUNKS


def columns(source, chunk, target, sem, pad):
    rows = pl.ds(chunk * PER, PER)
    at = pl.ds(pad + chunk * PER, PER)
    return [pltpu.make_async_copy(source.at[rows, pl.ds(128 * t, 128)], target.at[t, at], sem(t)) for t in range(NT)]


def load_kernel(vel, mag, lab, v, b, hat, e, oa, ob, ol, oh, lraw, ve, be, sem, edge_sem):
    s = Sides()

    def copies(ch):
        some = pl.ds(ch * PER, PER)
        out = [pltpu.make_async_copy(lab.at[some], lraw.at[some], sem.at[ch, 4 * NT])]
        for i, comp in enumerate((0, 2)):
            out += columns(vel.at[comp], ch, v.at[comp], lambda t: sem.at[ch, i * NT + t], PAD)
            out += columns(mag.at[comp], ch, b.at[i], lambda t: sem.at[ch, (2 + i) * NT + t], 0)
        return out

    outer = []
    for i in range(2):
        rows = s.inner[2 + i]
        outer += [
            pltpu.make_async_copy(vel.at[1, rows], ve.at[i], edge_sem.at[i, 0]),
            pltpu.make_async_copy(mag.at[1, rows], be.at[i], edge_sem.at[i, 1]),
        ]
    chunks = [copies(ch) for ch in range(CHUNKS)]
    for copy in chunks[0] + outer + [copy for chunk in chunks[1:] for copy in chunk]:
        copy.start()
    fill_pads(v)
    fill_pads(e)
    fill_pads(hat, OUTSIDE)
    for ch in range(CHUNKS):
        for copy in chunks[ch]:
            copy.wait()

        @pl.loop(0, PER // 8, unroll=8)
        def _(i):
            raw = pl.ds(pl.multiple_of(ch * PER + i * 8, 8), 8)
            at = pl.ds(pl.multiple_of(PAD + ch * PER + i * 8, 8), 8)
            for t in range(NT):
                label = lraw[raw, pl.ds(128 * t, 128)]
                hat[t, at, :] = jnp.where(label == 0, 0.5, jnp.where(label == 1, 0.5 / 0.7, 0.125)).astype(F32)
                e[1, t, at, :] = v[2, t, at, :] * b[0, t, raw, :] - v[0, t, at, :] * b[1, t, raw, :]

    for copy in outer:
        copy.wait()
    for i, out in enumerate((ol, oh)):
        rows, inner = s.rows[2 + i], s.inner[2 + i]
        out[0] = hat[:, rows, :]
        for t in range(NT):
            col = pl.ds(128 * t, 128)
            out[1, t] = ve[i, :, col] * b[1, t, inner, :] - v[2, t, rows, :] * be[i, :, col]
    for out, rows in zip((oa, ob), s.rows):
        out[0] = hat[:, rows, :]
        out[1] = e[1, :, rows, :]
    ob[2] = v[0, :, s.rows[1], :]


def rest_kernel(w0, vel, mag, visc, hat, b, v_in, e_in, v, e, vnew, f, src, inv, phi, nu, near,
                ka, kb, kl, kh, mid, sem, visc_sem):
    del v_in, e_in
    chunks = [
        columns(vel.at[1], ch, v.at[1], lambda t: sem.at[ch, t], PAD)
        + columns(mag.at[1], ch, mid, lambda t: sem.at[ch, NT + t], 0)
        for ch in range(CHUNKS)
    ]
    last = [
        pltpu.make_async_copy(visc.at[:, pl.ds(128 * t, 128)], nu.at[t, pl.ds(PAD, CELLS)], visc_sem.at[t])
        for t in range(NT)
    ]
    for copy in [copy for chunk in chunks for copy in chunk] + last:
        copy.start()
    f[1, :, 0:PAD, :] = jnp.zeros((NT, PAD, 128), F32)
    fill_pads(phi)
    fill_pads(nu)
    for ch in range(CHUNKS):
        for copy in chunks[ch]:
            copy.wait()

        @pl.loop(0, PER // 8, unroll=8)
        def _(i):
            raw = pl.ds(pl.multiple_of(ch * PER + i * 8, 8), 8)
            at = pl.ds(pl.multiple_of(PAD + ch * PER + i * 8, 8), 8)
            v0, v1, v2 = (v[c, :, at, :] for c in range(3))
            b0, b1, b2 = b[0, :, raw, :], mid[:, raw, :], b[1, :, raw, :]
            e1 = e[1, :, at, :]
            e0, e2 = v1 * b2 - v2 * b1, v0 * b1 - v1 * b0
            e[0, :, at, :] = e0
            e[2, :, at, :] = e2
            gain = (0.5 * force_gain) * recip(hat[:, at, :])
            vnew[0, :, at, :] = gain * (e1 * b2 - e2 * b1)
            vnew[1, :, at, :] = gain * (e2 * b0 - e0 * b2)
            vnew[2, :, at, :] = gain * (e0 * b1 - e1 * b0)

    faces(w0, hat, e, f, src, inv, phi)
    s = Sides()
    fields = [b.at[0], mid, b.at[1]]
    for i, k in enumerate((ka, kb, kl, kh)):
        rows, at, d = s.rows[i], s.inner[i], s.dims[i]
        n1, n2 = (d + 1) % 3, (d + 2) % 3
        g = (0.25 * force_gain * s.signs[i]) * (s.masks[i] * recip(hat[:, rows, :]))
        k[0] = g * fields[n2][:, at, :]
        k[1] = -g * fields[n1][:, at, :]
    for copy in last:
        copy.wait()
    for c in range(3):
        near[c] = v[c, :, s.rows[0], :]
    near[3] = nu[:, s.rows[0], :]


def faces(w0, hat, e, f, src, inv, phi):
    zero = jnp.zeros(SHAPE, F32)
    sub = sublanes()

    def body(x, carry):
        fxm, qxm, hc, exc = carry
        r = row_of(x)
        fxo, qxo, hn, exn = [], [], [], []
        for y in range(2):
            base = r + 8 * y
            at, up, down = pl.ds(base, 8), pl.ds(base + 1, 8), pl.ds(base - 1, 8)
            ahead = pl.ds(base + NYL, 8)
            c = hc[y]
            hn.append(hat[:, ahead, :])
            exn.append(e[0, :, ahead, :])
            fx = recip(c + hn[y])
            qx = fx * (exc[y] + exn[y])
            fxo.append(fx)
            qxo.append(qx)
            ey = e[1, :, at, :]
            fy = recip(c + hat[:, up, :])
            fym = recip(c + hat[:, down, :])
            if y == 1:
                fy = jnp.where(sub == 7, 0.0, fy)
            else:
                fym = jnp.where(sub == 0, 0.0, fym)
            ez = e[2, :, at, :]
            fz = recip(c + z_up(c, OUTSIDE))
            fzm = recip(c + z_down(c, OUTSIDE))
            qy = fy * (ey + e[1, :, up, :]) - fym * (ey + e[1, :, down, :])
            qz = fz * (ez + z_up(ez)) - fzm * (ez + z_down(ez))
            source = 0.5 * (((qx - qxm[y]) + qy) + qz)
            inverse = recip((((fx + fxm[y]) + (fy + fym)) + (fz + fzm)) + 0.025 * recip(c))
            f[0, :, at, :] = fx
            f[1, :, at, :] = fy
            f[2, :, at, :] = fz
            src[:, at, :] = source
            inv[:, at, :] = inverse
            phi[:, at, :] = (-w0) * (source * inverse)
        return tuple(fxo), tuple(qxo), tuple(hn), tuple(exn)

    first = [pl.ds(PAD + 8 * y, 8) for y in range(2)]
    start = (
        (zero, zero),
        (zero, zero),
        tuple(hat[:, at, :] for at in first),
        tuple(e[0, :, at, :] for at in first),
    )
    lax.fori_loop(0, NXL, body, start, unroll=8)


SOURCE, INVERSE, BEHIND, *FLOW = (pl.ds(i * NYL, NYL) for i in range(6))
LINES = 6 * NYL


def flux_behind(phi, f, s, side):
    return f[0, :, s.face_behind[side], :] * phi[:, s.behind[side], :]


def first_edge_kernel(w0, ha, hb, hl, hh, sa, sb, sl, sh, v, near, f_in, src_in, inv_in, phi_in,
                      f, src, inv, phi, ca, cb, cl, ch, oa, ob, ol, oh):
    del f_in, src_in, inv_in, phi_in
    s = Sides()
    halos, sent, coefs = (ha, hb, hl, hh), (sa, sb, sl, sh), (ca, cb, cl, ch)

    def add(i):
        rows = s.rows[i]
        g = s.masks[i] * recip(sent[i][0] + halos[i][0])
        source = src[:, rows, :] + (0.5 * s.signs[i]) * (g * (sent[i][1] + halos[i][1]))
        return g, source, recip(recip(inv[:, rows, :]) + g)

    got = [add(i) for i in (2, 3)]
    for i, (g, source, inverse) in zip((2, 3), got):
        rows = s.rows[i]
        f[0, :, s.face_in[i - 2], :] = g
        coefs[i][...] = g
        src[:, rows, :] = source
        inv[:, rows, :] = inverse
        phi[:, rows, :] = (-w0) * (source * inverse)
    got = [add(i) for i in (0, 1)]
    for i, (g, source, inverse) in zip((0, 1), got):
        rows = s.rows[i]
        value = (-w0) * (source * inverse)
        coefs[i][...] = g * inverse
        src[:, rows, :] = source
        inv[:, rows, :] = inverse
        phi[:, rows, :] = value
        (oa, ob)[i][0] = value
    for c in range(3):
        oa[1 + c] = near[c]
    for i, (out, rows, x) in enumerate(zip((ol, oh), s.rows[2:], s.edge)):
        inverse = inv[:, rows, :]
        coefs[2 + i][...] = coefs[2 + i][...] * inverse
        out[:, SOURCE, :] = src[:, rows, :]
        out[:, INVERSE, :] = inverse
        out[:, BEHIND, :] = flux_behind(phi, f, s, i)
        for c in range(3):
            out[:, FLOW[c], :] = v[c, :, rows, :]
        out[:, pl.ds(LINES, 8), :] = jnp.zeros(SHAPE, F32)
        for j, coef in enumerate((ca, cb)):
            out[:, pl.ds(LINES + j, 1), :] = coef[:, pl.ds(x, 1), :]


def add_sides(w, phi, coefs, halos, rows):
    got = [phi[:, r, :] + w * (c[...] * h) for c, h, r in zip(coefs, halos, rows)]
    for r, value in zip(rows, got):
        phi[:, r, :] = value
    return got


def wide_edge_kernel(w, w0, old, f, phi_in, ca, cb, cl, ch, rl, rh, kl, kh, ha, hb, *rest):
    del phi_in
    s = Sides()
    phi, *outs = rest[-3:]
    ks = (kl, kh)
    if w0 is None:
        beyond = [(h[0], h[1]) for h in rest[:2]]
    else:
        beyond = [((-w0) * (k[:, SOURCE, :] * k[:, INVERSE, :]), k[:, BEHIND, :]) for k in ks]
    add_sides(w, phi, (cl, ch), (beyond[0][0], beyond[1][0]), s.rows[2:])
    edges = add_sides(w, phi, (ca, cb), (ha[0], hb[0]), s.rows[:2])
    row = lax.broadcasted_iota(jnp.int32, (NT, NYL, 128), 1)
    for side, (r, k, (c, flux)) in enumerate(zip((rl, rh), ks, beyond)):
        hat = r[0]
        fy = jnp.where(row == NYL - 1, 0.0, recip(hat + pltpu.roll(hat, NYL - 1, 1)))
        fz = recip(hat + z_up(hat, OUTSIDE))
        t = f[0, :, s.face_in[side], :] * old[:, s.rows[2 + side], :] + flux
        t = t + fy * pltpu.roll(c, NYL - 1, 1) + pltpu.roll(fy * c, 1, 1)
        t = t + fz * z_up(c) + z_down(fz * c)
        phi[:, s.beyond[side], :] = s.masks[2 + side] * (c + w * ((t - k[:, SOURCE, :]) * k[:, INVERSE, :] - c))
    for out, values, at in zip(outs, edges, (s.near, s.far)):
        out[0, :, pl.ds(0, NXL), :] = values
        more = out.shape[2] - NXL
        out[0, :, pl.ds(NXL, more), :] = jnp.zeros((NT, more, 128), F32)
        for side, (c, _) in enumerate(beyond):
            line = jnp.sum(jnp.where(row == at, c, 0.0), axis=1, keepdims=True)
            out[0, :, pl.ds(NXL + side, 1), :] = line


def narrow_edge_kernel(w, w_before, f, nu, near, phi_in, ca, cb, cl, ch, kl, kh, ha, hb, phi, oa, ob, ol, oh):
    del phi_in
    s = Sides()
    for j, (h, at) in enumerate(((ha, s.near), (hb, s.far))):
        for side, (k, c, plane) in enumerate(zip((kl, kh), (cl, ch), s.edge)):
            missing = w_before * (k[:, pl.ds(LINES + j, 1), :] * h[0, :, pl.ds(NXL + side, 1), :])
            row = pl.ds(PAD + plane * NYL + at, 1)
            phi[:, row, :] = phi[:, row, :] + w * (c[:, pl.ds(at, 1), :] * missing)
    inner = pl.ds(0, NXL)
    oa[0], ob[0] = add_sides(w, phi, (ca, cb), (ha[0, :, inner, :], hb[0, :, inner, :]), s.rows[:2])
    oa[1] = near[3]
    for i, (out, rows) in enumerate(zip((ol, oh), s.rows[2:])):
        out[0] = phi[:, rows, :]
        out[1] = flux_behind(phi, f, s, i)
        out[2] = nu[:, rows, :]


def predictor(v, nu, vnew, x0, x1):
    sub = sublanes()
    half = 0.5 * time_step

    @pl.loop(x0, x1, unroll=8)
    def _(x):
        r = row_of(x)
        for y in range(2):
            base = r + 8 * y
            at = pl.ds(base, 8)
            ups = (pl.ds(base + NYL, 8), pl.ds(base + 1, 8))
            downs = (pl.ds(base - NYL, 8), pl.ds(base - 1, 8))
            n = nu[:, at, :]
            vc = [v[c, :, at, :] for c in range(3)]
            coefs = []
            total = None
            for d in range(3):
                above = nu[:, ups[d], :] if d < 2 else z_up(n)
                below = nu[:, downs[d], :] if d < 2 else z_down(n)
                up = (n + above) - vc[d]
                down = (n + below) + vc[d]
                if d == 1 and y == 1:
                    up = jnp.where(sub == 7, 0.0, up)
                if d == 1 and y == 0:
                    down = jnp.where(sub == 0, 0.0, down)
                coefs.append((up, down))
                both = up + down
                total = both if total is None else total + both
            keep = 1.0 - half * total
            for c in range(3):
                acc = None
                for d in range(3):
                    above = v[c, :, ups[d], :] if d < 2 else z_up(vc[c])
                    below = v[c, :, downs[d], :] if d < 2 else z_down(vc[c])
                    term = coefs[d][0] * above + coefs[d][1] * below
                    acc = term if acc is None else acc + term
                vnew[c, :, at, :] = vnew[c, :, at, :] + (half * acc + keep * vc[c])


def sweep_kernel(w, phi, f, src, inv, out, x0=0, x1=NXL):
    if x0 == 0:
        fill_pads(out)

    def body(x, carry):
        pxm, pc = carry
        r = row_of(x)
        px, pn = [], []
        for y in range(2):
            base = r + 8 * y
            at, up, down = pl.ds(base, 8), pl.ds(base + 1, 8), pl.ds(base - 1, 8)
            pn.append(phi[:, pl.ds(base + NYL, 8), :])
            fx = f[0, :, at, :]
            c = pc[y]
            px.append(fx * c)
            t = fx * pn[y] + pxm[y]
            t = t + f[1, :, at, :] * phi[:, up, :]
            t = t + f[1, :, down, :] * phi[:, down, :]
            fz = f[2, :, at, :]
            t = t + fz * z_up(c)
            t = t + z_down(fz * c)
            out[:, at, :] = c + w * ((t - src[:, at, :]) * inv[:, at, :] - c)
        return tuple(px), tuple(pn)

    before = tuple(f[0, :, pl.ds(x0 * NYL + 8 * y, 8), :] * phi[:, pl.ds(x0 * NYL + 8 * y, 8), :] for y in range(2))
    start = (before, tuple(phi[:, pl.ds(PAD + x0 * NYL + 8 * y, 8), :] for y in range(2)))
    lax.fori_loop(x0, x1, body, start, unroll=min(16, x1 - x0))


CUT = 16


def sweep_flow_kernel(w, phi, f, src, inv, v, nu, out, flow):
    rows = Sides().rows[1]
    flow[0] = v[1, :, rows, :]
    flow[1] = v[2, :, rows, :]
    flow[2] = nu[:, rows, :]
    sweep_kernel(w, phi, f, src, inv, out, 0, CUT)


def sweep_end_kernel(w, phi, f, src, inv, out_in, out):
    del out_in
    sweep_kernel(w, phi, f, src, inv, out, CUT, NXL)


def sweep_predict_kernel(w, planes, phi, f, src, inv, v, nu, vnew_in, out, vnew):
    del vnew_in
    sweep_kernel(w, phi, f, src, inv, out)
    predictor(v, nu, vnew, *planes)


def force_kernel(phi, hat, b, v, nu, *rest):
    far0, near, near_nu, far, *along = rest[:8]
    sent = (
        (near[1], near[2], near[3], near_nu[1]),
        (far0[2], far[0], far[1], far[2]),
        *((*(along[i][:, rows, :] for rows in FLOW), along[2 + i][2]) for i in range(2)),
    )
    potential, result, vnew, sem, out_sem = rest[9:]
    copies = [
        pltpu.make_async_copy(phi.at[t, pl.ds(PAD, CELLS)], potential.at[:, pl.ds(128 * t, 128)], sem.at[t])
        for t in range(NT)
    ]
    for copy in copies:
        copy.start()

    s = Sides()
    half = 0.5 * time_step
    for pair in ((0, 1), (2, 3)):
        got = []
        for i in pair:
            rows, d, sign, mask = s.rows[i], s.dims[i], s.signs[i], s.masks[i]
            other = sent[i][:3]
            hn = mask * sent[i][3]
            vc = [v[c, :, rows, :] for c in range(3)]
            coef = half * ((nu[:, rows, :] + hn) - sign * vc[d])
            gone = half * hn if d == 0 else coef
            got.append([vnew[c, :, rows, :] + (coef * (mask * other[c]) - gone * vc[c]) for c in range(3)])
        for i, values in zip(pair, got):
            for c in range(3):
                vnew[c, :, s.rows[i], :] = values[c]

    sub = sublanes()
    for ch in range(CHUNKS):

        @pl.loop(ch * (NXL // CHUNKS), (ch + 1) * (NXL // CHUNKS), unroll=8)
        def _(x):
            r = row_of(x)
            for y in range(2):
                base = r + 8 * y
                at = pl.ds(base, 8)
                raw = pl.ds(pl.multiple_of(x * NYL + 8 * y, 8), 8)
                p = phi[:, at, :]
                yu = phi[:, pl.ds(base + 1, 8), :]
                yd = phi[:, pl.ds(base - 1, 8), :]
                if y == 1:
                    yu = jnp.where(sub == 7, 0.0, yu)
                else:
                    yd = jnp.where(sub == 0, 0.0, yd)
                diffs = (
                    phi[:, pl.ds(base + NYL, 8), :] - phi[:, pl.ds(base - NYL, 8), :],
                    yu - yd,
                    z_up(p) - z_down(p),
                )
                g = (-0.25 * force_gain) * recip(hat[:, at, :])
                c0, c1, c2 = (g * diff for diff in diffs)
                for t in range(NT):
                    b0, b1, b2 = (b[c, raw, pl.ds(128 * t, 128)] for c in range(3))
                    vnew[0, t, at, :] = vnew[0, t, at, :] + (c1[t] * b2 - c2[t] * b1)
                    vnew[1, t, at, :] = vnew[1, t, at, :] + (c2[t] * b0 - c0[t] * b2)
                    vnew[2, t, at, :] = vnew[2, t, at, :] + (c0[t] * b1 - c1[t] * b0)

        if ch == CHUNKS - 1:
            break
        low = ch * PER + (NYL if ch == 0 else 0)
        some = (ch + 1) * PER - low
        for t in range(NT):
            copy = pltpu.make_async_copy(
                vnew.at[1, t, pl.ds(PAD + low, some)],
                result.at[1, pl.ds(low, some), pl.ds(128 * t, 128)],
                out_sem.at[ch, t],
            )
            copy.start()
            copies.append(copy)
    for copy in copies:
        copy.wait()


PARTS = 4


def last_kernel(w, ka, kb, kl, kh, cl, ch, ha, hb, vnew_in, result_in, result, vnew, sem, edge_sem):
    del vnew_in, result_in
    planes = NXL // PARTS
    copies = []
    s = Sides()
    for side, (k, lines, plane) in enumerate(zip((kl, kh), (cl, ch), s.edge)):
        for j, (h, at) in enumerate(((ha, s.near), (hb, s.far))):
            missing = w * (lines[:, pl.ds(LINES + j, 1), :] * h[0, :, pl.ds(NXL + side, 1), :])
            row = pl.ds(PAD + plane * NYL + at, 1)
            for i, c in enumerate((1, 2)):
                vnew[c, :, row, :] = vnew[c, :, row, :] + k[i, :, pl.ds(at, 1), :] * missing
    for i, (low, some) in enumerate(((0, NYL), ((CHUNKS - 1) * PER, PER))):
        for t in range(NT):
            copy = pltpu.make_async_copy(
                vnew.at[1, t, pl.ds(PAD + low, some)],
                result.at[1, pl.ds(low, some), pl.ds(128 * t, 128)],
                edge_sem.at[i, t],
            )
            copy.start()
            copies.append(copy)
    for part in range(PARTS):
        s = Sides(part * planes, planes)
        some = pl.ds(part * planes, planes)
        got = []
        for k, h, rows in ((ka, ha, s.rows[0]), (kb, hb, s.rows[1])):
            halo = h[0, :, some, :]
            got += [(c, rows, vnew[c, :, rows, :] + k[j, :, some, :] * halo) for j, c in enumerate((2, 0))]
        for c, rows, value in got:
            vnew[c, :, rows, :] = value
        per = planes * NYL
        for c in (0, 2):
            for t in range(NT):
                copy = pltpu.make_async_copy(
                    vnew.at[c, t, pl.ds(PAD + part * per, per)],
                    result.at[c, pl.ds(part * per, per), pl.ds(128 * t, 128)],
                    sem.at[part, c // 2, t],
                )
                copy.start()
                copies.append(copy)
    for copy in copies:
        copy.wait()


def resident(*shape):
    return pltpu.VMEM(shape, F32)


def in_vmem(x):
    return pltpu.with_memory_space_constraint(x, pltpu.VMEM)


def in_hbm(x):
    return pltpu.with_memory_space_constraint(x, pltpu.HBM)


IN_VMEM = pl.BlockSpec(memory_space=pltpu.VMEM)
IN_HBM = pl.BlockSpec(memory_space=pl.ANY)

FIELD = (NT, ROWS, 128)


def run(kernel, name, ins, outs, aliases=None, scratch=(), flops=0, moved=0, limit=4 * MIB):
    args = [in_hbm(a) if hbm else in_vmem(a) for a, hbm in ins]
    return pl.pallas_call(
        kernel,
        out_shape=outs,
        in_specs=[IN_HBM if hbm else IN_VMEM for _, hbm in ins],
        out_specs=[IN_HBM if isinstance(o, jax.ShapeDtypeStruct) else IN_VMEM for o in outs],
        input_output_aliases=aliases or {},
        scratch_shapes=list(scratch),
        compiler_params=pltpu.CompilerParams(vmem_limit_bytes=limit),
        cost_estimate=pl.CostEstimate(flops=flops, bytes_accessed=moved, transcendentals=0),
        name=name,
    )(*args)


def vm(*arrays):
    return [(a, False) for a in arrays]


def next_chip(b):
    n = lax.axis_size("width") * 2
    return lax.ppermute(b, WIDTH, [(i, (((i + 1) ^ 1) - 1) % n) for i in range(n)])


def across(a, b):
    hb = next_chip(b)
    return lax.ppermute(a, "thick", [(0, 1), (1, 0)]), hb


def along(a, b):
    n, m = lax.axis_size("cast"), lax.axis_size("width") * 2
    second = []
    for i in range(n):
        j = ((i + 1) ^ 1) - 1
        second += [(i * m + k, j * m + k if 0 <= j < n else i * m + (k ^ 1)) for k in range(m)]
    hb = lax.ppermute(b, ("cast", *WIDTH), second)
    return lax.ppermute(a, "cast", [(i, i ^ 1) for i in range(n)]), hb


def rows_of(n, planes=NXL):
    return [resident(n, NT, planes, 128)] * 2


def planes_of(n):
    return [resident(n, NT, NYL, 128)] * 2


def local(velocity, magnetic, labels, viscosity):
    vel = velocity.reshape(3, CELLS, NT * 128)
    mag = magnetic.reshape(3, CELLS, NT * 128)
    lab = labels.reshape(CELLS, NT * 128)
    visc = viscosity.reshape(CELLS, NT * 128)
    dma = pltpu.SemaphoreType.DMA
    w = [sweep_weight(k) for k in range(ITERS)]
    field, fields = resident(*FIELD), resident(3, *FIELD)
    work = dict(flops=10_000_000, moved=16 * MIB)

    v, b, hat, e, *edges = run(
        load_kernel, "load", [(vel, True), (mag, True), (lab, True)],
        [fields, resident(2, NT, CELLS, 128), field, fields, resident(2, NT, NXL, 128), resident(3, NT, NXL, 128)] + planes_of(2),
        scratch=[
            pltpu.VMEM((CELLS, NT * 128), jnp.int32),
            pltpu.VMEM((2, NYL, NT * 128), F32),
            pltpu.VMEM((2, NYL, NT * 128), F32),
            dma((CHUNKS, 4 * NT + 1)),
            dma((2, 2)),
        ],
    )
    h1 = (*across(*edges[:2]), *along(*edges[2:]))
    v, e, vnew, f, src, inv, phi, nu, near, *products = run(
        functools.partial(rest_kernel, w[0]), "faces",
        [(vel, True), (mag, True), (visc, True)] + vm(hat, b, v, e),
        [fields, fields, fields, fields, field, field, field, field, resident(4, NT, NXL, 128)]
        + rows_of(2) + planes_of(2),
        aliases={5: 0, 6: 1},
        scratch=[pltpu.VMEM((NT, CELLS, 128), F32), dma((CHUNKS, 2 * NT)), dma((NT,))], **work,
    )
    f, src, inv, phi, *rest = run(
        functools.partial(first_edge_kernel, w[0]), "edges1", vm(*h1, *edges, v, near, f, src, inv, phi),
        [fields] + [field] * 3 + [resident(NT, NXL, 128)] * 2 + [resident(NT, NYL, 128)] * 2
        + [resident(4, NT, NXL, 128), resident(1, NT, NXL, 128)] + [resident(NT, LINES + 8, 128)] * 2,
        aliases={10: 0, 11: 1, 12: 2, 13: 3},
    )
    coefs, edges = rest[:4], rest[4:]

    h2 = (*across(*edges[:2]), *along(*edges[2:]))
    lines = h2[2:]
    old = phi
    phi, vnew = run(
        functools.partial(sweep_predict_kernel, w[1], (0, 24)), "sweep1", vm(phi, f, src, inv, v, nu, vnew),
        [field, fields], aliases={6: 1}, **work,
    )
    phi, *edges = run(
        functools.partial(wide_edge_kernel, w[1], w[0]), "edges2",
        vm(old, f, phi, *coefs, *h1[2:], *lines, *h2[:2]),
        [field, resident(1, NT, NXL + 8, 128), resident(1, NT, NXL + 16, 128)], aliases={2: 0},
    )

    h3 = across(*edges)
    half, flow = run(
        functools.partial(sweep_flow_kernel, w[2]), "sweep2", vm(phi, f, src, inv, v, nu),
        [field, resident(3, NT, NXL, 128)], **work,
    )
    (phi,) = run(
        functools.partial(sweep_end_kernel, w[2]), "rest2", vm(phi, f, src, inv, half), [field], aliases={4: 0}, **work
    )
    flow = next_chip(flow)
    phi, *edges = run(
        functools.partial(narrow_edge_kernel, w[2], w[1]), "edges3", vm(f, nu, near, phi, *coefs, *lines, *h3),
        [field, resident(2, NT, NXL, 128), resident(1, NT, NXL, 128)] + planes_of(3), aliases={3: 0},
    )

    h4 = (*across(*edges[:2]), *along(*edges[2:]))
    old = phi
    phi, vnew = run(
        functools.partial(sweep_predict_kernel, w[3], (24, 64)), "sweep3", vm(phi, f, src, inv, v, nu, vnew),
        [field, fields], aliases={6: 1}, **work,
    )
    phi, *edges = run(
        functools.partial(wide_edge_kernel, w[3], None), "edges4",
        vm(old, f, phi, *coefs, *h1[2:], *lines, *h4, flow),
        [field, resident(1, NT, NXL + 8, 128), resident(1, NT, NXL + 16, 128)], aliases={2: 0},
    )

    h5 = across(*edges)
    potential, result, vnew = run(
        force_kernel, "force", vm(phi, hat, mag, v, nu, h1[1], h2[0], h4[0], flow, *lines, *h4[2:], vnew),
        [jax.ShapeDtypeStruct((CELLS, NT * 128), F32), jax.ShapeDtypeStruct((3, CELLS, NT * 128), F32), fields],
        aliases={13: 2}, scratch=[dma((NT,)), dma((CHUNKS - 1, NT))], **work,
    )
    result, _ = run(
        functools.partial(last_kernel, w[3]), "last", vm(*products, *lines, *h5, vnew) + [(result, True)],
        [jax.ShapeDtypeStruct((3, CELLS, NT * 128), F32), fields],
        aliases={8: 1, 9: 0}, scratch=[dma((PARTS, 2, NT)), dma((2, NT))],
    )
    return result.reshape(velocity.shape), potential.reshape(labels.shape)


def solution(mesh):
    fields = P(None, "cast", WIDTH, None)
    scalar = P("cast", WIDTH, None)
    return jax.shard_map(
        local,
        mesh=mesh,
        in_specs=(fields, fields, scalar, scalar),
        out_specs=(fields, scalar),
        check_vma=False,
    )
```

```python
import functools
import math

import jax
import jax.numpy as jnp
from jax import lax
from jax.experimental import pallas as pl
from jax.experimental.pallas import tpu as pltpu
from jax.sharding import PartitionSpec as P

ITERS = 4
time_step = 0.1
force_gain = 0.3

NXL = 64
NYL = 16
NT = 4
PAD = 16
CELLS = NXL * NYL
ROWS = CELLS + 2 * PAD
F32 = jnp.float32
WIDTH = ("width", "thick")
MIB = 1024 * 1024
SHAPE = (NT, 8, 128)
OUTSIDE = 1e30


def sweep_weight(k):
    return 2.0 / (2.15 + 1.75 * math.cos(math.pi * (2 * k + 1) / (2 * ITERS)))


def z_up(a, fill=0.0):
    r = pltpu.roll(a, 127, 2)
    after = jnp.concatenate([r[1:], jnp.full_like(r[:1], fill)], axis=0)
    return jnp.where(lax.broadcasted_iota(jnp.int32, a.shape, 2) == 127, after, r)


def z_down(a, fill=0.0):
    r = pltpu.roll(a, 1, 2)
    before = jnp.concatenate([jnp.full_like(r[:1], fill), r[:-1]], axis=0)
    return jnp.where(lax.broadcasted_iota(jnp.int32, a.shape, 2) == 0, before, r)


def recip(d):
    return pltpu.reciprocal(d, approx=True)


def sublanes():
    return lax.broadcasted_iota(jnp.int32, SHAPE, 1)


def row_of(x):
    return pl.multiple_of(PAD + x * NYL, NYL)


def fill_pads(ref, value=0.0):
    lead = (slice(None),) * (len(ref.shape) - 2)
    block = jnp.full(ref.shape[:-2] + (PAD, 128), value, F32)
    ref[lead + (pl.ds(0, PAD),)] = block
    ref[lead + (pl.ds(PAD + CELLS, PAD),)] = block


class Sides:
    def __init__(self, x0=0, planes=NXL):
        thick = lax.axis_index("thick")
        place = lax.axis_index("width") * 2 + thick
        last = lax.axis_size("width") * 2 - 1
        cast = lax.axis_index("cast")
        odd = lax.rem(cast, 2)
        self.near = (NYL - 1) * (1 - thick)
        self.far = (NYL - 1) * thick
        self.high = (1 - odd, odd)
        self.edge = tuple(h * (NXL - 1) for h in self.high)

        def plane(x):
            return pl.ds(pl.multiple_of(x * NYL, NYL), NYL)

        self.beyond = tuple(plane(h * (NXL + 1)) for h in self.high)
        self.face_in = tuple(plane(h * NXL) for h in self.high)
        self.behind = tuple(plane(1 + 1 + h * (NXL - 3)) for h in self.high)
        self.face_behind = tuple(plane(1 + h * (NXL - 2)) for h in self.high)

        def rows(pad):
            start = pad + x0 * NYL
            return (
                pl.ds(start + self.near, planes, stride=NYL),
                pl.ds(start + self.far, planes, stride=NYL),
                *(plane(pad // NYL + x) for x in self.edge),
            )

        self.rows = rows(PAD)
        self.inner = rows(0)
        self.dims = (1, 1, 0, 0)

        def number(condition, yes, no):
            return jnp.where(condition, yes, no).astype(F32)

        up = number(thick == 0, 1.0, -1.0)
        ahead = number(odd == 0, 1.0, -1.0)
        self.signs = (up, -up, ahead, -ahead)
        self.masks = (
            1.0,
            number(((thick == 0) & (place > 0)) | ((thick == 1) & (place < last)), 1.0, 0.0),
            1.0,
            number((cast > 0) & (cast < lax.axis_size("cast") - 1), 1.0, 0.0),
        )


CHUNKS = 4
PER = CELLS // CHUNKS


def columns(source, chunk, target, sem, pad):
    rows = pl.ds(chunk * PER, PER)
    at = pl.ds(pad + chunk * PER, PER)
    return [pltpu.make_async_copy(source.at[rows, pl.ds(128 * t, 128)], target.at[t, at], sem(t)) for t in range(NT)]


def load_kernel(vel, mag, lab, v, b, hat, e, oa, ob, ol, oh, lraw, ve, be, sem, edge_sem):
    s = Sides()

    def copies(ch):
        some = pl.ds(ch * PER, PER)
        out = [pltpu.make_async_copy(lab.at[some], lraw.at[some], sem.at[ch, 4 * NT])]
        for i, comp in enumerate((0, 2)):
            out += columns(vel.at[comp], ch, v.at[comp], lambda t: sem.at[ch, i * NT + t], PAD)
            out += columns(mag.at[comp], ch, b.at[i], lambda t: sem.at[ch, (2 + i) * NT + t], 0)
        return out

    outer = []
    for i in range(2):
        rows = s.inner[2 + i]
        outer += [
            pltpu.make_async_copy(vel.at[1, rows], ve.at[i], edge_sem.at[i, 0]),
            pltpu.make_async_copy(mag.at[1, rows], be.at[i], edge_sem.at[i, 1]),
        ]
    chunks = [copies(ch) for ch in range(CHUNKS)]
    for copy in chunks[0] + outer + [copy for chunk in chunks[1:] for copy in chunk]:
        copy.start()
    fill_pads(v)
    fill_pads(e)
    fill_pads(hat, OUTSIDE)
    for ch in range(CHUNKS):
        for copy in chunks[ch]:
            copy.wait()

        @pl.loop(0, PER // 8, unroll=8)
        def _(i):
            raw = pl.ds(pl.multiple_of(ch * PER + i * 8, 8), 8)
            at = pl.ds(pl.multiple_of(PAD + ch * PER + i * 8, 8), 8)
            for t in range(NT):
                label = lraw[raw, pl.ds(128 * t, 128)]
                hat[t, at, :] = jnp.where(label == 0, 0.5, jnp.where(label == 1, 0.5 / 0.7, 0.125)).astype(F32)
                e[1, t, at, :] = v[2, t, at, :] * b[0, t, raw, :] - v[0, t, at, :] * b[1, t, raw, :]

    for copy in outer:
        copy.wait()
    for i, out in enumerate((ol, oh)):
        rows, inner = s.rows[2 + i], s.inner[2 + i]
        out[0] = hat[:, rows, :]
        for t in range(NT):
            col = pl.ds(128 * t, 128)
            out[1, t] = ve[i, :, col] * b[1, t, inner, :] - v[2, t, rows, :] * be[i, :, col]
    for out, rows in zip((oa, ob), s.rows):
        out[0] = hat[:, rows, :]
        out[1] = e[1, :, rows, :]
    ob[2] = v[0, :, s.rows[1], :]


def rest_kernel(w0, vel, mag, visc, hat, b, v_in, e_in, v, e, vnew, f, src, inv, phi, nu, near,
                ka, kb, kl, kh, mid, sem, visc_sem):
    del v_in, e_in
    chunks = [
        columns(vel.at[1], ch, v.at[1], lambda t: sem.at[ch, t], PAD)
        + columns(mag.at[1], ch, mid, lambda t: sem.at[ch, NT + t], 0)
        for ch in range(CHUNKS)
    ]
    last = [
        pltpu.make_async_copy(visc.at[:, pl.ds(128 * t, 128)], nu.at[t, pl.ds(PAD, CELLS)], visc_sem.at[t])
        for t in range(NT)
    ]
    for copy in [copy for chunk in chunks for copy in chunk] + last:
        copy.start()
    f[1, :, 0:PAD, :] = jnp.zeros((NT, PAD, 128), F32)
    fill_pads(phi)
    fill_pads(nu)
    for ch in range(CHUNKS):
        for copy in chunks[ch]:
            copy.wait()

        @pl.loop(0, PER // 8, unroll=8)
        def _(i):
            raw = pl.ds(pl.multiple_of(ch * PER + i * 8, 8), 8)
            at = pl.ds(pl.multiple_of(PAD + ch * PER + i * 8, 8), 8)
            v0, v1, v2 = (v[c, :, at, :] for c in range(3))
            b0, b1, b2 = b[0, :, raw, :], mid[:, raw, :], b[1, :, raw, :]
            e1 = e[1, :, at, :]
            e0, e2 = v1 * b2 - v2 * b1, v0 * b1 - v1 * b0
            e[0, :, at, :] = e0
            e[2, :, at, :] = e2
            gain = (0.5 * force_gain) * recip(hat[:, at, :])
            vnew[0, :, at, :] = gain * (e1 * b2 - e2 * b1)
            vnew[1, :, at, :] = gain * (e2 * b0 - e0 * b2)
            vnew[2, :, at, :] = gain * (e0 * b1 - e1 * b0)

    faces(w0, hat, e, f, src, inv, phi)
    s = Sides()
    fields = [b.at[0], mid, b.at[1]]
    for i, k in enumerate((ka, kb, kl, kh)):
        rows, at, d = s.rows[i], s.inner[i], s.dims[i]
        n1, n2 = (d + 1) % 3, (d + 2) % 3
        g = (0.25 * force_gain * s.signs[i]) * (s.masks[i] * recip(hat[:, rows, :]))
        k[0] = g * fields[n2][:, at, :]
        k[1] = -g * fields[n1][:, at, :]
    for copy in last:
        copy.wait()
    for c in range(3):
        near[c] = v[c, :, s.rows[0], :]
    near[3] = nu[:, s.rows[0], :]


def faces(w0, hat, e, f, src, inv, phi):
    zero = jnp.zeros(SHAPE, F32)
    sub = sublanes()

    def body(x, carry):
        fxm, qxm, hc, exc = carry
        r = row_of(x)
        fxo, qxo, hn, exn = [], [], [], []
        for y in range(2):
            base = r + 8 * y
            at, up, down = pl.ds(base, 8), pl.ds(base + 1, 8), pl.ds(base - 1, 8)
            ahead = pl.ds(base + NYL, 8)
            c = hc[y]
            hn.append(hat[:, ahead, :])
            exn.append(e[0, :, ahead, :])
            fx = recip(c + hn[y])
            qx = fx * (exc[y] + exn[y])
            fxo.append(fx)
            qxo.append(qx)
            ey = e[1, :, at, :]
            fy = recip(c + hat[:, up, :])
            fym = recip(c + hat[:, down, :])
            if y == 1:
                fy = jnp.where(sub == 7, 0.0, fy)
            else:
                fym = jnp.where(sub == 0, 0.0, fym)
            ez = e[2, :, at, :]
            fz = recip(c + z_up(c, OUTSIDE))
            fzm = recip(c + z_down(c, OUTSIDE))
            qy = fy * (ey + e[1, :, up, :]) - fym * (ey + e[1, :, down, :])
            qz = fz * (ez + z_up(ez)) - fzm * (ez + z_down(ez))
            source = 0.5 * (((qx - qxm[y]) + qy) + qz)
            inverse = recip((((fx + fxm[y]) + (fy + fym)) + (fz + fzm)) + 0.025 * recip(c))
            f[0, :, at, :] = fx
            f[1, :, at, :] = fy
            f[2, :, at, :] = fz
            src[:, at, :] = source
            inv[:, at, :] = inverse
            phi[:, at, :] = (-w0) * (source * inverse)
        return tuple(fxo), tuple(qxo), tuple(hn), tuple(exn)

    first = [pl.ds(PAD + 8 * y, 8) for y in range(2)]
    start = (
        (zero, zero),
        (zero, zero),
        tuple(hat[:, at, :] for at in first),
        tuple(e[0, :, at, :] for at in first),
    )
    lax.fori_loop(0, NXL, body, start, unroll=8)


SOURCE, INVERSE, BEHIND, *FLOW = (pl.ds(i * NYL, NYL) for i in range(6))
LINES = 6 * NYL


def flux_behind(phi, f, s, side):
    return f[0, :, s.face_behind[side], :] * phi[:, s.behind[side], :]


def first_edge_kernel(w0, ha, hb, hl, hh, sa, sb, sl, sh, v, near, f_in, src_in, inv_in, phi_in,
                      f, src, inv, phi, ca, cb, cl, ch, oa, ob, ol, oh):
    del f_in, src_in, inv_in, phi_in
    s = Sides()
    halos, sent, coefs = (ha, hb, hl, hh), (sa, sb, sl, sh), (ca, cb, cl, ch)

    def add(i):
        rows = s.rows[i]
        g = s.masks[i] * recip(sent[i][0] + halos[i][0])
        source = src[:, rows, :] + (0.5 * s.signs[i]) * (g * (sent[i][1] + halos[i][1]))
        return g, source, recip(recip(inv[:, rows, :]) + g)

    got = [add(i) for i in (2, 3)]
    for i, (g, source, inverse) in zip((2, 3), got):
        rows = s.rows[i]
        f[0, :, s.face_in[i - 2], :] = g
        coefs[i][...] = g
        src[:, rows, :] = source
        inv[:, rows, :] = inverse
        phi[:, rows, :] = (-w0) * (source * inverse)
    got = [add(i) for i in (0, 1)]
    for i, (g, source, inverse) in zip((0, 1), got):
        rows = s.rows[i]
        value = (-w0) * (source * inverse)
        coefs[i][...] = g * inverse
        src[:, rows, :] = source
        inv[:, rows, :] = inverse
        phi[:, rows, :] = value
        (oa, ob)[i][0] = value
    for c in range(3):
        oa[1 + c] = near[c]
    for i, (out, rows, x) in enumerate(zip((ol, oh), s.rows[2:], s.edge)):
        inverse = inv[:, rows, :]
        coefs[2 + i][...] = coefs[2 + i][...] * inverse
        out[:, SOURCE, :] = src[:, rows, :]
        out[:, INVERSE, :] = inverse
        out[:, BEHIND, :] = flux_behind(phi, f, s, i)
        for c in range(3):
            out[:, FLOW[c], :] = v[c, :, rows, :]
        out[:, pl.ds(LINES, 8), :] = jnp.zeros(SHAPE, F32)
        for j, coef in enumerate((ca, cb)):
            out[:, pl.ds(LINES + j, 1), :] = coef[:, pl.ds(x, 1), :]


def add_sides(w, phi, coefs, halos, rows):
    got = [phi[:, r, :] + w * (c[...] * h) for c, h, r in zip(coefs, halos, rows)]
    for r, value in zip(rows, got):
        phi[:, r, :] = value
    return got


def wide_edge_kernel(w, w0, old, f, phi_in, ca, cb, cl, ch, rl, rh, kl, kh, ha, hb, *rest):
    del phi_in
    s = Sides()
    phi, *outs = rest[-3:]
    ks = (kl, kh)
    if w0 is None:
        beyond = [(h[0], h[1]) for h in rest[:2]]
    else:
        beyond = [((-w0) * (k[:, SOURCE, :] * k[:, INVERSE, :]), k[:, BEHIND, :]) for k in ks]
    add_sides(w, phi, (cl, ch), (beyond[0][0], beyond[1][0]), s.rows[2:])
    edges = add_sides(w, phi, (ca, cb), (ha[0], hb[0]), s.rows[:2])
    row = lax.broadcasted_iota(jnp.int32, (NT, NYL, 128), 1)
    for side, (r, k, (c, flux)) in enumerate(zip((rl, rh), ks, beyond)):
        hat = r[0]
        fy = jnp.where(row == NYL - 1, 0.0, recip(hat + pltpu.roll(hat, NYL - 1, 1)))
        fz = recip(hat + z_up(hat, OUTSIDE))
        t = f[0, :, s.face_in[side], :] * old[:, s.rows[2 + side], :] + flux
        t = t + fy * pltpu.roll(c, NYL - 1, 1) + pltpu.roll(fy * c, 1, 1)
        t = t + fz * z_up(c) + z_down(fz * c)
        phi[:, s.beyond[side], :] = s.masks[2 + side] * (c + w * ((t - k[:, SOURCE, :]) * k[:, INVERSE, :] - c))
    for out, values, at in zip(outs, edges, (s.near, s.far)):
        out[0, :, pl.ds(0, NXL), :] = values
        more = out.shape[2] - NXL
        out[0, :, pl.ds(NXL, more), :] = jnp.zeros((NT, more, 128), F32)
        for side, (c, _) in enumerate(beyond):
            line = jnp.sum(jnp.where(row == at, c, 0.0), axis=1, keepdims=True)
            out[0, :, pl.ds(NXL + side, 1), :] = line


def narrow_edge_kernel(w, w_before, f, nu, near, phi_in, ca, cb, cl, ch, kl, kh, ha, hb, phi, oa, ob, ol, oh):
    del phi_in
    s = Sides()
    for j, (h, at) in enumerate(((ha, s.near), (hb, s.far))):
        for side, (k, c, plane) in enumerate(zip((kl, kh), (cl, ch), s.edge)):
            missing = w_before * (k[:, pl.ds(LINES + j, 1), :] * h[0, :, pl.ds(NXL + side, 1), :])
            row = pl.ds(PAD + plane * NYL + at, 1)
            phi[:, row, :] = phi[:, row, :] + w * (c[:, pl.ds(at, 1), :] * missing)
    inner = pl.ds(0, NXL)
    oa[0], ob[0] = add_sides(w, phi, (ca, cb), (ha[0, :, inner, :], hb[0, :, inner, :]), s.rows[:2])
    oa[1] = near[3]
    for i, (out, rows) in enumerate(zip((ol, oh), s.rows[2:])):
        out[0] = phi[:, rows, :]
        out[1] = flux_behind(phi, f, s, i)
        out[2] = nu[:, rows, :]


def predictor(v, nu, vnew, x0, x1):
    sub = sublanes()
    half = 0.5 * time_step

    @pl.loop(x0, x1, unroll=8)
    def _(x):
        r = row_of(x)
        for y in range(2):
            base = r + 8 * y
            at = pl.ds(base, 8)
            ups = (pl.ds(base + NYL, 8), pl.ds(base + 1, 8))
            downs = (pl.ds(base - NYL, 8), pl.ds(base - 1, 8))
            n = nu[:, at, :]
            vc = [v[c, :, at, :] for c in range(3)]
            coefs = []
            total = None
            for d in range(3):
                above = nu[:, ups[d], :] if d < 2 else z_up(n)
                below = nu[:, downs[d], :] if d < 2 else z_down(n)
                up = (n + above) - vc[d]
                down = (n + below) + vc[d]
                if d == 1 and y == 1:
                    up = jnp.where(sub == 7, 0.0, up)
                if d == 1 and y == 0:
                    down = jnp.where(sub == 0, 0.0, down)
                coefs.append((up, down))
                both = up + down
                total = both if total is None else total + both
            keep = 1.0 - half * total
            for c in range(3):
                acc = None
                for d in range(3):
                    above = v[c, :, ups[d], :] if d < 2 else z_up(vc[c])
                    below = v[c, :, downs[d], :] if d < 2 else z_down(vc[c])
                    term = coefs[d][0] * above + coefs[d][1] * below
                    acc = term if acc is None else acc + term
                vnew[c, :, at, :] = vnew[c, :, at, :] + (half * acc + keep * vc[c])


def sweep_kernel(w, phi, f, src, inv, out, x0=0, x1=NXL):
    if x0 == 0:
        fill_pads(out)

    def body(x, carry):
        pxm, pc = carry
        r = row_of(x)
        px, pn = [], []
        for y in range(2):
            base = r + 8 * y
            at, up, down = pl.ds(base, 8), pl.ds(base + 1, 8), pl.ds(base - 1, 8)
            pn.append(phi[:, pl.ds(base + NYL, 8), :])
            fx = f[0, :, at, :]
            c = pc[y]
            px.append(fx * c)
            t = fx * pn[y] + pxm[y]
            t = t + f[1, :, at, :] * phi[:, up, :]
            t = t + f[1, :, down, :] * phi[:, down, :]
            fz = f[2, :, at, :]
            t = t + fz * z_up(c)
            t = t + z_down(fz * c)
            out[:, at, :] = c + w * ((t - src[:, at, :]) * inv[:, at, :] - c)
        return tuple(px), tuple(pn)

    before = tuple(f[0, :, pl.ds(x0 * NYL + 8 * y, 8), :] * phi[:, pl.ds(x0 * NYL + 8 * y, 8), :] for y in range(2))
    start = (before, tuple(phi[:, pl.ds(PAD + x0 * NYL + 8 * y, 8), :] for y in range(2)))
    lax.fori_loop(x0, x1, body, start, unroll=min(16, x1 - x0))


CUT = 8


def sweep_flow_kernel(w, phi, f, src, inv, v, nu, out, flow):
    rows = Sides().rows[1]
    flow[0] = v[1, :, rows, :]
    flow[1] = v[2, :, rows, :]
    flow[2] = nu[:, rows, :]
    sweep_kernel(w, phi, f, src, inv, out, 0, CUT)


def sweep_end_kernel(w, phi, f, src, inv, out_in, out):
    del out_in
    sweep_kernel(w, phi, f, src, inv, out, CUT, NXL)


def sweep_predict_kernel(w, planes, phi, f, src, inv, v, nu, vnew_in, out, vnew):
    del vnew_in
    sweep_kernel(w, phi, f, src, inv, out)
    predictor(v, nu, vnew, *planes)


def force_kernel(phi, hat, b, v, nu, *rest):
    far0, near, near_nu, far, *along = rest[:8]
    sent = (
        (near[1], near[2], near[3], near_nu[1]),
        (far0[2], far[0], far[1], far[2]),
        *((*(along[i][:, rows, :] for rows in FLOW), along[2 + i][2]) for i in range(2)),
    )
    potential, result, vnew, sem, out_sem = rest[9:]
    copies = [
        pltpu.make_async_copy(phi.at[t, pl.ds(PAD, CELLS)], potential.at[:, pl.ds(128 * t, 128)], sem.at[t])
        for t in range(NT)
    ]
    for copy in copies:
        copy.start()

    s = Sides()
    half = 0.5 * time_step
    for pair in ((0, 1), (2, 3)):
        got = []
        for i in pair:
            rows, d, sign, mask = s.rows[i], s.dims[i], s.signs[i], s.masks[i]
            other = sent[i][:3]
            hn = mask * sent[i][3]
            vc = [v[c, :, rows, :] for c in range(3)]
            coef = half * ((nu[:, rows, :] + hn) - sign * vc[d])
            gone = half * hn if d == 0 else coef
            got.append([vnew[c, :, rows, :] + (coef * (mask * other[c]) - gone * vc[c]) for c in range(3)])
        for i, values in zip(pair, got):
            for c in range(3):
                vnew[c, :, s.rows[i], :] = values[c]

    sub = sublanes()
    for ch in range(CHUNKS):

        @pl.loop(ch * (NXL // CHUNKS), (ch + 1) * (NXL // CHUNKS), unroll=8)
        def _(x):
            r = row_of(x)
            for y in range(2):
                base = r + 8 * y
                at = pl.ds(base, 8)
                raw = pl.ds(pl.multiple_of(x * NYL + 8 * y, 8), 8)
                p = phi[:, at, :]
                yu = phi[:, pl.ds(base + 1, 8), :]
                yd = phi[:, pl.ds(base - 1, 8), :]
                if y == 1:
                    yu = jnp.where(sub == 7, 0.0, yu)
                else:
                    yd = jnp.where(sub == 0, 0.0, yd)
                diffs = (
                    phi[:, pl.ds(base + NYL, 8), :] - phi[:, pl.ds(base - NYL, 8), :],
                    yu - yd,
                    z_up(p) - z_down(p),
                )
                g = (-0.25 * force_gain) * recip(hat[:, at, :])
                c0, c1, c2 = (g * diff for diff in diffs)
                for t in range(NT):
                    b0, b1, b2 = (b[c, raw, pl.ds(128 * t, 128)] for c in range(3))
                    vnew[0, t, at, :] = vnew[0, t, at, :] + (c1[t] * b2 - c2[t] * b1)
                    vnew[1, t, at, :] = vnew[1, t, at, :] + (c2[t] * b0 - c0[t] * b2)
                    vnew[2, t, at, :] = vnew[2, t, at, :] + (c0[t] * b1 - c1[t] * b0)

        if ch == CHUNKS - 1:
            break
        low = ch * PER + (NYL if ch == 0 else 0)
        some = (ch + 1) * PER - low
        for t in range(NT):
            copy = pltpu.make_async_copy(
                vnew.at[1, t, pl.ds(PAD + low, some)],
                result.at[1, pl.ds(low, some), pl.ds(128 * t, 128)],
                out_sem.at[ch, t],
            )
            copy.start()
            copies.append(copy)
    for copy in copies:
        copy.wait()


PARTS = 4


def last_kernel(w, ka, kb, kl, kh, cl, ch, ha, hb, vnew_in, result_in, result, vnew, sem, edge_sem):
    del vnew_in, result_in
    planes = NXL // PARTS
    copies = []
    s = Sides()
    for side, (k, lines, plane) in enumerate(zip((kl, kh), (cl, ch), s.edge)):
        for j, (h, at) in enumerate(((ha, s.near), (hb, s.far))):
            missing = w * (lines[:, pl.ds(LINES + j, 1), :] * h[0, :, pl.ds(NXL + side, 1), :])
            row = pl.ds(PAD + plane * NYL + at, 1)
            for i, c in enumerate((1, 2)):
                vnew[c, :, row, :] = vnew[c, :, row, :] + k[i, :, pl.ds(at, 1), :] * missing
    for i, (low, some) in enumerate(((0, NYL), ((CHUNKS - 1) * PER, PER))):
        for t in range(NT):
            copy = pltpu.make_async_copy(
                vnew.at[1, t, pl.ds(PAD + low, some)],
                result.at[1, pl.ds(low, some), pl.ds(128 * t, 128)],
                edge_sem.at[i, t],
            )
            copy.start()
            copies.append(copy)
    for part in range(PARTS):
        s = Sides(part * planes, planes)
        some = pl.ds(part * planes, planes)
        got = []
        for k, h, rows in ((ka, ha, s.rows[0]), (kb, hb, s.rows[1])):
            halo = h[0, :, some, :]
            got += [(c, rows, vnew[c, :, rows, :] + k[j, :, some, :] * halo) for j, c in enumerate((2, 0))]
        for c, rows, value in got:
            vnew[c, :, rows, :] = value
        per = planes * NYL
        for c in (0, 2):
            for t in range(NT):
                copy = pltpu.make_async_copy(
                    vnew.at[c, t, pl.ds(PAD + part * per, per)],
                    result.at[c, pl.ds(part * per, per), pl.ds(128 * t, 128)],
                    sem.at[part, c // 2, t],
                )
                copy.start()
                copies.append(copy)
    for copy in copies:
        copy.wait()


def resident(*shape):
    return pltpu.VMEM(shape, F32)


def in_vmem(x):
    return pltpu.with_memory_space_constraint(x, pltpu.VMEM)


def in_hbm(x):
    return pltpu.with_memory_space_constraint(x, pltpu.HBM)


IN_VMEM = pl.BlockSpec(memory_space=pltpu.VMEM)
IN_HBM = pl.BlockSpec(memory_space=pl.ANY)

FIELD = (NT, ROWS, 128)


def run(kernel, name, ins, outs, aliases=None, scratch=(), flops=0, moved=0, limit=4 * MIB):
    args = [in_hbm(a) if hbm else in_vmem(a) for a, hbm in ins]
    return pl.pallas_call(
        kernel,
        out_shape=outs,
        in_specs=[IN_HBM if hbm else IN_VMEM for _, hbm in ins],
        out_specs=[IN_HBM if isinstance(o, jax.ShapeDtypeStruct) else IN_VMEM for o in outs],
        input_output_aliases=aliases or {},
        scratch_shapes=list(scratch),
        compiler_params=pltpu.CompilerParams(vmem_limit_bytes=limit),
        cost_estimate=pl.CostEstimate(flops=flops, bytes_accessed=moved, transcendentals=0),
        name=name,
    )(*args)


def vm(*arrays):
    return [(a, False) for a in arrays]


def next_chip(b):
    n = lax.axis_size("width") * 2
    return lax.ppermute(b, WIDTH, [(i, (((i + 1) ^ 1) - 1) % n) for i in range(n)])


def across(a, b):
    hb = next_chip(b)
    return lax.ppermute(a, "thick", [(0, 1), (1, 0)]), hb


def along(a, b):
    n, m = lax.axis_size("cast"), lax.axis_size("width") * 2
    second = []
    for i in range(n):
        j = ((i + 1) ^ 1) - 1
        second += [(i * m + k, j * m + k if 0 <= j < n else i * m + (k ^ 1)) for k in range(m)]
    hb = lax.ppermute(b, ("cast", *WIDTH), second)
    return lax.ppermute(a, "cast", [(i, i ^ 1) for i in range(n)]), hb


def rows_of(n, planes=NXL):
    return [resident(n, NT, planes, 128)] * 2


def planes_of(n):
    return [resident(n, NT, NYL, 128)] * 2


def local(velocity, magnetic, labels, viscosity):
    vel = velocity.reshape(3, CELLS, NT * 128)
    mag = magnetic.reshape(3, CELLS, NT * 128)
    lab = labels.reshape(CELLS, NT * 128)
    visc = viscosity.reshape(CELLS, NT * 128)
    dma = pltpu.SemaphoreType.DMA
    w = [sweep_weight(k) for k in range(ITERS)]
    field, fields = resident(*FIELD), resident(3, *FIELD)
    work = dict(flops=10_000_000, moved=16 * MIB)

    v, b, hat, e, *edges = run(
        load_kernel, "load", [(vel, True), (mag, True), (lab, True)],
        [fields, resident(2, NT, CELLS, 128), field, fields, resident(2, NT, NXL, 128), resident(3, NT, NXL, 128)] + planes_of(2),
        scratch=[
            pltpu.VMEM((CELLS, NT * 128), jnp.int32),
            pltpu.VMEM((2, NYL, NT * 128), F32),
            pltpu.VMEM((2, NYL, NT * 128), F32),
            dma((CHUNKS, 4 * NT + 1)),
            dma((2, 2)),
        ],
    )
    h1 = (*across(*edges[:2]), *along(*edges[2:]))
    v, e, vnew, f, src, inv, phi, nu, near, *products = run(
        functools.partial(rest_kernel, w[0]), "faces",
        [(vel, True), (mag, True), (visc, True)] + vm(hat, b, v, e),
        [fields, fields, fields, fields, field, field, field, field, resident(4, NT, NXL, 128)]
        + rows_of(2) + planes_of(2),
        aliases={5: 0, 6: 1},
        scratch=[pltpu.VMEM((NT, CELLS, 128), F32), dma((CHUNKS, 2 * NT)), dma((NT,))], **work,
    )
    f, src, inv, phi, *rest = run(
        functools.partial(first_edge_kernel, w[0]), "edges1", vm(*h1, *edges, v, near, f, src, inv, phi),
        [fields] + [field] * 3 + [resident(NT, NXL, 128)] * 2 + [resident(NT, NYL, 128)] * 2
        + [resident(4, NT, NXL, 128), resident(1, NT, NXL, 128)] + [resident(NT, LINES + 8, 128)] * 2,
        aliases={10: 0, 11: 1, 12: 2, 13: 3},
    )
    coefs, edges = rest[:4], rest[4:]

    h2 = (*across(*edges[:2]), *along(*edges[2:]))
    lines = h2[2:]
    old = phi
    phi, vnew = run(
        functools.partial(sweep_predict_kernel, w[1], (0, 40)), "sweep1", vm(phi, f, src, inv, v, nu, vnew),
        [field, fields], aliases={6: 1}, **work,
    )
    phi, *edges = run(
        functools.partial(wide_edge_kernel, w[1], w[0]), "edges2",
        vm(old, f, phi, *coefs, *h1[2:], *lines, *h2[:2]),
        [field, resident(1, NT, NXL + 8, 128), resident(1, NT, NXL + 16, 128)], aliases={2: 0},
    )

    h3 = across(*edges)
    half, flow = run(
        functools.partial(sweep_flow_kernel, w[2]), "sweep2", vm(phi, f, src, inv, v, nu),
        [field, resident(3, NT, NXL, 128)], **work,
    )
    (phi,) = run(
        functools.partial(sweep_end_kernel, w[2]), "rest2", vm(phi, f, src, inv, half), [field], aliases={4: 0}, **work
    )
    flow = next_chip(flow)
    phi, *edges = run(
        functools.partial(narrow_edge_kernel, w[2], w[1]), "edges3", vm(f, nu, near, phi, *coefs, *lines, *h3),
        [field, resident(2, NT, NXL, 128), resident(1, NT, NXL, 128)] + planes_of(3), aliases={3: 0},
    )

    h4 = (*across(*edges[:2]), *along(*edges[2:]))
    old = phi
    phi, vnew = run(
        functools.partial(sweep_predict_kernel, w[3], (40, 64)), "sweep3", vm(phi, f, src, inv, v, nu, vnew),
        [field, fields], aliases={6: 1}, **work,
    )
    phi, *edges = run(
        functools.partial(wide_edge_kernel, w[3], None), "edges4",
        vm(old, f, phi, *coefs, *h1[2:], *lines, *h4, flow),
        [field, resident(1, NT, NXL + 8, 128), resident(1, NT, NXL + 16, 128)], aliases={2: 0},
    )

    h5 = across(*edges)
    potential, result, vnew = run(
        force_kernel, "force", vm(phi, hat, mag, v, nu, h1[1], h2[0], h4[0], flow, *lines, *h4[2:], vnew),
        [jax.ShapeDtypeStruct((CELLS, NT * 128), F32), jax.ShapeDtypeStruct((3, CELLS, NT * 128), F32), fields],
        aliases={13: 2}, scratch=[dma((NT,)), dma((CHUNKS - 1, NT))], **work,
    )
    result, _ = run(
        functools.partial(last_kernel, w[3]), "last", vm(*products, *lines, *h5, vnew) + [(result, True)],
        [jax.ShapeDtypeStruct((3, CELLS, NT * 128), F32), fields],
        aliases={8: 1, 9: 0}, scratch=[dma((PARTS, 2, NT)), dma((2, NT))],
    )
    return result.reshape(velocity.shape), potential.reshape(labels.shape)


def solution(mesh):
    fields = P(None, "cast", WIDTH, None)
    scalar = P("cast", WIDTH, None)
    return jax.shard_map(
        local,
        mesh=mesh,
        in_specs=(fields, fields, scalar, scalar),
        out_specs=(fields, scalar),
        check_vma=False,
    )
```
